32 devices in a mesh: seq: 8 (over z, x), tp: 4 (over y, core).
Axes of the slice: x: 2, y: 2, z: 4, core: 2. Of those that a mesh axis runs over, the one named last changes fastest.
Arguments:
- tokens: bfloat16 [16, 1024, 768], P(None, 'seq'), may hold values from -6 to 6
- rand_blocks: int32 [16, 16, 12, 3], P(None, None, 'tp'), may hold values from 0 to 15, as said below
- query_weight: bfloat16 [768, 768], P(None, 'tp'), may hold values from -0.21875 to 0.21875
- query_bias: float32 [768], P('tp'), may hold values from -3 to 3
- key_weight: bfloat16 [768, 768], P(None, 'tp'), may hold values from -0.21875 to 0.21875
- value_weight: bfloat16 [768, 768], P(None, 'tp'), may hold values from -0.21875 to 0.21875
- value_bias: float32 [768], P('tp'), may hold values from -1.2 to 1.2
- output_weight: bfloat16 [768, 768], P('tp'), may hold values from -0.875 to 0.875
- output_bias: float32 [768], replicated, may hold values from -1.8 to 1.8
- attn_gain: float32 [768], replicated, may hold values from 0.25 to 1.75
- attn_shift: float32 [768], replicated, may hold values from -1.8 to 1.8
- up_weight: bfloat16 [768, 3072], P(None, 'tp'), may hold values from -0.21875 to 0.21875
- up_bias: float32 [3072], P('tp'), may hold values from -3 to 3
- down_weight: bfloat16 [3072, 768], P('tp'), may hold values from -0.109375 to 0.109375
- down_bias: float32 [768], replicated, may hold values from -1.8 to 1.8
- ffn_gain: float32 [768], replicated, may hold values from 0.25 to 1.75
- ffn_shift: float32 [768], replicated, may hold values from -1.8 to 1.8
- cotangent: bfloat16 [16, 1024, 768], P(None, 'seq'), may hold values from -6 to 6
Outputs:
- layer_output: bfloat16 [16, 1024, 768], P(None, 'seq')
- input_grad: float32 [16, 1024, 768], P(None, 'seq')
- grad_qweight: float32 [768, 768], P(None, 'tp')
- grad_qbias: float32 [768], P('tp')
- grad_kweight: float32 [768, 768], P(None, 'tp')
- grad_vweight: float32 [768, 768], P(None, 'tp')
- grad_vbias: float32 [768], P('tp')
- grad_oweight: float32 [768, 768], P('tp')
- grad_obias: float32 [768], replicated
- grad_attngain: float32 [768], replicated
- grad_attnshift: float32 [768], replicated
- grad_upweight: float32 [768, 3072], P(None, 'tp')
- grad_upbias: float32 [3072], P('tp')
- grad_downweight: float32 [3072, 768], P('tp')
- grad_downbias: float32 [768], replicated
- grad_ffngain: float32 [768], replicated
- grad_ffnshift: float32 [768], replicated
The draws below stay inside these ranges and needn't reach their ends.
Inputs may be any that keep to these rules, and one draw needn't show every extreme that they name: `rand_blocks`: entries name blocks of the same sequence; the entries of query blocks 0 and 15 are not read. Group the entries by head group (heads g * 3 to (g + 1) * 3 - 1) and by query run (query blocks p * 2 to (p + 1) * 2 - 1, all sequences): in each such group at most 72 entries name blocks of any one key run (blocks o * 2 to (o + 1) * 2 - 1), and one key run is named exactly 72 times by every group.
All inputs are finite; a program needn't handle non-finite values.
Results may differ from the reference program's by a relative error of at most 0.015.
Values may be sent and summed in bfloat16 or wider, within the bound.
A program may use at most 384 MiB of HBM per device.

```python
import jax
import jax.numpy as jnp
from jax import lax

D = 768
H = 12
HD = 64
FF = 3072
BLOCK = 64
BLOCKS_DEV = 2
SEQS = 16
HEADS_DEV = 3
NB = 16
LEN = 1024
CAP = 72


def permuted(subkey):
    return jax.random.permutation(subkey, SEQS * BLOCKS_DEV * HEADS_DEV * 3)


def draw_rand_blocks(key, part):
    key = jax.random.fold_in(key, 7)
    n_runs = NB // BLOCKS_DEV
    groups = H // HEADS_DEV
    hot_key, perm_key, pick_key = jax.random.split(key, 3)
    hottest = jax.random.randint(hot_key, (), 0, n_runs)
    orders = jax.vmap(permuted)(jax.random.split(perm_key, n_runs * groups))
    spill = jnp.maximum(orders - CAP, 0) % (n_runs - 1)
    others = spill + (spill >= hottest).astype(jnp.int32)
    owners = jnp.where(orders < CAP, hottest, others)
    within = jax.random.randint(pick_key, owners.shape, 0, BLOCKS_DEV)
    chosen = (owners * BLOCKS_DEV + within).reshape(n_runs, groups, SEQS, BLOCKS_DEV, HEADS_DEV, 3)
    return chosen.transpose(2, 0, 3, 1, 4, 5).reshape(SEQS, NB, H, 3).astype(jnp.int32)


def steps_of(stream_key, extent, pieces, smallest, high):
    level = 1.0
    for axis_at, blocks in pieces:
        heights = jax.random.uniform(jax.random.fold_in(jax.random.fold_in(stream_key, 6), axis_at), (blocks,), jnp.float32, smallest / len(pieces), high / len(pieces))
        level = level * jnp.repeat(jnp.exp(heights), extent[axis_at] // blocks).reshape((-1,) + (1,) * (len(extent) - 1 - axis_at))
    return level


def scatter_about(stream_key, extent, deviation, bound, cuts=(), held_as=jnp.bfloat16):
    values = deviation * jax.random.normal(stream_key, extent, jnp.float32)
    if cuts:
        values = values * steps_of(stream_key, extent, cuts, -0.22, 0.18)
    return jnp.clip(values, -bound, bound).astype(held_as)


def setup_inputs(seed: int = 0) -> dict:
    key_list = jax.random.split(jax.random.key(seed), 19)
    tokens = scatter_about(key_list[0], (SEQS, LEN, D), 1.0, 6.0, ((1, 8),))
    rand_blocks = draw_rand_blocks(jax.random.fold_in(key_list[18], 71), 0)
    query_weight = scatter_about(key_list[2], (D, D), D ** -0.5, 0.21875, ((1, 4),))
    query_bias = scatter_about(key_list[3], (D,), 0.5, 3.0, ((0, 4),), jnp.float32)
    key_weight = scatter_about(key_list[4], (D, D), D ** -0.5, 0.21875, ((1, 4),))
    value_weight = scatter_about(key_list[5], (D, D), D ** -0.5, 0.21875, ((1, 4),))
    value_bias = scatter_about(key_list[6], (D,), 0.2, 1.2, ((0, 4),), jnp.float32)
    output_weight = scatter_about(key_list[7], (D, D), (D // 16) ** -0.5, 0.875, ((0, 4),))
    output_bias = scatter_about(key_list[8], (D,), 0.3, 1.8, (), jnp.float32)
    attn_gain = jnp.clip(1.0 + 0.15 * jax.random.normal(key_list[9], (D,), jnp.float32), 0.25, 1.75)
    attn_shift = scatter_about(key_list[10], (D,), 0.3, 1.8, (), jnp.float32)
    up_weight = scatter_about(key_list[11], (D, FF), D ** -0.5, 0.21875, ((1, 4),))
    up_bias = scatter_about(key_list[12], (FF,), 0.5, 3.0, ((0, 4),), jnp.float32)
    down_weight = scatter_about(key_list[13], (FF, D), FF ** -0.5, 0.109375, ((0, 4),))
    down_bias = scatter_about(key_list[14], (D,), 0.3, 1.8, (), jnp.float32)
    ffn_gain = jnp.clip(1.0 + 0.15 * jax.random.normal(key_list[15], (D,), jnp.float32), 0.25, 1.75)
    ffn_shift = scatter_about(key_list[16], (D,), 0.3, 1.8, (), jnp.float32)
    cotangent = scatter_about(key_list[17], (SEQS, LEN, D), 1.0, 6.0, ((1, 8),))
    return dict(tokens=tokens, rand_blocks=rand_blocks, query_weight=query_weight, query_bias=query_bias, key_weight=key_weight, value_weight=value_weight, value_bias=value_bias, output_weight=output_weight, output_bias=output_bias, attn_gain=attn_gain, attn_shift=attn_shift, up_weight=up_weight, up_bias=up_bias, down_weight=down_weight, down_bias=down_bias, ffn_gain=ffn_gain, ffn_shift=ffn_shift, cotangent=cotangent)


@jax.custom_vjp
def low(v):
    return lax.optimization_barrier(v.astype(jnp.bfloat16)).astype(jnp.float32)

@jax.custom_vjp
def lowered_backward(v):
    return v

def low_keep(v):
    return (low(v), None)

def low_pass(kept, grad):
    return (grad,)

def back_keep(v):
    return (v, None)

def back_low(kept, grad):
    return (low(grad),)
low.defvjp(low_keep, low_pass)
lowered_backward.defvjp(back_keep, back_low)
norm_eps = 1e-06
masked_score = -1e+30
highest_precision = lax.Precision.HIGHEST

def matmul(left, right):
    return jnp.dot(left, right, precision=highest_precision, preferred_element_type=jnp.float32)

def layer_norm(resid, gain, shift):
    centre = resid - lax.optimization_barrier(jnp.mean(resid, -1, keepdims=True))
    spread = lax.optimization_barrier(jnp.mean(centre * centre, -1, keepdims=True))
    return centre * lax.rsqrt(spread + norm_eps) * gain + shift

def softmax_row_probs(scores):
    top_score = lax.optimization_barrier(jnp.max(scores, -1, keepdims=True))
    expo = jnp.exp(scores - top_score)
    return expo / lax.optimization_barrier(jnp.sum(expo, -1, keepdims=True))

def head_attention(packed):
    query_rows, keys, values, chosen = packed
    nblocks = query_rows.shape[0]
    blocks = jnp.arange(nblocks, dtype=jnp.int32)
    before = jnp.clip(blocks - 1, 0, nblocks - 1)
    after = jnp.clip(blocks + 1, 0, nblocks - 1)
    end_keys = jnp.broadcast_to(jnp.stack([keys[0], keys[nblocks - 1]])[None], (nblocks, 2, BLOCK, HD))
    end_values = jnp.broadcast_to(jnp.stack([values[0], values[nblocks - 1]])[None], (nblocks, 2, BLOCK, HD))
    rand_keys = lowered_backward(keys[chosen])
    rand_values = lowered_backward(values[chosen])
    gathered_keys = jnp.concatenate([end_keys, keys[before][:, None], keys[:, None], keys[after][:, None], rand_keys], 1).reshape(nblocks, 8 * BLOCK, HD)
    gathered_values = jnp.concatenate([end_values, values[before][:, None], values[:, None], values[after][:, None], rand_values], 1).reshape(nblocks, 8 * BLOCK, HD)
    unscaled_scores = lowered_backward(jnp.einsum('hwg,hsg->hws', query_rows, gathered_keys, precision=highest_precision)) * 0.125
    slot_ids = jnp.arange(8 * BLOCK, dtype=jnp.int32) // BLOCK
    dropped = (slot_ids == 2)[None, :] & (blocks == 1)[:, None] | (slot_ids == 4)[None, :] & (blocks == nblocks - 2)[:, None]
    unscaled_scores = jnp.where(dropped[:, None, :], masked_score, unscaled_scores)
    sparse_attention = jnp.einsum('cmg,cgl->cml', softmax_row_probs(unscaled_scores), gathered_values, precision=highest_precision)
    end_query = jnp.concatenate([query_rows[0], query_rows[nblocks - 1]], 0)
    end_raw = lowered_backward(matmul(end_query, keys.reshape(-1, HD).T)) * 0.125
    end_out = matmul(softmax_row_probs(end_raw), values.reshape(-1, HD))
    return sparse_attention.at[0].set(end_out[:BLOCK]).at[nblocks - 1].set(end_out[BLOCK:])

def split_heads(matrix):
    return matrix.reshape(NB, BLOCK, H, HD).transpose(2, 0, 1, 3)

def forward_one(seq_tokens, chosen, params):
    query_weight, query_bias, key_weight, value_weight, value_bias, output_weight, output_bias, attn_gain, attn_shift, up_weight, up_bias, down_weight, down_bias, ffn_gain, ffn_shift = params
    query = low(lowered_backward(matmul(seq_tokens, query_weight) + query_bias))
    keyed = low(lowered_backward(matmul(seq_tokens, key_weight)))
    valued = low(lowered_backward(matmul(seq_tokens, value_weight) + value_bias))
    heads_out = lax.map(jax.checkpoint(head_attention), (split_heads(query), split_heads(keyed), split_heads(valued), chosen.transpose(1, 0, 2)))
    attn = heads_out.transpose(1, 2, 0, 3).reshape(NB * BLOCK, H * HD)
    attn_low = low(lowered_backward(attn))
    branch = lowered_backward(matmul(attn_low, output_weight) + output_bias)
    normed = layer_norm(seq_tokens + branch, attn_gain, attn_shift)
    pre_act = lowered_backward(matmul(low(normed), up_weight) + up_bias)
    act_low = low(jax.nn.gelu(pre_act, approximate=False))
    ffn = lowered_backward(matmul(act_low, down_weight) + down_bias)
    return layer_norm(normed + ffn, ffn_gain, ffn_shift)

def reference(tokens, rand_blocks, query_weight, query_bias, key_weight, value_weight, value_bias, output_weight, output_bias, attn_gain, attn_shift, up_weight, up_bias, down_weight, down_bias, ffn_gain, ffn_shift, cotangent):
    params = tuple((array_in.astype(jnp.float32) for array_in in (query_weight, query_bias, key_weight, value_weight, value_bias, output_weight, output_bias, attn_gain, attn_shift, up_weight, up_bias, down_weight, down_bias, ffn_gain, ffn_shift)))

    def one_sequence(totals, packed):
        seq_tokens, chosen, seq_cot = packed

        def forward(inputs, weights):
            return forward_one(inputs, chosen, weights)
        result, pullback = jax.vjp(forward, seq_tokens.astype(jnp.float32), params)
        token_grad, weight_grads = pullback(seq_cot.astype(jnp.float32))
        totals = jax.tree.map(jnp.add, totals, weight_grads)
        return (totals, (result.astype(jnp.bfloat16), token_grad))
    zeroes = jax.tree.map(jnp.zeros_like, params)
    summed, (layer_output, input_grad) = lax.scan(one_sequence, zeroes, (tokens, rand_blocks, cotangent))
    return (layer_output, input_grad, summed[0], summed[1], summed[2], summed[3], summed[4], summed[5], summed[6], summed[7], summed[8], summed[9], summed[10], summed[11], summed[12], summed[13], summed[14])
```

```python
import jax
import jax.numpy as jnp
from jax import lax
from jax.sharding import PartitionSpec as P
from jax.experimental import pallas as pl
from jax.experimental.pallas import tpu as pltpu

HD = 64
BLOCK = 64


norm_eps = 1e-06
masked_score = -1e30
highest_precision = lax.Precision.HIGHEST


def with_halo(shard, sides, width):
    for axis, dim in sides:
        size, length = (lax.axis_size(axis), shard.shape[dim])
        up = [(i, (i + 1) % size) for i in range(size - 1)]
        down = [(j, i) for i, j in up]
        last = lax.slice_in_dim(shard, length - width, length, axis=dim)
        first = lax.slice_in_dim(shard, 0, width, axis=dim)
        before = lax.ppermute(last, axis, up)
        after = lax.ppermute(first, axis, down)
        shard = jnp.concatenate([before, shard, after], axis=dim)
    return shard


def joined(shard, axis, combine):
    everything = jax.tree.map(lambda part: lax.all_gather(part, axis), shard)
    first = jax.tree.map(lambda part: part[0], everything)

    def hop(k, so_far):
        return combine(so_far, jax.tree.map(lambda part: part[k], everything))

    return lax.fori_loop(1, lax.axis_size(axis), hop, first)


def layer_norm(resid, gain, shift):
    centre = resid - jnp.mean(resid, -1, keepdims=True)
    spread = jnp.mean(centre * centre, -1, keepdims=True)
    return centre * lax.rsqrt(spread + norm_eps) * gain + shift


def gelu_exact(values):
    return jax.nn.gelu(values, approximate=False)


def plain_dot(left, right):
    return jnp.dot(left, right, preferred_element_type=jnp.float32)


def rows_dot(left, right):
    return lax.dot_general(
        left, right, (((0,), (0,)), ((), ())), preferred_element_type=jnp.float32
    )


def back_dot(left, right):
    return lax.dot_general(
        left, right, (((1,), (1,)), ((), ())), preferred_element_type=jnp.float32
    )


def softmax_row_probs(scores):
    top_score = jnp.max(scores, -1, keepdims=True)
    expo = jnp.exp(scores - top_score)
    return expo / jnp.sum(expo, -1, keepdims=True)


def head_sum_fwd(pieces):
    return lax.psum(pieces, "tp")


def head_sum_back(pieces):
    return lax.psum(pieces, "tp")


def merge_rows(first, second):
    top_score = jnp.maximum(first[0], second[0])
    scale_one = jnp.exp(first[0] - top_score)
    scale_two = jnp.exp(second[0] - top_score)
    return (
        top_score,
        first[1] * scale_one + second[1] * scale_two,
        first[2] * scale_one[..., None] + second[2] * scale_two[..., None],
    )


def tile_plan(rand_blocks, my_index, n_dev, per_dev, seqs, heads):
    count = seqs * per_dev * heads * 3
    capacity = max(2, 2 * count // n_dev)
    requests = (
        rand_blocks.reshape(seqs, n_dev, per_dev, heads, 3)
        .transpose(1, 0, 2, 3, 4)
        .reshape(n_dev, count)
    )
    is_mine = requests // per_dev == my_index
    ranking = jnp.cumsum(is_mine.astype(jnp.int32), 1) - 1
    slot_ids = jnp.arange(capacity, dtype=jnp.int32)
    select = is_mine[:, None, :] & (ranking[:, None, :] == slot_ids[None, :, None])
    filled = jnp.any(select, 2)
    position = jnp.arange(count, dtype=jnp.int32)
    seq_of = position // (per_dev * heads * 3)
    head_of = position // 3 % heads
    tile_of = (seq_of[None, :] * per_dev + requests % per_dev) * heads + head_of[None, :]
    send_index = jnp.sum(jnp.where(select, tile_of[:, None, :], 0), 2)
    own_requests = lax.dynamic_slice_in_dim(rand_blocks, my_index * per_dev, per_dev, 1).reshape(
        count
    )
    own_owner = own_requests // per_dev
    onehot = (own_owner[:, None] == jnp.arange(n_dev, dtype=jnp.int32)[None, :]).astype(jnp.int32)
    own_rank = jnp.sum((jnp.cumsum(onehot, 0) - 1) * onehot, 1)
    recv_index = own_owner * capacity + own_rank
    return (capacity, send_index, filled, recv_index)


def pick_tiles(incoming, recv_index, seqs, per_dev, heads, block, hsize):
    stacked = incoming.reshape(-1, block, 2 * hsize)
    return jnp.take(stacked, recv_index, 0).reshape(seqs, per_dev, heads, 3, block, 2 * hsize)


def assemble(end_part, window_part, tile_part, seqs, per_dev, heads, block, hsize):
    ends_wide = jnp.broadcast_to(end_part[:, None], (seqs, per_dev, heads, 2 * block, hsize))
    return jnp.concatenate(
        [ends_wide, window_part, tile_part.reshape(seqs, per_dev, heads, 3 * block, hsize)], 3
    )


def split_sequences(
    tokens,
    rand_blocks,
    query_weight,
    query_bias,
    key_weight,
    value_weight,
    value_bias,
    output_weight,
    output_bias,
    attn_gain,
    attn_shift,
    up_weight,
    up_bias,
    down_weight,
    down_bias,
    ffn_gain,
    ffn_shift,
    cotangent,
):
    seqs, rows, width = tokens.shape
    block = BLOCK
    hsize = HD
    per_dev = rows // block
    n_dev = lax.axis_size("seq")
    my_index = lax.axis_index("seq")
    n_blocks = per_dev * n_dev
    heads = query_weight.shape[1] // hsize
    hidden = heads * hsize
    n_tok = seqs * rows
    is_first = my_index == 0
    is_last = my_index == n_dev - 1
    flat = tokens.reshape(n_tok, width)
    query_low = (plain_dot(flat, query_weight) + query_bias).astype(jnp.bfloat16)
    key_low = plain_dot(flat, key_weight).astype(jnp.bfloat16)
    value_low = (plain_dot(flat, value_weight) + value_bias).astype(jnp.bfloat16)
    keyval = jnp.concatenate([key_low, value_low], 1).reshape(seqs, rows, 2 * hidden)
    extended = with_halo(keyval, (("seq", 1),), block)
    windows = jnp.stack(
        [extended[:, offset * block : (offset + 3) * block] for offset in range(per_dev)], 1
    )
    windows = windows.reshape(seqs, per_dev, 3 * block, 2, heads, hsize)
    win_key = windows[:, :, :, 0].transpose(0, 1, 3, 2, 4)
    win_value = windows[:, :, :, 1].transpose(0, 1, 3, 2, 4)
    triple = jnp.concatenate([query_low.reshape(seqs, rows, hidden), keyval], 2).astype(jnp.float32)
    own_ends = jnp.stack(
        [
            jnp.where(is_first, triple[:, :block], 0.0),
            jnp.where(is_last, triple[:, rows - block :], 0.0),
        ],
        1,
    )
    ends = lax.psum(own_ends.astype(jnp.bfloat16), "seq").reshape(seqs, 2, block, 3, heads, hsize)
    end_query = ends[:, :, :, 0].transpose(0, 3, 1, 2, 4).reshape(seqs, heads, 2 * block, hsize)
    end_key = ends[:, :, :, 1].transpose(0, 3, 1, 2, 4).reshape(seqs, heads, 2 * block, hsize)
    end_value = ends[:, :, :, 2].transpose(0, 3, 1, 2, 4).reshape(seqs, heads, 2 * block, hsize)
    capacity, send_index, filled, recv_index = tile_plan(
        rand_blocks, my_index, n_dev, per_dev, seqs, heads
    )
    table = (
        keyval.reshape(seqs, per_dev, block, 2, heads, hsize)
        .transpose(0, 1, 4, 2, 3, 5)
        .reshape(seqs * per_dev * heads, block, 2 * hsize)
    )
    outgoing = jnp.take(table, send_index.reshape(-1), 0).reshape(n_dev, capacity, block, 2 * hsize)
    outgoing = jnp.where(filled[:, :, None, None], outgoing, jnp.zeros((), jnp.bfloat16))
    incoming = lax.all_to_all(outgoing, "seq", split_axis=0, concat_axis=0, tiled=True)
    tiles = pick_tiles(incoming, recv_index, seqs, per_dev, heads, block, hsize)
    q_blocks = query_low.reshape(seqs, per_dev, block, heads, hsize).transpose(0, 1, 3, 2, 4)
    keys_all = assemble(end_key, win_key, tiles[..., :hsize], seqs, per_dev, heads, block, hsize)
    values_all = assemble(
        end_value, win_value, tiles[..., hsize:], seqs, per_dev, heads, block, hsize
    )
    block_ids = my_index * per_dev + jnp.arange(per_dev, dtype=jnp.int32)
    slot_ids = jnp.arange(8 * block, dtype=jnp.int32) // block
    dropped = (slot_ids == 2)[None, :] & (block_ids == 1)[:, None] | (slot_ids == 4)[None, :] & (
        block_ids == n_blocks - 2
    )[:, None]
    unscaled_scores = (
        jnp.einsum("sbhqd,sbhkd->sbhqk", q_blocks, keys_all, preferred_element_type=jnp.float32)
        * 0.125
    )
    unscaled_scores = jnp.where(dropped[None, :, None, None, :], masked_score, unscaled_scores)
    weights = softmax_row_probs(unscaled_scores)
    sparse_attention = jnp.einsum(
        "sbhqk,sbhkd->sbhqd",
        weights,
        values_all.astype(jnp.float32),
        precision=highest_precision,
        preferred_element_type=jnp.float32,
    )
    key_local = key_low.reshape(seqs, rows, heads, hsize).transpose(0, 2, 1, 3)
    value_local = value_low.reshape(seqs, rows, heads, hsize).transpose(0, 2, 1, 3)
    end_raw = (
        jnp.einsum("shqd,shkd->shqk", end_query, key_local, preferred_element_type=jnp.float32)
        * 0.125
    )
    end_top = jnp.max(end_raw, -1)
    end_expo = jnp.exp(end_raw - end_top[..., None])
    end_total = jnp.sum(end_expo, -1)
    end_acc = jnp.einsum(
        "shqk,shkd->shqd",
        end_expo,
        value_local.astype(jnp.float32),
        precision=highest_precision,
        preferred_element_type=jnp.float32,
    )
    merged_top, merged_total, merged_acc = joined((end_top, end_total, end_acc), "seq", merge_rows)
    end_out = merged_acc / merged_total[..., None]
    end_lse = merged_top + jnp.log(merged_total)
    end_split = end_out.reshape(seqs, heads, 2, block, hsize)
    first_rows = block_ids == 0
    last_rows = block_ids == n_blocks - 1
    attn = jnp.where(
        first_rows[None, :, None, None, None], end_split[:, None, :, 0], sparse_attention
    )
    attn = jnp.where(last_rows[None, :, None, None, None], end_split[:, None, :, 1], attn)
    attn_low = attn.transpose(0, 1, 3, 2, 4).reshape(n_tok, hidden).astype(jnp.bfloat16)
    branch = head_sum_fwd(plain_dot(attn_low, output_weight)) + output_bias
    resid = flat.astype(jnp.float32) + branch
    normed = layer_norm(resid, attn_gain, attn_shift)
    normed_low = normed.astype(jnp.bfloat16)
    pre_act = plain_dot(normed_low, up_weight) + up_bias
    act_low = gelu_exact(pre_act).astype(jnp.bfloat16)
    ffn = head_sum_fwd(plain_dot(act_low, down_weight)) + down_bias
    resid_two = normed + ffn
    layer_output = (
        layer_norm(resid_two, ffn_gain, ffn_shift).astype(jnp.bfloat16).reshape(seqs, rows, width)
    )
    cot_flat = cotangent.reshape(n_tok, width).astype(jnp.float32)
    norm_two, pull_two = jax.vjp(layer_norm, resid_two, ffn_gain, ffn_shift)
    grad_resid2, grad_ffngain, grad_ffnshift = pull_two(cot_flat)
    grad_ffn = grad_resid2.astype(jnp.bfloat16)
    grad_downbias = jnp.sum(grad_ffn.astype(jnp.float32), 0)
    grad_downweight = rows_dot(act_low, grad_ffn)
    grad_act = back_dot(grad_ffn, down_weight)
    gelu_out, pull_gelu = jax.vjp(gelu_exact, pre_act)
    grad_pre = pull_gelu(grad_act)[0].astype(jnp.bfloat16)
    grad_upbias = jnp.sum(grad_pre.astype(jnp.float32), 0)
    grad_upweight = rows_dot(normed_low, grad_pre)
    grad_normed = grad_resid2 + head_sum_back(back_dot(grad_pre, up_weight))
    norm_one, pull_one = jax.vjp(layer_norm, resid, attn_gain, attn_shift)
    grad_resid, grad_attngain, grad_attnshift = pull_one(grad_normed)
    grad_branch = grad_resid.astype(jnp.bfloat16)
    grad_obias = jnp.sum(grad_branch.astype(jnp.float32), 0)
    grad_oweight = rows_dot(attn_low, grad_branch)
    grad_attn = back_dot(grad_branch, output_weight).astype(jnp.bfloat16)
    grad_heads = grad_attn.reshape(seqs, per_dev, block, heads, hsize).transpose(0, 1, 3, 2, 4)
    global_mask = (first_rows | last_rows)[None, :, None, None, None]
    grad_sparse = jnp.where(global_mask, jnp.zeros((), jnp.bfloat16), grad_heads)
    own_dout = jnp.stack(
        [
            jnp.where(is_first, grad_heads[:, 0].astype(jnp.float32), 0.0),
            jnp.where(is_last, grad_heads[:, per_dev - 1].astype(jnp.float32), 0.0),
        ],
        2,
    ).reshape(seqs, heads, 2 * block, hsize)
    own_delta = jnp.sum(own_dout * end_out, -1)
    end_dout, end_delta = lax.psum((own_dout, own_delta), "seq")
    end_dlow = end_dout.astype(jnp.bfloat16)
    end_prob = jnp.exp(end_raw - end_lse[..., None])
    end_dprob = jnp.einsum(
        "shqd,shkd->shqk", end_dlow, value_local, preferred_element_type=jnp.float32
    )
    end_dscore = (end_prob * (end_dprob - end_delta[..., None]) * 0.125).astype(jnp.bfloat16)
    end_dquery_part = jnp.einsum(
        "shqk,shkd->shqd", end_dscore, key_local, preferred_element_type=jnp.float32
    )
    local_dkey = jnp.einsum(
        "shqk,shqd->shkd", end_dscore, end_query, preferred_element_type=jnp.float32
    )
    local_dvalue = jnp.einsum(
        "shqk,shqd->shkd",
        end_prob,
        end_dout,
        precision=highest_precision,
        preferred_element_type=jnp.float32,
    )
    again = lax.all_to_all(outgoing, "seq", split_axis=0, concat_axis=0, tiled=True)
    back_tiles = pick_tiles(again, recv_index, seqs, per_dev, heads, block, hsize)
    keys_back = assemble(
        end_key, win_key, back_tiles[..., :hsize], seqs, per_dev, heads, block, hsize
    )
    values_back = assemble(
        end_value, win_value, back_tiles[..., hsize:], seqs, per_dev, heads, block, hsize
    )
    grad_prob = jnp.einsum(
        "sbhqd,sbhkd->sbhqk", grad_sparse, values_back, preferred_element_type=jnp.float32
    )
    row_delta = jnp.sum(weights * grad_prob, -1, keepdims=True)
    grad_score = (weights * (grad_prob - row_delta) * 0.125).astype(jnp.bfloat16)
    grad_qblocks = jnp.einsum(
        "sbhqk,sbhkd->sbhqd", grad_score, keys_back, preferred_element_type=jnp.float32
    )
    grad_keysall = jnp.einsum(
        "sbhqk,sbhqd->sbhkd", grad_score, q_blocks, preferred_element_type=jnp.float32
    )
    grad_valsall = jnp.einsum(
        "sbhqk,sbhqd->sbhkd",
        weights,
        grad_sparse.astype(jnp.float32),
        precision=highest_precision,
        preferred_element_type=jnp.float32,
    )
    end_dkey = jnp.sum(grad_keysall[:, :, :, : 2 * block], 1)
    end_dvalue = jnp.sum(grad_valsall[:, :, :, : 2 * block], 1)
    win_grad = jnp.stack(
        [
            grad_keysall[:, :, :, 2 * block : 5 * block].transpose(0, 1, 3, 2, 4),
            grad_valsall[:, :, :, 2 * block : 5 * block].transpose(0, 1, 3, 2, 4),
        ],
        3,
    ).reshape(seqs, per_dev, 3 * block, 2 * hidden)
    rand_grad = (
        jnp.concatenate(
            [
                grad_keysall[:, :, :, 5 * block :].reshape(seqs, per_dev, heads, 3, block, hsize),
                grad_valsall[:, :, :, 5 * block :].reshape(seqs, per_dev, heads, 3, block, hsize),
            ],
            5,
        )
        .reshape(-1, block, 2 * hsize)
        .astype(jnp.bfloat16)
    )
    ext_grad = jnp.zeros((seqs, rows + 2 * block, 2 * hidden), jnp.float32)
    for offset in range(per_dev):
        ext_grad = ext_grad.at[:, offset * block : (offset + 3) * block].add(win_grad[:, offset])
    rims = jnp.concatenate([ext_grad[:, :block], ext_grad[:, rows + block :]], 1)
    returned_rims = with_halo(rims.astype(jnp.bfloat16), (("seq", 1),), block).astype(rims.dtype)
    middle_zero = jnp.zeros((seqs, rows - 2 * block, 2 * hidden), jnp.float32)
    kv_grad = ext_grad[:, block : rows + block] + jnp.concatenate(
        [returned_rims[:, :block], middle_zero, returned_rims[:, 3 * block :]], 1
    )
    sent_back = (
        jnp.zeros((n_dev * capacity, block, 2 * hsize), jnp.bfloat16)
        .at[recv_index]
        .set(rand_grad)
        .reshape(n_dev, capacity, block, 2 * hsize)
    )
    arrived = lax.all_to_all(sent_back, "seq", split_axis=0, concat_axis=0, tiled=True)
    arrived = jnp.where(filled[:, :, None, None], arrived.astype(jnp.float32), 0.0)
    table_grad = (
        jnp.zeros((seqs * per_dev * heads, block, 2 * hsize), jnp.float32)
        .at[send_index.reshape(-1)]
        .add(arrived.reshape(-1, block, 2 * hsize))
    )
    kv_grad = kv_grad + table_grad.reshape(seqs, per_dev, heads, block, 2, hsize).transpose(
        0, 1, 3, 4, 2, 5
    ).reshape(seqs, rows, 2 * hidden)
    kv_grad = kv_grad + jnp.stack(
        [local_dkey.transpose(0, 2, 1, 3), local_dvalue.transpose(0, 2, 1, 3)], 2
    ).reshape(seqs, rows, 2 * hidden)
    end_dquery, end_dkey_all, end_dvalue_all = (
        lax.psum(end_dquery_part.astype(jnp.bfloat16), "seq").astype(jnp.float32),
        lax.psum(end_dkey.astype(jnp.bfloat16), "seq").astype(jnp.float32),
        lax.psum(end_dvalue.astype(jnp.bfloat16), "seq").astype(jnp.float32),
    )
    end_kv = jnp.stack(
        [end_dkey_all.transpose(0, 2, 1, 3), end_dvalue_all.transpose(0, 2, 1, 3)], 2
    ).reshape(seqs, 2 * block, 2 * hidden)
    kv_grad = kv_grad + jnp.concatenate(
        [
            jnp.where(is_first, end_kv[:, :block], 0.0),
            middle_zero,
            jnp.where(is_last, end_kv[:, block:], 0.0),
        ],
        1,
    )
    end_q = end_dquery.transpose(0, 2, 1, 3).reshape(seqs, 2 * block, hidden)
    query_zero = jnp.zeros((seqs, rows - 2 * block, hidden), jnp.float32)
    grad_query = grad_qblocks.transpose(0, 1, 3, 2, 4).reshape(seqs, rows, hidden)
    grad_query = grad_query + jnp.concatenate(
        [
            jnp.where(is_first, end_q[:, :block], 0.0),
            query_zero,
            jnp.where(is_last, end_q[:, block:], 0.0),
        ],
        1,
    )
    query_glow = grad_query.reshape(n_tok, hidden).astype(jnp.bfloat16)
    kv_glow = kv_grad.reshape(n_tok, 2 * hidden).astype(jnp.bfloat16)
    key_glow = kv_glow[:, :hidden]
    value_glow = kv_glow[:, hidden:]
    grad_qbias = jnp.sum(query_glow.astype(jnp.float32), 0)
    grad_vbias = jnp.sum(value_glow.astype(jnp.float32), 0)
    grad_qweight = rows_dot(flat, query_glow)
    grad_kweight = rows_dot(flat, key_glow)
    grad_vweight = rows_dot(flat, value_glow)
    into_tokens = (
        back_dot(query_glow, query_weight)
        + back_dot(key_glow, key_weight)
        + back_dot(value_glow, value_weight)
    )
    input_grad = (grad_resid + head_sum_back(into_tokens)).reshape(seqs, rows, width)
    totals = lax.psum(
        (
            grad_qweight,
            grad_qbias,
            grad_kweight,
            grad_vweight,
            grad_vbias,
            grad_oweight,
            grad_obias,
            grad_attngain,
            grad_attnshift,
            grad_upweight,
            grad_upbias,
            grad_downweight,
            grad_downbias,
            grad_ffngain,
            grad_ffnshift,
        ),
        "seq",
    )
    return (
        layer_output,
        input_grad,
        totals[0],
        totals[1],
        totals[2],
        totals[3],
        totals[4],
        totals[5],
        totals[6],
        totals[7],
        totals[8],
        totals[9],
        totals[10],
        totals[11],
        totals[12],
        totals[13],
        totals[14],
    )


HALF_ROOT = 0.7071067811865476
PDF_SCALE = 0.3989422804014327


def attend_kernel(q_ref, ko_ref, kx_ref, vo_ref, vx_ref, bo_ref, bx_ref, o_ref, lse_ref):
    span = q_ref.shape[0]
    blocks = span // BLOCK
    lane = lax.broadcasted_iota(jnp.int32, (1, 2 * HD), 1) // HD
    vo_t = vo_ref[...].T
    vx_t = vx_ref[...].T
    outs = []
    for h in range(2):
        qh = (jnp.where(lane == h, q_ref[...], 0.0) * 0.125).astype(jnp.bfloat16)

        def scores(k_ref, b_ref):
            raw = back_dot(k_ref[...], qh).reshape(blocks, BLOCK, span)
            return (raw + b_ref[h][:, None, :]).reshape(span, span)

        so = scores(ko_ref, bo_ref)
        sx = scores(kx_ref, bx_ref)
        top = jnp.maximum(jnp.max(so, 0, keepdims=True), jnp.max(sx, 0, keepdims=True))
        po = jnp.exp(so - top)
        px = jnp.exp(sx - top)
        total = jnp.sum(po, 0, keepdims=True) + jnp.sum(px, 0, keepdims=True)
        rows = slice(h * HD, (h + 1) * HD)
        acc = plain_dot(vo_t[rows], po.astype(jnp.bfloat16))
        acc = acc + plain_dot(vx_t[rows], px.astype(jnp.bfloat16))
        outs.append(acc / total)
        lse_ref[0, h : h + 1, :] = top + jnp.log(total)
    o_ref[...] = jnp.concatenate(outs, 0).T.astype(jnp.bfloat16)


def attend_back_kernel(
    q_ref, ko_ref, kx_ref, vo_ref, vx_ref, bo_ref, bx_ref, lse_ref, o_ref, g_ref,
    dq_ref, dko_ref, dkx_ref, dvo_ref, dvx_ref,
):
    span = q_ref.shape[0]
    blocks = span // BLOCK
    lane = lax.broadcasted_iota(jnp.int32, (1, 2 * HD), 1) // HD
    weighted = (o_ref[...].astype(jnp.float32) * g_ref[...].astype(jnp.float32)).T
    parts = ((ko_ref, vo_ref, bo_ref), (kx_ref, vx_ref, bx_ref))
    k_ts = [k_ref[...].T for k_ref, _, _ in parts]
    dks = [None, None]
    dvs = [None, None]
    dq_ts = []
    for h in range(2):
        mine = lane == h
        rows = slice(h * HD, (h + 1) * HD)
        qh = (jnp.where(mine, q_ref[...], 0.0) * 0.125).astype(jnp.bfloat16)
        gh = jnp.where(mine, g_ref[...], 0.0).astype(jnp.bfloat16)
        delta = jnp.sum(weighted[rows], 0, keepdims=True)
        lse = lse_ref[0, h : h + 1, :]
        dq_t = None
        for at, (k_ref, v_ref, b_ref) in enumerate(parts):
            raw = back_dot(k_ref[...], qh).reshape(blocks, BLOCK, span)
            raw = (raw + b_ref[h][:, None, :]).reshape(span, span)
            prob = jnp.exp(raw - lse)
            dprob = back_dot(v_ref[...], gh)
            dscore = (prob * (dprob - delta)).astype(jnp.bfloat16)
            dv = plain_dot(prob.astype(jnp.bfloat16), gh)
            dk = plain_dot(dscore, qh)
            dvs[at] = dv if dvs[at] is None else dvs[at] + dv
            dks[at] = dk if dks[at] is None else dks[at] + dk
            piece = plain_dot(k_ts[at][rows], dscore)
            dq_t = piece if dq_t is None else dq_t + piece
        dq_ts.append(dq_t * 0.125)
    dq_ref[...] = jnp.concatenate(dq_ts, 0).T.astype(dq_ref.dtype)
    for ref, value in ((dko_ref, dks[0]), (dkx_ref, dks[1]), (dvo_ref, dvs[0]), (dvx_ref, dvs[1])):
        ref[...] = value.astype(ref.dtype)


def pair_specs(span, blocks):
    tile = pl.BlockSpec((span, 2 * HD), lambda i: (0, i))
    bias = pl.BlockSpec((2, blocks, span), lambda i: (i, 0, 0))
    lse = pl.BlockSpec((1, 2, span), lambda i: (i, 0, 0))
    return tile, bias, lse


def attend(q, ko, kx, vo, vx, bo, bx):
    span, width = q.shape
    heads = width // HD
    tile, bias, lse = pair_specs(span, span // BLOCK)
    return pl.pallas_call(
        attend_kernel,
        grid=(heads // 2,),
        in_specs=[tile] * 5 + [bias] * 2,
        out_specs=[tile, lse],
        out_shape=[
            jax.ShapeDtypeStruct((span, width), jnp.bfloat16),
            jax.ShapeDtypeStruct((heads // 2, 2, span), jnp.float32),
        ],
        compiler_params=pltpu.CompilerParams(vmem_limit_bytes=48 * 2**20),
        cost_estimate=pl.CostEstimate(
            flops=heads * span * span * 2 * 2 * 2 * HD * 4,
            bytes_accessed=span * width * 12,
            transcendentals=heads * span * span * 2,
        ),
    )(q, ko, kx, vo, vx, bo, bx)


def attend_back(q, ko, kx, vo, vx, bo, bx, lse_all, o, g):
    span, width = q.shape
    heads = width // HD
    tile, bias, lse = pair_specs(span, span // BLOCK)
    low = jax.ShapeDtypeStruct((span, width), jnp.bfloat16)
    full = jax.ShapeDtypeStruct((span, width), jnp.float32)
    return pl.pallas_call(
        attend_back_kernel,
        grid=(heads // 2,),
        in_specs=[tile] * 5 + [bias] * 2 + [lse] + [tile] * 2,
        out_specs=[tile] * 5,
        out_shape=[low, full, low, full, low],
        compiler_params=pltpu.CompilerParams(vmem_limit_bytes=48 * 2**20),
        cost_estimate=pl.CostEstimate(
            flops=heads * span * span * 2 * 2 * 5 * HD * 4,
            bytes_accessed=span * width * 30,
            transcendentals=heads * span * span * 2,
        ),
    )(q, ko, kx, vo, vx, bo, bx, lse_all, o, g)


def swap(piece, bits):
    size = lax.axis_size("tp")
    return lax.ppermute(piece, "tp", [(i, i ^ bits) for i in range(size)])


def gathered_over_tp(own):
    far = swap(own, 2)
    return own, swap(own, 1), far, swap(far, 1)


def by_core(parts, core):
    swapped = (parts[1], parts[0], parts[3], parts[2])
    return [jnp.where(core == 0, a, b) for a, b in zip(parts, swapped)]


def seq_exchange(pieces, sign):
    size = lax.axis_size("seq")
    return [pieces[0]] + [
        lax.ppermute(pieces[k], "seq", [(i, (i + sign * k) % size) for i in range(size)])
        for k in range(1, size)
    ]


def norm_parts(resid):
    centre = resid - jnp.mean(resid, -1, keepdims=True)
    inverse = lax.rsqrt(jnp.mean(centre * centre, -1, keepdims=True) + norm_eps)
    return centre * inverse, inverse


def norm_back(grad, unit, inverse, gain):
    scaled = grad * gain
    pull = scaled - jnp.mean(scaled, -1, keepdims=True)
    pull = pull - unit * jnp.mean(scaled * unit, -1, keepdims=True)
    return pull * inverse, jnp.sum(grad * unit, 0), jnp.sum(grad, 0)


def key_bias(ids, query_ids, key_ids, n_blocks):
    b = query_ids[None, None, :]
    k = key_ids[None, :, None]
    one = lambda flag: flag.astype(jnp.int32)
    count = (
        one(k == 0)
        + one(k == n_blocks - 1)
        + one((k == b - 1) & (b != 1))
        + one(k == b)
        + one((k == b + 1) & (b != n_blocks - 2))
    )
    for at in range(3):
        count = count + one(ids[:, None, :, at] == k)
    whole = (b == 0) | (b == n_blocks - 1)
    count = jnp.where(whole, 1, count).astype(jnp.float32)
    bias = jnp.where(count > 0, jnp.log(jnp.maximum(count, 1.0)), masked_score)
    return jnp.repeat(bias, BLOCK, axis=2)


def whole_sequences(
    tokens,
    rand_blocks,
    query_weight,
    query_bias,
    key_weight,
    value_weight,
    value_bias,
    output_weight,
    output_bias,
    attn_gain,
    attn_shift,
    up_weight,
    up_bias,
    down_weight,
    down_bias,
    ffn_gain,
    ffn_shift,
    cotangent,
):
    seqs, rows, width = tokens.shape
    n_dev = lax.axis_size("seq")
    me = lax.axis_index("seq")
    t = lax.axis_index("tp")
    side, core = t // 2, t % 2
    n_blocks = rows // BLOCK * n_dev
    hidden = query_weight.shape[1]
    units = up_weight.shape[1]
    span = n_dev * BLOCK

    def to_owner(array):
        cut = array.reshape(n_dev, 2, 2, BLOCK, width)
        cut = lax.dynamic_index_in_dim(cut, side, 1, False)
        cut = lax.dynamic_index_in_dim(cut, core, 1, False)
        pieces = [
            lax.dynamic_index_in_dim(cut, (me + k) % n_dev, 0, False) for k in range(n_dev)
        ]
        return jnp.concatenate(seq_exchange(pieces, 1), 0)

    x = to_owner(tokens)
    qkv_own = jnp.concatenate([query_weight.T, key_weight.T, value_weight.T], 0)
    qkv_w = by_core(gathered_over_tp(qkv_own), core)
    cot = to_owner(cotangent)

    flat_rand = rand_blocks.reshape(seqs, -1).astype(jnp.float32)
    small_own = jnp.concatenate([query_bias, value_bias, up_bias])

    def small_for(bits):
        sid = 2 * me + (t ^ bits) // 2
        row = lax.dynamic_index_in_dim(flat_rand, sid, 0, False)
        return jnp.concatenate([row, small_own])

    smalls = [small_for(0)] + [swap(small_for(bits), bits) for bits in (1, 2, 3)]
    smalls = by_core(smalls, core)
    n_rand = flat_rand.shape[1]
    ids = jnp.stack([s[:n_rand] for s in smalls]).astype(jnp.int32)
    heads_dev = hidden // HD
    ids = ids.reshape(4, n_dev, 2, heads_dev, 3)
    ids = lax.dynamic_index_in_dim(ids, core, 2, False)
    source = (me - jnp.arange(n_dev, dtype=jnp.int32)) % n_dev
    ids = jnp.take(ids, source, 1).transpose(0, 2, 1, 3).reshape(4 * heads_dev, n_dev, 3)
    q_bias = jnp.concatenate([s[n_rand : n_rand + hidden] for s in smalls])
    v_bias = jnp.concatenate([s[n_rand + hidden : n_rand + 2 * hidden] for s in smalls])
    u_bias = jnp.concatenate([s[n_rand + 2 * hidden :] for s in smalls])
    own_ids = 2 * source + core
    bias_own = key_bias(ids, own_ids, own_ids, n_blocks)
    bias_far = key_bias(ids, own_ids, 2 * source + 1 - core, n_blocks)

    wq = jnp.concatenate([w[:hidden] for w in qkv_w], 0)
    wk = jnp.concatenate([w[hidden : 2 * hidden] for w in qkv_w], 0)
    wv = jnp.concatenate([w[2 * hidden :] for w in qkv_w], 0)
    k_own = back_dot(x, wk).astype(jnp.bfloat16)
    v_own = (back_dot(x, wv) + v_bias).astype(jnp.bfloat16)
    k_far, v_far = swap(k_own, 1), swap(v_own, 1)
    q = (back_dot(x, wq) + q_bias).astype(jnp.bfloat16)

    wo = jnp.concatenate(by_core(gathered_over_tp(output_weight), core), 0)
    w_up = jnp.concatenate(by_core(gathered_over_tp(up_weight), core), 1)
    w_down = jnp.concatenate(by_core(gathered_over_tp(down_weight), core), 0)

    attn_low, lse = attend(q, k_own, k_far, v_own, v_far, bias_own, bias_far)
    branch = plain_dot(attn_low, wo) + output_bias
    unit_one, inverse_one = norm_parts(x.astype(jnp.float32) + branch)
    normed = unit_one * attn_gain + attn_shift
    normed_low = normed.astype(jnp.bfloat16)
    pre_act = plain_dot(normed_low, w_up) + u_bias
    cdf = 0.5 * (1.0 + lax.erf(pre_act * HALF_ROOT))
    act_low = (pre_act * cdf).astype(jnp.bfloat16)
    slope = (cdf + pre_act * (PDF_SCALE * jnp.exp(-0.5 * pre_act * pre_act))).astype(jnp.bfloat16)
    ffn = plain_dot(act_low, w_down) + down_bias
    unit_two, inverse_two = norm_parts(normed + ffn)
    out_low = (unit_two * ffn_gain + ffn_shift).astype(jnp.bfloat16)

    g_resid2, grad_ffngain, grad_ffnshift = norm_back(
        cot.astype(jnp.float32), unit_two, inverse_two, ffn_gain
    )
    g_ffn = g_resid2.astype(jnp.bfloat16)
    grad_downbias = jnp.sum(g_ffn.astype(jnp.float32), 0)
    grad_down = rows_dot(act_low, g_ffn)
    g_pre = (back_dot(g_ffn, w_down) * slope.astype(jnp.float32)).astype(jnp.bfloat16)
    grad_upbias = jnp.sum(g_pre.astype(jnp.float32), 0)
    grad_up = [
        rows_dot(normed_low, g_pre[:, r * units : (r + 1) * units]) for r in range(4)
    ]

    def reduced(parts):
        parts = by_core(parts, core)
        near = swap(jnp.concatenate([parts[1], parts[3]], 0).astype(jnp.bfloat16), 1)
        height = parts[0].shape[0]
        mine = parts[0] + near[:height].astype(jnp.float32)
        other = parts[2] + near[height:].astype(jnp.float32)
        mine = mine + swap(other.astype(jnp.bfloat16), 2).astype(jnp.float32)
        return lax.psum(mine.astype(jnp.bfloat16), "seq").astype(jnp.float32)

    ffn_total = reduced(
        [
            jnp.concatenate([grad_down[r * units : (r + 1) * units], grad_up[r]], 0)
            for r in range(4)
        ]
    )
    g_normed = g_resid2 + back_dot(g_pre, w_up)
    g_resid, grad_attngain, grad_attnshift = norm_back(g_normed, unit_one, inverse_one, attn_gain)
    g_branch = g_resid.astype(jnp.bfloat16)
    grad_obias = jnp.sum(g_branch.astype(jnp.float32), 0)
    grad_o = rows_dot(attn_low, g_branch)
    g_attn = back_dot(g_branch, wo).astype(jnp.bfloat16)

    dq, dk_own, dk_far, dv_own, dv_far = attend_back(
        q, k_own, k_far, v_own, v_far, bias_own, bias_far, lse, attn_low, g_attn
    )
    dk = (dk_own + swap(dk_far, 1).astype(jnp.float32)).astype(jnp.bfloat16)
    dv = (dv_own + swap(dv_far, 1).astype(jnp.float32)).astype(jnp.bfloat16)
    grad_qbias = jnp.sum(dq.astype(jnp.float32), 0)
    grad_vbias = jnp.sum(dv.astype(jnp.float32), 0)
    grad_q = rows_dot(dq, x)
    grad_k = rows_dot(dk, x)
    grad_v = rows_dot(dv, x)
    input_grad = g_resid + plain_dot(dq, wq) + plain_dot(dk, wk) + plain_dot(dv, wv)
    attn_total = reduced(
        [
            jnp.concatenate([m[r * hidden : (r + 1) * hidden] for m in (grad_o, grad_q, grad_k, grad_v)], 0)
            for r in range(4)
        ]
    )

    def absolute(vector):
        parts = vector.reshape(4, -1)
        return jnp.take(parts, jnp.arange(4) ^ (2 * side), 0).reshape(-1)

    small_total = lax.psum(
        jnp.concatenate(
            [
                absolute(grad_qbias),
                absolute(grad_vbias),
                absolute(grad_upbias),
                grad_obias,
                grad_attngain,
                grad_attnshift,
                grad_downbias,
                grad_ffngain,
                grad_ffnshift,
            ]
        ),
        ("seq", "tp"),
    )

    def share(start, size):
        whole = small_total[start : start + 4 * size].reshape(4, size)
        return lax.dynamic_index_in_dim(whole, t, 0, False)

    tail = 8 * hidden + 4 * units
    rep = [small_total[tail + i * width : tail + (i + 1) * width] for i in range(6)]

    def from_owner(array):
        pieces = [array[k * BLOCK : (k + 1) * BLOCK] for k in range(n_dev)]
        got = jnp.stack(seq_exchange(pieces, -1))
        got = lax.dynamic_slice_in_dim(
            jnp.concatenate([got, got], 0), (n_dev - me) % n_dev, n_dev, 0
        )
        r0, r1, r2, r3 = gathered_over_tp(got)
        near = jnp.where(core == 0, jnp.stack([r0, r1], 1), jnp.stack([r1, r0], 1))
        far = jnp.where(core == 0, jnp.stack([r2, r3], 1), jnp.stack([r3, r2], 1))
        both = jnp.where(side == 0, jnp.stack([near, far], 1), jnp.stack([far, near], 1))
        return both.reshape(seqs, rows, width)

    layer_output = from_owner(out_low)
    input_out = from_owner(input_grad.astype(jnp.bfloat16)).astype(jnp.float32)
    g_o, g_q, g_k, g_v = (attn_total[i * hidden : (i + 1) * hidden] for i in range(4))
    return (
        layer_output,
        input_out,
        g_q.T,
        share(0, hidden),
        g_k.T,
        g_v.T,
        share(4 * hidden, hidden),
        g_o,
        rep[0],
        rep[1],
        rep[2],
        ffn_total[units:],
        share(8 * hidden, units),
        ffn_total[:units],
        rep[3],
        rep[4],
        rep[5],
    )


def per_device(tokens, *rest):
    seqs, rows, _ = tokens.shape
    n_dev = lax.axis_size("seq")
    if lax.axis_size("tp") == 4 and seqs == 2 * n_dev and rows == 2 * BLOCK:
        return whole_sequences(tokens, *rest)
    return split_sequences(tokens, *rest)


def solution(mesh):
    placed = (
        P(None, "seq", None),
        P(None, None, "tp", None),
        P(None, "tp"),
        P("tp"),
        P(None, "tp"),
        P(None, "tp"),
        P("tp"),
        P("tp", None),
        P(),
        P(),
        P(),
        P(None, "tp"),
        P("tp"),
        P("tp", None),
        P(),
        P(),
        P(),
        P(None, "seq", None),
    )
    return jax.shard_map(
        per_device,
        mesh=mesh,
        in_specs=placed,
        out_specs=(
            P(None, "seq", None),
            P(None, "seq", None),
            P(None, "tp"),
            P("tp"),
            P(None, "tp"),
            P(None, "tp"),
            P("tp"),
            P("tp", None),
            P(),
            P(),
            P(),
            P(None, "tp"),
            P("tp"),
            P("tp", None),
            P(),
            P(),
            P(),
        ),
        check_vma=False,
    )
```

```python
from functools import partial

import jax
import jax.numpy as jnp
from jax import lax
from jax.sharding import PartitionSpec as P
from jax.experimental import pallas as pl
from jax.experimental.pallas import tpu as pltpu

HD = 64
BLOCK = 64


norm_eps = 1e-06
masked_score = -1e30
highest_precision = lax.Precision.HIGHEST


def with_halo(shard, sides, width):
    for axis, dim in sides:
        size, length = (lax.axis_size(axis), shard.shape[dim])
        up = [(i, (i + 1) % size) for i in range(size - 1)]
        down = [(j, i) for i, j in up]
        last = lax.slice_in_dim(shard, length - width, length, axis=dim)
        first = lax.slice_in_dim(shard, 0, width, axis=dim)
        before = lax.ppermute(last, axis, up)
        after = lax.ppermute(first, axis, down)
        shard = jnp.concatenate([before, shard, after], axis=dim)
    return shard


def joined(shard, axis, combine):
    everything = jax.tree.map(lambda part: lax.all_gather(part, axis), shard)
    first = jax.tree.map(lambda part: part[0], everything)

    def hop(k, so_far):
        return combine(so_far, jax.tree.map(lambda part: part[k], everything))

    return lax.fori_loop(1, lax.axis_size(axis), hop, first)


def layer_norm(resid, gain, shift):
    centre = resid - jnp.mean(resid, -1, keepdims=True)
    spread = jnp.mean(centre * centre, -1, keepdims=True)
    return centre * lax.rsqrt(spread + norm_eps) * gain + shift


def gelu_exact(values):
    return jax.nn.gelu(values, approximate=False)


def plain_dot(left, right):
    return jnp.dot(left, right, preferred_element_type=jnp.float32)


def rows_dot(left, right):
    return lax.dot_general(
        left, right, (((0,), (0,)), ((), ())), preferred_element_type=jnp.float32
    )


def back_dot(left, right):
    return lax.dot_general(
        left, right, (((1,), (1,)), ((), ())), preferred_element_type=jnp.float32
    )


def softmax_row_probs(scores):
    top_score = jnp.max(scores, -1, keepdims=True)
    expo = jnp.exp(scores - top_score)
    return expo / jnp.sum(expo, -1, keepdims=True)


def head_sum_fwd(pieces):
    return lax.psum(pieces, "tp")


def head_sum_back(pieces):
    return lax.psum(pieces, "tp")


def merge_rows(first, second):
    top_score = jnp.maximum(first[0], second[0])
    scale_one = jnp.exp(first[0] - top_score)
    scale_two = jnp.exp(second[0] - top_score)
    return (
        top_score,
        first[1] * scale_one + second[1] * scale_two,
        first[2] * scale_one[..., None] + second[2] * scale_two[..., None],
    )


def tile_plan(rand_blocks, my_index, n_dev, per_dev, seqs, heads):
    count = seqs * per_dev * heads * 3
    capacity = max(2, 2 * count // n_dev)
    requests = (
        rand_blocks.reshape(seqs, n_dev, per_dev, heads, 3)
        .transpose(1, 0, 2, 3, 4)
        .reshape(n_dev, count)
    )
    is_mine = requests // per_dev == my_index
    ranking = jnp.cumsum(is_mine.astype(jnp.int32), 1) - 1
    slot_ids = jnp.arange(capacity, dtype=jnp.int32)
    select = is_mine[:, None, :] & (ranking[:, None, :] == slot_ids[None, :, None])
    filled = jnp.any(select, 2)
    position = jnp.arange(count, dtype=jnp.int32)
    seq_of = position // (per_dev * heads * 3)
    head_of = position // 3 % heads
    tile_of = (seq_of[None, :] * per_dev + requests % per_dev) * heads + head_of[None, :]
    send_index = jnp.sum(jnp.where(select, tile_of[:, None, :], 0), 2)
    own_requests = lax.dynamic_slice_in_dim(rand_blocks, my_index * per_dev, per_dev, 1).reshape(
        count
    )
    own_owner = own_requests // per_dev
    onehot = (own_owner[:, None] == jnp.arange(n_dev, dtype=jnp.int32)[None, :]).astype(jnp.int32)
    own_rank = jnp.sum((jnp.cumsum(onehot, 0) - 1) * onehot, 1)
    recv_index = own_owner * capacity + own_rank
    return (capacity, send_index, filled, recv_index)


def pick_tiles(incoming, recv_index, seqs, per_dev, heads, block, hsize):
    stacked = incoming.reshape(-1, block, 2 * hsize)
    return jnp.take(stacked, recv_index, 0).reshape(seqs, per_dev, heads, 3, block, 2 * hsize)


def assemble(end_part, window_part, tile_part, seqs, per_dev, heads, block, hsize):
    ends_wide = jnp.broadcast_to(end_part[:, None], (seqs, per_dev, heads, 2 * block, hsize))
    return jnp.concatenate(
        [ends_wide, window_part, tile_part.reshape(seqs, per_dev, heads, 3 * block, hsize)], 3
    )


def split_sequences(
    tokens,
    rand_blocks,
    query_weight,
    query_bias,
    key_weight,
    value_weight,
    value_bias,
    output_weight,
    output_bias,
    attn_gain,
    attn_shift,
    up_weight,
    up_bias,
    down_weight,
    down_bias,
    ffn_gain,
    ffn_shift,
    cotangent,
):
    seqs, rows, width = tokens.shape
    block = BLOCK
    hsize = HD
    per_dev = rows // block
    n_dev = lax.axis_size("seq")
    my_index = lax.axis_index("seq")
    n_blocks = per_dev * n_dev
    heads = query_weight.shape[1] // hsize
    hidden = heads * hsize
    n_tok = seqs * rows
    is_first = my_index == 0
    is_last = my_index == n_dev - 1
    flat = tokens.reshape(n_tok, width)
    query_low = (plain_dot(flat, query_weight) + query_bias).astype(jnp.bfloat16)
    key_low = plain_dot(flat, key_weight).astype(jnp.bfloat16)
    value_low = (plain_dot(flat, value_weight) + value_bias).astype(jnp.bfloat16)
    keyval = jnp.concatenate([key_low, value_low], 1).reshape(seqs, rows, 2 * hidden)
    extended = with_halo(keyval, (("seq", 1),), block)
    windows = jnp.stack(
        [extended[:, offset * block : (offset + 3) * block] for offset in range(per_dev)], 1
    )
    windows = windows.reshape(seqs, per_dev, 3 * block, 2, heads, hsize)
    win_key = windows[:, :, :, 0].transpose(0, 1, 3, 2, 4)
    win_value = windows[:, :, :, 1].transpose(0, 1, 3, 2, 4)
    triple = jnp.concatenate([query_low.reshape(seqs, rows, hidden), keyval], 2).astype(jnp.float32)
    own_ends = jnp.stack(
        [
            jnp.where(is_first, triple[:, :block], 0.0),
            jnp.where(is_last, triple[:, rows - block :], 0.0),
        ],
        1,
    )
    ends = lax.psum(own_ends.astype(jnp.bfloat16), "seq").reshape(seqs, 2, block, 3, heads, hsize)
    end_query = ends[:, :, :, 0].transpose(0, 3, 1, 2, 4).reshape(seqs, heads, 2 * block, hsize)
    end_key = ends[:, :, :, 1].transpose(0, 3, 1, 2, 4).reshape(seqs, heads, 2 * block, hsize)
    end_value = ends[:, :, :, 2].transpose(0, 3, 1, 2, 4).reshape(seqs, heads, 2 * block, hsize)
    capacity, send_index, filled, recv_index = tile_plan(
        rand_blocks, my_index, n_dev, per_dev, seqs, heads
    )
    table = (
        keyval.reshape(seqs, per_dev, block, 2, heads, hsize)
        .transpose(0, 1, 4, 2, 3, 5)
        .reshape(seqs * per_dev * heads, block, 2 * hsize)
    )
    outgoing = jnp.take(table, send_index.reshape(-1), 0).reshape(n_dev, capacity, block, 2 * hsize)
    outgoing = jnp.where(filled[:, :, None, None], outgoing, jnp.zeros((), jnp.bfloat16))
    incoming = lax.all_to_all(outgoing, "seq", split_axis=0, concat_axis=0, tiled=True)
    tiles = pick_tiles(incoming, recv_index, seqs, per_dev, heads, block, hsize)
    q_blocks = query_low.reshape(seqs, per_dev, block, heads, hsize).transpose(0, 1, 3, 2, 4)
    keys_all = assemble(end_key, win_key, tiles[..., :hsize], seqs, per_dev, heads, block, hsize)
    values_all = assemble(
        end_value, win_value, tiles[..., hsize:], seqs, per_dev, heads, block, hsize
    )
    block_ids = my_index * per_dev + jnp.arange(per_dev, dtype=jnp.int32)
    slot_ids = jnp.arange(8 * block, dtype=jnp.int32) // block
    dropped = (slot_ids == 2)[None, :] & (block_ids == 1)[:, None] | (slot_ids == 4)[None, :] & (
        block_ids == n_blocks - 2
    )[:, None]
    unscaled_scores = (
        jnp.einsum("sbhqd,sbhkd->sbhqk", q_blocks, keys_all, preferred_element_type=jnp.float32)
        * 0.125
    )
    unscaled_scores = jnp.where(dropped[None, :, None, None, :], masked_score, unscaled_scores)
    weights = softmax_row_probs(unscaled_scores)
    sparse_attention = jnp.einsum(
        "sbhqk,sbhkd->sbhqd",
        weights,
        values_all.astype(jnp.float32),
        precision=highest_precision,
        preferred_element_type=jnp.float32,
    )
    key_local = key_low.reshape(seqs, rows, heads, hsize).transpose(0, 2, 1, 3)
    value_local = value_low.reshape(seqs, rows, heads, hsize).transpose(0, 2, 1, 3)
    end_raw = (
        jnp.einsum("shqd,shkd->shqk", end_query, key_local, preferred_element_type=jnp.float32)
        * 0.125
    )
    end_top = jnp.max(end_raw, -1)
    end_expo = jnp.exp(end_raw - end_top[..., None])
    end_total = jnp.sum(end_expo, -1)
    end_acc = jnp.einsum(
        "shqk,shkd->shqd",
        end_expo,
        value_local.astype(jnp.float32),
        precision=highest_precision,
        preferred_element_type=jnp.float32,
    )
    merged_top, merged_total, merged_acc = joined((end_top, end_total, end_acc), "seq", merge_rows)
    end_out = merged_acc / merged_total[..., None]
    end_lse = merged_top + jnp.log(merged_total)
    end_split = end_out.reshape(seqs, heads, 2, block, hsize)
    first_rows = block_ids == 0
    last_rows = block_ids == n_blocks - 1
    attn = jnp.where(
        first_rows[None, :, None, None, None], end_split[:, None, :, 0], sparse_attention
    )
    attn = jnp.where(last_rows[None, :, None, None, None], end_split[:, None, :, 1], attn)
    attn_low = attn.transpose(0, 1, 3, 2, 4).reshape(n_tok, hidden).astype(jnp.bfloat16)
    branch = head_sum_fwd(plain_dot(attn_low, output_weight)) + output_bias
    resid = flat.astype(jnp.float32) + branch
    normed = layer_norm(resid, attn_gain, attn_shift)
    normed_low = normed.astype(jnp.bfloat16)
    pre_act = plain_dot(normed_low, up_weight) + up_bias
    act_low = gelu_exact(pre_act).astype(jnp.bfloat16)
    ffn = head_sum_fwd(plain_dot(act_low, down_weight)) + down_bias
    resid_two = normed + ffn
    layer_output = (
        layer_norm(resid_two, ffn_gain, ffn_shift).astype(jnp.bfloat16).reshape(seqs, rows, width)
    )
    cot_flat = cotangent.reshape(n_tok, width).astype(jnp.float32)
    norm_two, pull_two = jax.vjp(layer_norm, resid_two, ffn_gain, ffn_shift)
    grad_resid2, grad_ffngain, grad_ffnshift = pull_two(cot_flat)
    grad_ffn = grad_resid2.astype(jnp.bfloat16)
    grad_downbias = jnp.sum(grad_ffn.astype(jnp.float32), 0)
    grad_downweight = rows_dot(act_low, grad_ffn)
    grad_act = back_dot(grad_ffn, down_weight)
    gelu_out, pull_gelu = jax.vjp(gelu_exact, pre_act)
    grad_pre = pull_gelu(grad_act)[0].astype(jnp.bfloat16)
    grad_upbias = jnp.sum(grad_pre.astype(jnp.float32), 0)
    grad_upweight = rows_dot(normed_low, grad_pre)
    grad_normed = grad_resid2 + head_sum_back(back_dot(grad_pre, up_weight))
    norm_one, pull_one = jax.vjp(layer_norm, resid, attn_gain, attn_shift)
    grad_resid, grad_attngain, grad_attnshift = pull_one(grad_normed)
    grad_branch = grad_resid.astype(jnp.bfloat16)
    grad_obias = jnp.sum(grad_branch.astype(jnp.float32), 0)
    grad_oweight = rows_dot(attn_low, grad_branch)
    grad_attn = back_dot(grad_branch, output_weight).astype(jnp.bfloat16)
    grad_heads = grad_attn.reshape(seqs, per_dev, block, heads, hsize).transpose(0, 1, 3, 2, 4)
    global_mask = (first_rows | last_rows)[None, :, None, None, None]
    grad_sparse = jnp.where(global_mask, jnp.zeros((), jnp.bfloat16), grad_heads)
    own_dout = jnp.stack(
        [
            jnp.where(is_first, grad_heads[:, 0].astype(jnp.float32), 0.0),
            jnp.where(is_last, grad_heads[:, per_dev - 1].astype(jnp.float32), 0.0),
        ],
        2,
    ).reshape(seqs, heads, 2 * block, hsize)
    own_delta = jnp.sum(own_dout * end_out, -1)
    end_dout, end_delta = lax.psum((own_dout, own_delta), "seq")
    end_dlow = end_dout.astype(jnp.bfloat16)
    end_prob = jnp.exp(end_raw - end_lse[..., None])
    end_dprob = jnp.einsum(
        "shqd,shkd->shqk", end_dlow, value_local, preferred_element_type=jnp.float32
    )
    end_dscore = (end_prob * (end_dprob - end_delta[..., None]) * 0.125).astype(jnp.bfloat16)
    end_dquery_part = jnp.einsum(
        "shqk,shkd->shqd", end_dscore, key_local, preferred_element_type=jnp.float32
    )
    local_dkey = jnp.einsum(
        "shqk,shqd->shkd", end_dscore, end_query, preferred_element_type=jnp.float32
    )
    local_dvalue = jnp.einsum(
        "shqk,shqd->shkd",
        end_prob,
        end_dout,
        precision=highest_precision,
        preferred_element_type=jnp.float32,
    )
    again = lax.all_to_all(outgoing, "seq", split_axis=0, concat_axis=0, tiled=True)
    back_tiles = pick_tiles(again, recv_index, seqs, per_dev, heads, block, hsize)
    keys_back = assemble(
        end_key, win_key, back_tiles[..., :hsize], seqs, per_dev, heads, block, hsize
    )
    values_back = assemble(
        end_value, win_value, back_tiles[..., hsize:], seqs, per_dev, heads, block, hsize
    )
    grad_prob = jnp.einsum(
        "sbhqd,sbhkd->sbhqk", grad_sparse, values_back, preferred_element_type=jnp.float32
    )
    row_delta = jnp.sum(weights * grad_prob, -1, keepdims=True)
    grad_score = (weights * (grad_prob - row_delta) * 0.125).astype(jnp.bfloat16)
    grad_qblocks = jnp.einsum(
        "sbhqk,sbhkd->sbhqd", grad_score, keys_back, preferred_element_type=jnp.float32
    )
    grad_keysall = jnp.einsum(
        "sbhqk,sbhqd->sbhkd", grad_score, q_blocks, preferred_element_type=jnp.float32
    )
    grad_valsall = jnp.einsum(
        "sbhqk,sbhqd->sbhkd",
        weights,
        grad_sparse.astype(jnp.float32),
        precision=highest_precision,
        preferred_element_type=jnp.float32,
    )
    end_dkey = jnp.sum(grad_keysall[:, :, :, : 2 * block], 1)
    end_dvalue = jnp.sum(grad_valsall[:, :, :, : 2 * block], 1)
    win_grad = jnp.stack(
        [
            grad_keysall[:, :, :, 2 * block : 5 * block].transpose(0, 1, 3, 2, 4),
            grad_valsall[:, :, :, 2 * block : 5 * block].transpose(0, 1, 3, 2, 4),
        ],
        3,
    ).reshape(seqs, per_dev, 3 * block, 2 * hidden)
    rand_grad = (
        jnp.concatenate(
            [
                grad_keysall[:, :, :, 5 * block :].reshape(seqs, per_dev, heads, 3, block, hsize),
                grad_valsall[:, :, :, 5 * block :].reshape(seqs, per_dev, heads, 3, block, hsize),
            ],
            5,
        )
        .reshape(-1, block, 2 * hsize)
        .astype(jnp.bfloat16)
    )
    ext_grad = jnp.zeros((seqs, rows + 2 * block, 2 * hidden), jnp.float32)
    for offset in range(per_dev):
        ext_grad = ext_grad.at[:, offset * block : (offset + 3) * block].add(win_grad[:, offset])
    rims = jnp.concatenate([ext_grad[:, :block], ext_grad[:, rows + block :]], 1)
    returned_rims = with_halo(rims.astype(jnp.bfloat16), (("seq", 1),), block).astype(rims.dtype)
    middle_zero = jnp.zeros((seqs, rows - 2 * block, 2 * hidden), jnp.float32)
    kv_grad = ext_grad[:, block : rows + block] + jnp.concatenate(
        [returned_rims[:, :block], middle_zero, returned_rims[:, 3 * block :]], 1
    )
    sent_back = (
        jnp.zeros((n_dev * capacity, block, 2 * hsize), jnp.bfloat16)
        .at[recv_index]
        .set(rand_grad)
        .reshape(n_dev, capacity, block, 2 * hsize)
    )
    arrived = lax.all_to_all(sent_back, "seq", split_axis=0, concat_axis=0, tiled=True)
    arrived = jnp.where(filled[:, :, None, None], arrived.astype(jnp.float32), 0.0)
    table_grad = (
        jnp.zeros((seqs * per_dev * heads, block, 2 * hsize), jnp.float32)
        .at[send_index.reshape(-1)]
        .add(arrived.reshape(-1, block, 2 * hsize))
    )
    kv_grad = kv_grad + table_grad.reshape(seqs, per_dev, heads, block, 2, hsize).transpose(
        0, 1, 3, 4, 2, 5
    ).reshape(seqs, rows, 2 * hidden)
    kv_grad = kv_grad + jnp.stack(
        [local_dkey.transpose(0, 2, 1, 3), local_dvalue.transpose(0, 2, 1, 3)], 2
    ).reshape(seqs, rows, 2 * hidden)
    end_dquery, end_dkey_all, end_dvalue_all = (
        lax.psum(end_dquery_part.astype(jnp.bfloat16), "seq").astype(jnp.float32),
        lax.psum(end_dkey.astype(jnp.bfloat16), "seq").astype(jnp.float32),
        lax.psum(end_dvalue.astype(jnp.bfloat16), "seq").astype(jnp.float32),
    )
    end_kv = jnp.stack(
        [end_dkey_all.transpose(0, 2, 1, 3), end_dvalue_all.transpose(0, 2, 1, 3)], 2
    ).reshape(seqs, 2 * block, 2 * hidden)
    kv_grad = kv_grad + jnp.concatenate(
        [
            jnp.where(is_first, end_kv[:, :block], 0.0),
            middle_zero,
            jnp.where(is_last, end_kv[:, block:], 0.0),
        ],
        1,
    )
    end_q = end_dquery.transpose(0, 2, 1, 3).reshape(seqs, 2 * block, hidden)
    query_zero = jnp.zeros((seqs, rows - 2 * block, hidden), jnp.float32)
    grad_query = grad_qblocks.transpose(0, 1, 3, 2, 4).reshape(seqs, rows, hidden)
    grad_query = grad_query + jnp.concatenate(
        [
            jnp.where(is_first, end_q[:, :block], 0.0),
            query_zero,
            jnp.where(is_last, end_q[:, block:], 0.0),
        ],
        1,
    )
    query_glow = grad_query.reshape(n_tok, hidden).astype(jnp.bfloat16)
    kv_glow = kv_grad.reshape(n_tok, 2 * hidden).astype(jnp.bfloat16)
    key_glow = kv_glow[:, :hidden]
    value_glow = kv_glow[:, hidden:]
    grad_qbias = jnp.sum(query_glow.astype(jnp.float32), 0)
    grad_vbias = jnp.sum(value_glow.astype(jnp.float32), 0)
    grad_qweight = rows_dot(flat, query_glow)
    grad_kweight = rows_dot(flat, key_glow)
    grad_vweight = rows_dot(flat, value_glow)
    into_tokens = (
        back_dot(query_glow, query_weight)
        + back_dot(key_glow, key_weight)
        + back_dot(value_glow, value_weight)
    )
    input_grad = (grad_resid + head_sum_back(into_tokens)).reshape(seqs, rows, width)
    totals = lax.psum(
        (
            grad_qweight,
            grad_qbias,
            grad_kweight,
            grad_vweight,
            grad_vbias,
            grad_oweight,
            grad_obias,
            grad_attngain,
            grad_attnshift,
            grad_upweight,
            grad_upbias,
            grad_downweight,
            grad_downbias,
            grad_ffngain,
            grad_ffnshift,
        ),
        "seq",
    )
    return (
        layer_output,
        input_grad,
        totals[0],
        totals[1],
        totals[2],
        totals[3],
        totals[4],
        totals[5],
        totals[6],
        totals[7],
        totals[8],
        totals[9],
        totals[10],
        totals[11],
        totals[12],
        totals[13],
        totals[14],
    )


HALF_ROOT = 0.7071067811865476
PDF_SCALE = 0.3989422804014327


MESH = pl.DeviceIdType.MESH


def place():
    me, t = lax.axis_index("seq"), lax.axis_index("tp")
    side, core = lax.div(t, 2), lax.rem(t, 2)
    return me, t, side, core


def tp_peer(side, core, bits):
    there = 1 - side if bits & 2 else side
    return there * 2 + (1 - core if bits & 1 else core)


def greet(peers):
    barrier = pltpu.get_barrier_semaphore()
    for peer in peers:
        pl.semaphore_signal(barrier, inc=1, device_id=peer, device_id_type=MESH)
    pl.semaphore_wait(barrier, len(peers))


def remote(src, dst, sends, recvs, at, peer):
    return pltpu.make_async_remote_copy(
        src_ref=src,
        dst_ref=dst,
        send_sem=sends.at[at],
        recv_sem=recvs.at[at],
        device_id=peer,
        device_id_type=MESH,
    )


def enter_kernel(
    n_dev, tok, rand, wq, wk, wv, pack,
    x, q, ko, vo, kf, vf, wt_out, packs, ids,
    wt, rand_v, ids_for, tok_send, tok_recv, w_send, w_recv, s_send, s_recv, kv_send, kv_recv, local,
):
    me, t, side, core = place()
    half = lax.rem(me, 2)
    beside = (me + 1 - 2 * half, t)
    near, across = (me, tp_peer(side, core, 1)), (me, tp_peer(side, core, 2))
    hidden = wq.shape[1]
    part = hidden // 2
    greet(
        [(lax.rem(me + k, n_dev), t) for k in range(1, n_dev)]
        + [(me, tp_peer(side, core, bits)) for bits in (1, 2, 3)]
    )
    own_tok = pltpu.make_async_copy(
        tok.at[2 * me + side, pl.ds(core * BLOCK, BLOCK), :], x.at[pl.ds(0, BLOCK), :], local.at[0]
    )
    own_rand = pltpu.make_async_copy(rand.at[pl.ds(2 * me, 2)], rand_v, local.at[1])
    own_rand.start()
    own_tok.start()
    moves = []
    for k in range(1, n_dev):
        to = lax.rem(me + k, n_dev)
        move = remote(
            tok.at[2 * to + side, pl.ds(core * BLOCK, BLOCK), :],
            x.at[pl.ds(k * BLOCK, BLOCK), :],
            tok_send, tok_recv, k - 1, (to, t),
        )
        move.start()
        moves.append(move)

    def rows(h):
        return pl.ds(h * part, part)

    weights = {}
    for m, w in ((1, wk), (2, wv), (0, wq)):
        wt[m, core] = w[...].T
        to_y = remote(
            wt.at[m, core, rows(half)], wt.at[m, 2 + core, rows(half)], w_send, w_recv, (m, 0), across
        )
        to_core = remote(wt.at[m, core], wt.at[m, core], w_send, w_recv, (m, 1), near)
        to_y.start()
        to_core.start()
        weights[m] = [to_y, to_core]

    packs[core] = pack[...]
    own_rand.wait()
    lane = lax.broadcasted_iota(jnp.int32, (1, n_dev * BLOCK), 1)
    for y in range(2):
        for c in range(2):
            tiles = [
                rand_v[y, 2 * lax.rem(me - i + n_dev, n_dev) + c] for i in range(n_dev)
            ]
            for h in range(tiles[0].shape[0]):
                for r in range(3):
                    row = jnp.broadcast_to(tiles[0][h : h + 1, r : r + 1], lane.shape)
                    for i in range(1, n_dev):
                        row = jnp.where(lane // BLOCK == i, tiles[i][h : h + 1, r : r + 1], row)
                    ids_for[2 * y + c, h, r : r + 1, :] = row
    heads = ids_for.shape[1]
    ids[pl.ds(core * heads, heads)] = ids_for[t]
    for bits in (1, 2, 3):
        slot = (bits & 2) + core
        to = tp_peer(side, core, bits)
        for n, (src, dst) in enumerate(
            ((pack, packs.at[slot]), (ids_for.at[to], ids.at[pl.ds(slot * heads, heads)]))
        ):
            move = remote(src, dst, s_send, s_recv, (bits - 1, n), (me, to))
            move.start()
            moves.append(move)

    for m in (1, 2, 0):
        weights[m][0].wait_recv()
        held = wt.at[m, 2 + core, rows(half)]
        for n, peer in ((2, beside), (3, near)):
            move = remote(held, held, w_send, w_recv, (m, n), peer)
            move.start()
            weights[m].append(move)
    for m in (1, 2, 0):
        weights[m][2].wait_recv()
        held = wt.at[m, 2 + core, rows(1 - half)]
        move = remote(held, held, w_send, w_recv, (m, 4), near)
        move.start()
        weights[m].append(move)
    for move in moves:
        move.wait_recv()
    own_tok.wait()

    def bias_of(start):
        return jnp.concatenate([packs[j, :, start : start + hidden] for j in range(4)], 1)

    def project(m):
        for n in (1, 3, 4):
            weights[m][n].wait_recv()
        return back_dot(x[...], wt[m].reshape(4 * hidden, x.shape[1]))

    sends = []
    ko[...] = project(1).astype(jnp.bfloat16)
    sends.append(remote(ko, kf, kv_send, kv_recv, 0, near))
    sends[0].start()
    pad = pack.shape[1] - 2 * hidden
    vo[...] = (project(2) + bias_of(256)).astype(jnp.bfloat16)
    sends.append(remote(vo, vf, kv_send, kv_recv, 1, near))
    sends[1].start()
    q[...] = (project(0) + bias_of(0)).astype(jnp.bfloat16)
    keep = pltpu.make_async_copy(wt, wt_out, local.at[2])
    keep.start()
    for move in sends:
        move.wait_recv()
    for move in moves + sends + [move for m in range(3) for move in weights[m]]:
        move.wait_send()
    keep.wait()


def enter(tokens, rand_blocks, wq, wk, wv, pack, n_dev):
    width = tokens.shape[2]
    span = n_dev * BLOCK
    hidden = wq.shape[1]
    heads = hidden // HD
    vmem = pl.BlockSpec(memory_space=pltpu.VMEM)
    hbm = pl.BlockSpec(memory_space=pl.ANY)
    low = jax.ShapeDtypeStruct((span, width), jnp.bfloat16)
    wt = (3, 4, hidden, width)
    dma = pltpu.SemaphoreType.DMA
    return pl.pallas_call(
        partial(enter_kernel, n_dev),
        in_specs=[hbm, hbm, vmem, vmem, vmem, vmem],
        out_specs=[vmem] * 6 + [hbm, vmem, vmem],
        out_shape=[low] * 6
        + [
            jax.ShapeDtypeStruct(wt, jnp.bfloat16),
            jax.ShapeDtypeStruct((4,) + pack.shape, jnp.float32),
            jax.ShapeDtypeStruct((4 * heads, 3, span), jnp.int32),
        ],
        scratch_shapes=[
            pltpu.VMEM(wt, jnp.bfloat16),
            pltpu.VMEM((2,) + rand_blocks.shape[1:], jnp.int32),
            pltpu.VMEM((4, heads, 3, span), jnp.int32),
            dma((n_dev - 1,)),
            dma((n_dev - 1,)),
            dma((3, 5)),
            dma((3, 5)),
            dma((3, 2)),
            dma((3, 2)),
            dma((2,)),
            dma((2,)),
            dma((3,)),
        ],
        compiler_params=pltpu.CompilerParams(
            collective_id=0, has_side_effects=True, vmem_limit_bytes=48 * 2**20
        ),
    )(tokens, rand_blocks, wq, wk, wv, pack)


def list_bias(ids_ref, h, key_shift, me, core, n_dev, span):
    n_blocks = 2 * n_dev
    row = lax.broadcasted_iota(jnp.int32, (n_dev, span), 0)
    lane = lax.broadcasted_iota(jnp.int32, (n_dev, span), 1)
    wrap = lambda i: lax.rem(me - i + n_dev, n_dev)
    k = 2 * wrap(row) + (1 - core if key_shift else core)
    b = 2 * wrap(lane // BLOCK) + core
    one = lambda flag: jnp.where(flag, 1.0, 0.0)
    count = (
        one(k == 0)
        + one(k == n_blocks - 1)
        + one((k == b - 1) & (b != 1))
        + one(k == b)
        + one((k == b + 1) & (b != n_blocks - 2))
    )
    for r in range(3):
        count = count + one(ids_ref[h, r : r + 1, :] == k)
    count = jnp.where((b == 0) | (b == n_blocks - 1), 1.0, count)
    return jnp.where(count > 0.5, jnp.log(jnp.maximum(count, 1.0)), masked_score)


def attend_gather_kernel(
    n_dev, q_ref, ko_ref, kx_ref, vo_ref, vx_ref, ids_ref, cot, wo, up, down,
    o_ref, lse_ref, cot_out, wo_out, up_out, down_out,
    c_send, c_recv, w_send, w_recv, local,
):
    me, t, side, core = place()
    step = pl.program_id(0)
    last = pl.num_programs(0) - 1
    half = lax.rem(me, 2)
    beside = (me + 1 - 2 * half, t)
    near, across = (me, tp_peer(side, core, 1)), (me, tp_peer(side, core, 2))
    tall = wo.shape[0]
    units = down.shape[0]
    part = units // 4

    def cot_moves():
        return [
            remote(
                cot.at[2 * lax.rem(me + k, n_dev) + side, pl.ds(core * BLOCK, BLOCK), :],
                cot_out.at[pl.ds(k * BLOCK, BLOCK), :],
                c_send, c_recv, k - 1, (lax.rem(me + k, n_dev), t),
            )
            for k in range(1, n_dev)
        ]

    def local_moves():
        pairs = (
            (cot.at[2 * me + side, pl.ds(core * BLOCK, BLOCK), :], cot_out.at[pl.ds(0, BLOCK), :]),
            (wo, slot(0, core)),
            (up, slot(1, core)),
            (down, slot(2, core)),
        )
        return [pltpu.make_async_copy(a, b, local.at[n]) for n, (a, b) in enumerate(pairs)]

    def slot(m, j, start=None):
        if m == 0:
            return wo_out.at[pl.ds(j * tall, tall), :]
        rows = pl.ds(0, units) if start is None else pl.ds(start, part)
        if m == 1:
            return up_out.at[rows, pl.ds(j * units, units)]
        if start is None:
            return down_out.at[pl.ds(j * units, units), :]
        return down_out.at[pl.ds(j * units + start, part), :]

    pieces = [(0, None)] + [(m, n) for m in (1, 2) for n in (0, 1)]

    def start_of(n, h):
        return None if n is None else (2 * h + n) * part

    def own(m, start):
        ref = (wo, up, down)[m]
        return ref if start is None else ref.at[pl.ds(start, part), :]

    def over_y(at):
        m, n = pieces[at]
        s = start_of(n, half)
        return remote(own(m, s), slot(m, 2 + core, s), w_send, w_recv, (at, 0), across)

    def over_x(at, h):
        m, n = pieces[at]
        held = slot(m, 2 + core, start_of(n, h))
        return remote(held, held, w_send, w_recv, (at, 1), beside)

    def to_near(at, h, sem):
        m, n = pieces[at]
        held = slot(m, 2 + core, start_of(n, h))
        return remote(held, held, w_send, w_recv, (at, sem), near)

    def own_near(m):
        return remote((wo, up, down)[m], slot(m, core), w_send, w_recv, (m, 4), near)

    @pl.when(step == 0)
    def _():
        greet(
            [(lax.rem(me + k, n_dev), t) for k in range(1, n_dev)] + [near, across]
        )
        for at in range(len(pieces)):
            over_y(at).start()
        for move in cot_moves():
            move.start()
        for m in range(3):
            own_near(m).start()
        for move in local_moves():
            move.start()

    attend_pair(n_dev, q_ref, ko_ref, kx_ref, vo_ref, vx_ref, ids_ref, o_ref, lse_ref, me, core)

    def pass_on(at):
        over_y(at).wait_recv()
        to_near(at, half, 2).start()
        if at:
            over_x(at, half).start()

    def pass_side(at):
        over_x(at, half).wait_recv()
        to_near(at, 1 - half, 3).start()

    @pl.when(step == last - 2)
    def _():
        pass_on(0)

    @pl.when(step == last)
    def _():
        n = len(pieces)
        for at in range(1, n):
            pass_on(at)
            if at > 1:
                pass_side(at - 1)
        pass_side(n - 1)
        for move in local_moves():
            move.wait()
        for move in cot_moves():
            move.wait()
        for m in range(3):
            own_near(m).wait()
        for at in range(n):
            over_y(at).wait_send()
            to_near(at, half, 2).wait()
            if at:
                over_x(at, half).wait_send()
                to_near(at, 1 - half, 3).wait()


def attend_pair(n_dev, q_ref, ko_ref, kx_ref, vo_ref, vx_ref, ids_ref, o_ref, lse_ref, me, core):
    span = q_ref.shape[0]
    blocks = span // BLOCK
    lane = lax.broadcasted_iota(jnp.int32, (1, 2 * HD), 1) // HD
    vo_t = vo_ref[...].T
    vx_t = vx_ref[...].T
    outs = []
    for h in range(2):
        qh = (jnp.where(lane == h, q_ref[...], 0.0) * 0.125).astype(jnp.bfloat16)

        def scores(k_ref, far):
            bias = list_bias(ids_ref, h, far, me, core, n_dev, span)
            raw = back_dot(k_ref[...], qh).reshape(blocks, BLOCK, span)
            return (raw + bias[:, None, :]).reshape(span, span)

        so = scores(ko_ref, False)
        sx = scores(kx_ref, True)
        top = jnp.maximum(jnp.max(so, 0, keepdims=True), jnp.max(sx, 0, keepdims=True))
        po = jnp.exp(so - top)
        px = jnp.exp(sx - top)
        total = jnp.sum(po, 0, keepdims=True) + jnp.sum(px, 0, keepdims=True)
        rows = slice(h * HD, (h + 1) * HD)
        acc = plain_dot(vo_t[rows], po.astype(jnp.bfloat16))
        acc = acc + plain_dot(vx_t[rows], px.astype(jnp.bfloat16))
        outs.append(acc / total)
        lse_ref[0, h : h + 1, :] = top + jnp.log(total)
    o_ref[...] = jnp.concatenate(outs, 0).T.astype(jnp.bfloat16)


def attend_gather(q, ko, kx, vo, vx, ids, cot, wo, up, down, n_dev):
    span, width = q.shape
    heads = width // HD
    units = down.shape[0]
    tile = pl.BlockSpec((span, 2 * HD), lambda i: (0, i))
    ids_spec = pl.BlockSpec((2, 3, span), lambda i: (i, 0, 0))
    lse = pl.BlockSpec((1, 2, span), lambda i: (i, 0, 0))
    hbm = pl.BlockSpec(memory_space=pl.ANY)
    dma = pltpu.SemaphoreType.DMA
    low = lambda *shape: jax.ShapeDtypeStruct(shape, jnp.bfloat16)
    return pl.pallas_call(
        partial(attend_gather_kernel, n_dev),
        grid=(heads // 2,),
        in_specs=[tile] * 5 + [ids_spec] + [hbm] * 4,
        out_specs=[tile, lse] + [hbm] * 4,
        out_shape=[
            low(span, width),
            jax.ShapeDtypeStruct((heads // 2, 2, span), jnp.float32),
            low(span, width),
            low(4 * wo.shape[0], width),
            low(width, 4 * units),
            low(4 * units, width),
        ],
        scratch_shapes=[
            dma((n_dev - 1,)),
            dma((n_dev - 1,)),
            dma((5, 5)),
            dma((5, 5)),
            dma((4,)),
        ],
        compiler_params=pltpu.CompilerParams(
            collective_id=1, has_side_effects=True, vmem_limit_bytes=48 * 2**20
        ),
    )(q, ko, kx, vo, vx, ids, cot, wo, up, down)


def attend_back_kernel(
    n_dev, q_ref, ko_ref, kx_ref, vo_ref, vx_ref, ids_ref, lse_ref, o_ref, g_ref,
    dq_ref, dko_ref, dkx_ref, dvo_ref, dvx_ref,
):
    span = q_ref.shape[0]
    blocks = span // BLOCK
    lane = lax.broadcasted_iota(jnp.int32, (1, 2 * HD), 1) // HD
    weighted = (o_ref[...].astype(jnp.float32) * g_ref[...].astype(jnp.float32)).T
    me, _, _, core = place()
    parts = ((ko_ref, vo_ref), (kx_ref, vx_ref))
    k_ts = [k_ref[...].T for k_ref, _ in parts]
    dks = [None, None]
    dvs = [None, None]
    dq_ts = []
    for h in range(2):
        mine = lane == h
        rows = slice(h * HD, (h + 1) * HD)
        qh = (jnp.where(mine, q_ref[...], 0.0) * 0.125).astype(jnp.bfloat16)
        gh = jnp.where(mine, g_ref[...], 0.0).astype(jnp.bfloat16)
        delta = jnp.sum(weighted[rows], 0, keepdims=True)
        lse = lse_ref[0, h : h + 1, :]
        dq_t = None
        for at, (k_ref, v_ref) in enumerate(parts):
            bias = list_bias(ids_ref, h, at == 1, me, core, n_dev, span)
            raw = back_dot(k_ref[...], qh).reshape(blocks, BLOCK, span)
            raw = (raw + bias[:, None, :]).reshape(span, span)
            prob = jnp.exp(raw - lse)
            dprob = back_dot(v_ref[...], gh)
            dscore = (prob * (dprob - delta)).astype(jnp.bfloat16)
            dv = plain_dot(prob.astype(jnp.bfloat16), gh)
            dk = plain_dot(dscore, qh)
            dvs[at] = dv if dvs[at] is None else dvs[at] + dv
            dks[at] = dk if dks[at] is None else dks[at] + dk
            piece = plain_dot(k_ts[at][rows], dscore)
            dq_t = piece if dq_t is None else dq_t + piece
        dq_ts.append(dq_t * 0.125)
    dq_ref[...] = jnp.concatenate(dq_ts, 0).T.astype(dq_ref.dtype)
    for ref, value in ((dko_ref, dks[0]), (dkx_ref, dks[1]), (dvo_ref, dvs[0]), (dvx_ref, dvs[1])):
        ref[...] = value.astype(ref.dtype)


def pair_specs(span):
    tile = pl.BlockSpec((span, 2 * HD), lambda i: (0, i))
    ids = pl.BlockSpec((2, 3, span), lambda i: (i, 0, 0))
    lse = pl.BlockSpec((1, 2, span), lambda i: (i, 0, 0))
    return tile, ids, lse


def attend_back(q, ko, kx, vo, vx, ids, lse_all, o, g, n_dev):
    span, width = q.shape
    heads = width // HD
    tile, ids_spec, lse = pair_specs(span)
    low = jax.ShapeDtypeStruct((span, width), jnp.bfloat16)
    full = jax.ShapeDtypeStruct((span, width), jnp.float32)
    return pl.pallas_call(
        partial(attend_back_kernel, n_dev),
        grid=(heads // 2,),
        in_specs=[tile] * 5 + [ids_spec] + [lse] + [tile] * 2,
        out_specs=[tile] * 5,
        out_shape=[low, full, low, full, low],
        compiler_params=pltpu.CompilerParams(vmem_limit_bytes=48 * 2**20),
        cost_estimate=pl.CostEstimate(
            flops=heads * span * span * 2 * 2 * 5 * HD * 4,
            bytes_accessed=span * width * 30,
            transcendentals=heads * span * span * 2,
        ),
    )(q, ko, kx, vo, vx, ids, lse_all, o, g)


def flip(index, bit):
    value = lax.rem(lax.div(index, bit), 2)
    return index + bit - 2 * bit * value, value


class Reduction:
    def __init__(self, sources, spots, bufs, sems):
        self.sources = sources
        self.me, self.t, self.side, self.core = spots
        self.load, self.b0, self.ys, self.b1, self.acc, self.halves, self.got, self.f = bufs
        self.send, self.recv, self.send0, self.recv0, self.local = sems
        self.near = (self.me, tp_peer(self.side, self.core, 1))
        self.across = (self.me, tp_peer(self.side, self.core, 2))
        self.mates = []
        self.bits = []
        for bit in (1, 2, 4):
            mate, value = flip(self.me, bit)
            self.mates.append((mate, self.t))
            self.bits.append(value)

    def rows(self, depth):
        start, size = 0, self.f.shape[1]
        other = 0
        for level in range(depth):
            size //= 2
            other = start + (1 - self.bits[level]) * size
            start = start + self.bits[level] * size
        return start, other, size

    def parts(self, ch, block):
        at = 0
        for ref in self.sources[ch](block):
            yield ref, pl.ds(at, ref.shape[0])
            at += ref.shape[0]

    def first(self, ch):
        at = [(y, *part) for y in range(2) for part in self.parts(ch, 2 * y + 1 - self.core)]
        return [
            remote(ref, self.b0.at[ch, y, rows, :], self.send0, self.recv0, (ch, n), self.near)
            for n, (y, ref, rows) in enumerate(at)
        ]

    def loads(self, ch):
        at = [(y, *part) for y in range(2) for part in self.parts(ch, 2 * y + self.core)]
        return [
            pltpu.make_async_copy(ref, self.load.at[ch, y, rows, :], self.local.at[ch, n])
            for n, (y, ref, rows) in enumerate(at)
        ]

    def over_y(self, ch):
        return remote(self.ys.at[ch], self.b1.at[ch], self.send, self.recv, (ch, 0), self.across)

    def halving(self, ch, level):
        size = self.rows(level + 1)[2]
        return remote(
            self.halves.at[ch, pl.ds(size, size), :],
            self.got.at[ch, pl.ds(size, size), :],
            self.send, self.recv, (ch, 1 + level), self.mates[level],
        )

    def gather(self, ch, level):
        start, _, size = self.rows(level + 1)
        held = self.f.at[ch, pl.ds(pl.multiple_of(start, 16), size), :]
        return remote(held, held, self.send, self.recv, (ch, 4 + level), self.mates[level])

    def stage(self, ch, s):
        full = jnp.float32
        if s == 0:
            for move in self.first(ch) + self.loads(ch):
                move.start()
        elif s == 1:
            for move in self.loads(ch):
                move.wait()
            for move in self.first(ch):
                move.wait_recv()
            self.ys[ch] = (self.load[ch, 1].astype(full) + self.b0[ch, 1].astype(full)).astype(jnp.bfloat16)
            self.over_y(ch).start()
            self.acc[ch] = self.load[ch, 0].astype(full) + self.b0[ch, 0].astype(full)
        elif s <= 4:
            level = s - 2
            start, _, size = self.rows(level)
            if s == 2:
                self.over_y(ch).wait_recv()
                came = self.b1[ch]
            else:
                self.halving(ch, level - 1).wait_recv()
                came = self.got[ch, pl.ds(size, size), :]
            here = pl.ds(pl.multiple_of(start, 16), size)
            self.acc[ch, here, :] = self.acc[ch, here, :] + came.astype(full)
            _, other, small = self.rows(level + 1)
            there = pl.ds(pl.multiple_of(other, 16), small)
            self.halves[ch, pl.ds(small, small), :] = self.acc[ch, there, :].astype(jnp.bfloat16)
            self.halving(ch, level).start()
        elif s == 5:
            start, _, size = self.rows(3)
            self.halving(ch, 2).wait_recv()
            here = pl.ds(pl.multiple_of(start, 16), size)
            total = self.acc[ch, here, :] + self.got[ch, pl.ds(size, size), :].astype(full)
            self.f[ch, here, :] = total.astype(jnp.bfloat16)
            self.gather(ch, 2).start()
        elif s <= 7:
            self.gather(ch, 8 - s).wait_recv()
            self.gather(ch, 7 - s).start()
        else:
            self.gather(ch, 0).wait_recv()

    def finish(self, ch):
        for move in self.first(ch):
            move.wait_send()
        self.over_y(ch).wait_send()
        for level in range(3):
            self.halving(ch, level).wait_send()
            self.gather(ch, level).wait_send()


class Return:
    def __init__(self, at, n_dev, src, dst, spots, sems):
        self.at, self.n_dev, self.src, self.dst = at, n_dev, src, dst
        self.me, self.t, self.side, self.core = spots
        self.send, self.recv, self.local = sems
        self.near = (self.me, tp_peer(self.side, self.core, 1))
        self.across = (self.me, tp_peer(self.side, self.core, 2))

    def block(self, s, side):
        return self.dst.at[s, side, pl.ds(self.core * BLOCK, BLOCK), :]

    def keep(self):
        return pltpu.make_async_copy(
            self.src.at[pl.ds(0, BLOCK), :], self.block(self.me, self.side), self.local.at[self.at]
        )

    def out(self, k):
        to = lax.rem(self.me - k + self.n_dev, self.n_dev)
        return remote(
            self.src.at[pl.ds(k * BLOCK, BLOCK), :], self.block(self.me, self.side),
            self.send, self.recv, (self.at, k - 1), (to, self.t),
        )

    def pass_on(self, n):
        side = 1 - self.side if n == 2 else self.side
        held = self.dst.at[:, side, pl.ds(self.core * BLOCK, BLOCK), :]
        peer = self.across if n == 0 else self.near
        return remote(held, held, self.send, self.recv, (self.at, self.n_dev - 1 + n), peer)

    def stage(self, s):
        if s == 0:
            self.keep().start()
            for k in range(1, self.n_dev):
                self.out(k).start()
        elif s == 1:
            self.keep().wait()
            for k in range(1, self.n_dev):
                self.out(k).wait_recv()
            self.pass_on(0).start()
            self.pass_on(1).start()
        elif s == 2:
            self.pass_on(0).wait_recv()
            self.pass_on(2).start()
        else:
            for k in range(1, self.n_dev):
                self.out(k).wait_send()
            self.pass_on(0).wait_send()
            self.pass_on(1).wait()
            self.pass_on(2).wait()


class SmallSum:
    def __init__(self, src, out, came, spots, sems):
        self.src, self.out, self.came = src, out, came
        me, t, side, core = spots
        self.send, self.recv = sems
        self.peers = [(me, tp_peer(side, core, 1)), (me, tp_peer(side, core, 2))]
        self.peers += [(flip(me, bit)[0], t) for bit in (1, 2, 4)]

    def move(self, n):
        held = self.out.at[n]
        return remote(held, self.came.at[n], self.send, self.recv, n, self.peers[n])

    def stage(self, n):
        if n == 0:
            self.out[0] = self.src[...]
        else:
            self.move(n - 1).wait_recv()
            self.out[n] = self.out[n - 1] + self.came[n - 1]
        if n < len(self.peers):
            self.move(n).start()

    def finish(self):
        for n in range(len(self.peers)):
            self.move(n).wait_send()


def all_peers(n_dev, me, t, side, core):
    return [(lax.rem(me + k, n_dev), t) for k in range(1, n_dev)] + [
        (me, tp_peer(side, core, bits)) for bits in (1, 2)
    ]


def blocks_of(ref, height, start, size):
    return lambda block: [ref.at[pl.ds(block * height + start, size), :]]


def columns_of(ref, wide, start, size):
    return lambda block: [ref.at[pl.ds(start, size), pl.ds(block * wide, wide)]]


def pair_of(one, two, height):
    return lambda block: [
        one.at[pl.ds(block * height, height), :], two.at[pl.ds(block * height, height), :]
    ]


def leave_kernel(
    n_dev, gd, gu, go, gq, gk, gv, low, ig, small,
    f, out, iout, total,
    load, b0, ys, b1, acc, halves, got, came,
    send, recv, send0, recv0, local, r_send, r_recv, r_local, s_send, s_recv,
):
    spots = place()
    units, hidden = gd.shape[0] // 4, go.shape[0] // 4
    rows = f.shape[1]
    sources = [blocks_of(gd, units, i * rows, rows) for i in range(units // rows)]
    sources += [columns_of(gu, units, i * rows, rows) for i in range(gu.shape[0] // rows)]
    sources += [pair_of(go, gq, hidden), pair_of(gk, gv, hidden)]
    red = Reduction(
        sources, spots, (load, b0, ys, b1, acc, halves, got, f), (send, recv, send0, recv0, local)
    )
    backs = [
        Return(n, n_dev, src, dst, spots, (r_send, r_recv, r_local))
        for n, (src, dst) in enumerate(((low, out), (ig, iout)))
    ]
    tiny = SmallSum(small, total, came, spots, (s_send, s_recv))
    greet(all_peers(n_dev, *spots))
    count = len(sources)
    for ch in range(count):
        red.stage(ch, 0)
    tiny.stage(0)
    for back in backs:
        back.stage(0)
    for ch in range(count):
        red.stage(ch, 1)
    for tick in range(count + 6):
        for ch in range(count):
            if 2 <= tick - ch + 2 <= 8:
                red.stage(ch, tick - ch + 2)
        if tick < 5:
            tiny.stage(tick + 1)
        if 2 <= tick < 5:
            for back in backs:
                back.stage(tick - 1)
    for ch in range(count):
        red.finish(ch)
    tiny.finish()


def leave(gd, gu, go, gq, gk, gv, low, ig, small, n_dev):
    width = low.shape[1]
    rows = 2 * (go.shape[0] // 4)
    count = (gd.shape[0] // 4 + gu.shape[0]) // rows + 2
    vmem = pl.BlockSpec(memory_space=pltpu.VMEM)
    hbm = pl.BlockSpec(memory_space=pl.ANY)
    dma = pltpu.SemaphoreType.DMA
    landed = jax.ShapeDtypeStruct((n_dev, 2, 2 * BLOCK, width), jnp.bfloat16)
    low_buf = lambda *shape: pltpu.VMEM(shape + (width,), jnp.bfloat16)
    return pl.pallas_call(
        partial(leave_kernel, n_dev),
        in_specs=[hbm] * 8 + [vmem],
        out_specs=[vmem, hbm, hbm, vmem],
        out_shape=[
            jax.ShapeDtypeStruct((count, rows, width), jnp.bfloat16),
            landed,
            landed,
            jax.ShapeDtypeStruct((6,) + small.shape, jnp.float32),
        ],
        scratch_shapes=[
            low_buf(count, 2, rows),
            low_buf(count, 2, rows),
            low_buf(count, rows),
            low_buf(count, rows),
            pltpu.VMEM((count, rows, width), jnp.float32),
            low_buf(count, rows),
            low_buf(count, rows),
            pltpu.VMEM((5,) + small.shape, jnp.float32),
            dma((count, 7)),
            dma((count, 7)),
            dma((count, 4)),
            dma((count, 4)),
            dma((count, 4)),
            dma((2, n_dev + 2)),
            dma((2, n_dev + 2)),
            dma((2,)),
            dma((5,)),
            dma((5,)),
        ],
        compiler_params=pltpu.CompilerParams(
            collective_id=2, has_side_effects=True, vmem_limit_bytes=58 * 2**20
        ),
    )(gd, gu, go, gq, gk, gv, low, ig, small)


def swap(piece, bits):
    size = lax.axis_size("tp")
    return lax.ppermute(piece, "tp", [(i, i ^ bits) for i in range(size)])


def norm_parts(resid):
    centre = resid - jnp.mean(resid, -1, keepdims=True)
    inverse = lax.rsqrt(jnp.mean(centre * centre, -1, keepdims=True) + norm_eps)
    return centre * inverse, inverse


def norm_back(grad, unit, inverse, gain):
    scaled = grad * gain
    pull = scaled - jnp.mean(scaled, -1, keepdims=True)
    pull = pull - unit * jnp.mean(scaled * unit, -1, keepdims=True)
    return pull * inverse, jnp.sum(grad * unit, 0), jnp.sum(grad, 0)


def whole_sequences(
    tokens,
    rand_blocks,
    query_weight,
    query_bias,
    key_weight,
    value_weight,
    value_bias,
    output_weight,
    output_bias,
    attn_gain,
    attn_shift,
    up_weight,
    up_bias,
    down_weight,
    down_bias,
    ffn_gain,
    ffn_shift,
    cotangent,
):
    seqs, rows, width = tokens.shape
    n_dev = lax.axis_size("seq")
    me = lax.axis_index("seq")
    t = lax.axis_index("tp")
    side, core = t // 2, t % 2
    n_blocks = rows // BLOCK * n_dev
    hidden = query_weight.shape[1]
    units = up_weight.shape[1]
    span = n_dev * BLOCK

    gap = jnp.zeros((256 - hidden,), jnp.float32)
    pack = jnp.concatenate([query_bias, gap, value_bias, gap, up_bias])[None]
    x, q, k_own, v_own, k_far, v_far, wt, packs, ids = enter(
        tokens, rand_blocks, query_weight, key_weight, value_weight, pack, n_dev
    )
    wq, wk, wv = (wt[m].reshape(4 * hidden, width) for m in range(3))
    u_bias = packs[:, 0, 512:].reshape(4 * units)
    attn_low, lse, cot, wo, w_up, w_down = attend_gather(
        q, k_own, k_far, v_own, v_far, ids, cotangent, output_weight, up_weight, down_weight, n_dev
    )
    branch = plain_dot(attn_low, wo) + output_bias
    unit_one, inverse_one = norm_parts(x.astype(jnp.float32) + branch)
    normed = unit_one * attn_gain + attn_shift
    normed_low = normed.astype(jnp.bfloat16)
    pre_act = plain_dot(normed_low, w_up) + u_bias
    cdf = 0.5 * (1.0 + lax.erf(pre_act * HALF_ROOT))
    act_low = (pre_act * cdf).astype(jnp.bfloat16)
    slope = (cdf + pre_act * (PDF_SCALE * jnp.exp(-0.5 * pre_act * pre_act))).astype(jnp.bfloat16)
    ffn = plain_dot(act_low, w_down) + down_bias
    unit_two, inverse_two = norm_parts(normed + ffn)
    out_low = (unit_two * ffn_gain + ffn_shift).astype(jnp.bfloat16)

    g_resid2, grad_ffngain, grad_ffnshift = norm_back(
        cot.astype(jnp.float32), unit_two, inverse_two, ffn_gain
    )
    g_ffn = g_resid2.astype(jnp.bfloat16)
    grad_downbias = jnp.sum(g_ffn.astype(jnp.float32), 0)
    grad_down = rows_dot(act_low, g_ffn).astype(jnp.bfloat16)
    g_pre = (back_dot(g_ffn, w_down) * slope.astype(jnp.float32)).astype(jnp.bfloat16)
    grad_upbias = jnp.sum(g_pre.astype(jnp.float32), 0)
    grad_up = rows_dot(normed_low, g_pre).astype(jnp.bfloat16)
    g_normed = g_resid2 + back_dot(g_pre, w_up)
    g_resid, grad_attngain, grad_attnshift = norm_back(g_normed, unit_one, inverse_one, attn_gain)
    g_branch = g_resid.astype(jnp.bfloat16)
    grad_obias = jnp.sum(g_branch.astype(jnp.float32), 0)
    grad_o = rows_dot(attn_low, g_branch).astype(jnp.bfloat16)
    g_attn = back_dot(g_branch, wo).astype(jnp.bfloat16)

    dq, dk_own, dk_far, dv_own, dv_far = attend_back(
        q, k_own, k_far, v_own, v_far, ids, lse, attn_low, g_attn, n_dev
    )
    dk = (dk_own + swap(dk_far, 1).astype(jnp.float32)).astype(jnp.bfloat16)
    dv = (dv_own + swap(dv_far, 1).astype(jnp.float32)).astype(jnp.bfloat16)
    grad_qbias = jnp.sum(dq.astype(jnp.float32), 0)
    grad_vbias = jnp.sum(dv.astype(jnp.float32), 0)
    grad_q = rows_dot(dq, x).astype(jnp.bfloat16)
    grad_k = rows_dot(dk, x).astype(jnp.bfloat16)
    grad_v = rows_dot(dv, x).astype(jnp.bfloat16)
    input_grad = g_resid + plain_dot(dq, wq) + plain_dot(dk, wk) + plain_dot(dv, wv)
    def absolute(vector):
        parts = vector.reshape(4, -1)
        return jnp.take(parts, jnp.arange(4) ^ (2 * side), 0).reshape(-1)

    small = jnp.concatenate(
        [
            absolute(grad_qbias),
            absolute(grad_vbias),
            absolute(grad_upbias),
            grad_obias,
            grad_attngain,
            grad_attnshift,
            grad_downbias,
            grad_ffngain,
            grad_ffnshift,
        ]
    )
    sums, layer_output, input_out, small_total = leave(
        grad_down, grad_up, grad_o, grad_q, grad_k, grad_v, out_low,
        input_grad.astype(jnp.bfloat16), small.reshape(-1, 128), n_dev,
    )
    small_total = small_total[5].reshape(-1)

    def share(start, size):
        whole = small_total[start : start + 4 * size].reshape(4, size)
        return lax.dynamic_index_in_dim(whole, t, 0, False)

    tail = 8 * hidden + 4 * units
    rep = [small_total[tail + i * width : tail + (i + 1) * width] for i in range(6)]

    sums = sums.astype(jnp.float32)
    half = units // sums.shape[1]
    g_down = sums[:half].reshape(units, width)
    g_up = sums[half : half + width // sums.shape[1]].reshape(width, units)
    g_o, g_q = sums[-2, :hidden], sums[-2, hidden:]
    g_k, g_v = sums[-1, :hidden], sums[-1, hidden:]
    return (
        layer_output.reshape(seqs, rows, width),
        input_out.astype(jnp.float32).reshape(seqs, rows, width),
        g_q.T,
        share(0, hidden),
        g_k.T,
        g_v.T,
        share(4 * hidden, hidden),
        g_o,
        rep[0],
        rep[1],
        rep[2],
        g_up,
        share(8 * hidden, units),
        g_down,
        rep[3],
        rep[4],
        rep[5],
    )


def per_device(tokens, *rest):
    seqs, rows, _ = tokens.shape
    n_dev = lax.axis_size("seq")
    if lax.axis_size("tp") == 4 and n_dev == 8 and seqs == 2 * n_dev and rows == 2 * BLOCK:
        return whole_sequences(tokens, *rest)
    return split_sequences(tokens, *rest)


def solution(mesh):
    placed = (
        P(None, "seq", None),
        P(None, None, "tp", None),
        P(None, "tp"),
        P("tp"),
        P(None, "tp"),
        P(None, "tp"),
        P("tp"),
        P("tp", None),
        P(),
        P(),
        P(),
        P(None, "tp"),
        P("tp"),
        P("tp", None),
        P(),
        P(),
        P(),
        P(None, "seq", None),
    )
    return jax.shard_map(
        per_device,
        mesh=mesh,
        in_specs=placed,
        out_specs=(
            P(None, "seq", None),
            P(None, "seq", None),
            P(None, "tp"),
            P("tp"),
            P(None, "tp"),
            P(None, "tp"),
            P("tp"),
            P("tp", None),
            P(),
            P(),
            P(),
            P(None, "tp"),
            P("tp"),
            P("tp", None),
            P(),
            P(),
            P(),
        ),
        check_vma=False,
    )
```

```python
from functools import partial

import jax
import jax.numpy as jnp
from jax import lax
from jax.sharding import PartitionSpec as P
from jax.experimental import pallas as pl
from jax.experimental.pallas import tpu as pltpu

HD = 64
BLOCK = 64


norm_eps = 1e-06
masked_score = -1e30
highest_precision = lax.Precision.HIGHEST


def with_halo(shard, sides, width):
    for axis, dim in sides:
        size, length = (lax.axis_size(axis), shard.shape[dim])
        up = [(i, (i + 1) % size) for i in range(size - 1)]
        down = [(j, i) for i, j in up]
        last = lax.slice_in_dim(shard, length - width, length, axis=dim)
        first = lax.slice_in_dim(shard, 0, width, axis=dim)
        before = lax.ppermute(last, axis, up)
        after = lax.ppermute(first, axis, down)
        shard = jnp.concatenate([before, shard, after], axis=dim)
    return shard


def joined(shard, axis, combine):
    everything = jax.tree.map(lambda part: lax.all_gather(part, axis), shard)
    first = jax.tree.map(lambda part: part[0], everything)

    def hop(k, so_far):
        return combine(so_far, jax.tree.map(lambda part: part[k], everything))

    return lax.fori_loop(1, lax.axis_size(axis), hop, first)


def layer_norm(resid, gain, shift):
    centre = resid - jnp.mean(resid, -1, keepdims=True)
    spread = jnp.mean(centre * centre, -1, keepdims=True)
    return centre * lax.rsqrt(spread + norm_eps) * gain + shift


def gelu_exact(values):
    return jax.nn.gelu(values, approximate=False)


def plain_dot(left, right):
    return jnp.dot(left, right, preferred_element_type=jnp.float32)


def rows_dot(left, right):
    return lax.dot_general(
        left, right, (((0,), (0,)), ((), ())), preferred_element_type=jnp.float32
    )


def back_dot(left, right):
    return lax.dot_general(
        left, right, (((1,), (1,)), ((), ())), preferred_element_type=jnp.float32
    )


def softmax_row_probs(scores):
    top_score = jnp.max(scores, -1, keepdims=True)
    expo = jnp.exp(scores - top_score)
    return expo / jnp.sum(expo, -1, keepdims=True)


def head_sum_fwd(pieces):
    return lax.psum(pieces, "tp")


def head_sum_back(pieces):
    return lax.psum(pieces, "tp")


def merge_rows(first, second):
    top_score = jnp.maximum(first[0], second[0])
    scale_one = jnp.exp(first[0] - top_score)
    scale_two = jnp.exp(second[0] - top_score)
    return (
        top_score,
        first[1] * scale_one + second[1] * scale_two,
        first[2] * scale_one[..., None] + second[2] * scale_two[..., None],
    )


def tile_plan(rand_blocks, my_index, n_dev, per_dev, seqs, heads):
    count = seqs * per_dev * heads * 3
    capacity = max(2, 2 * count // n_dev)
    requests = (
        rand_blocks.reshape(seqs, n_dev, per_dev, heads, 3)
        .transpose(1, 0, 2, 3, 4)
        .reshape(n_dev, count)
    )
    is_mine = requests // per_dev == my_index
    ranking = jnp.cumsum(is_mine.astype(jnp.int32), 1) - 1
    slot_ids = jnp.arange(capacity, dtype=jnp.int32)
    select = is_mine[:, None, :] & (ranking[:, None, :] == slot_ids[None, :, None])
    filled = jnp.any(select, 2)
    position = jnp.arange(count, dtype=jnp.int32)
    seq_of = position // (per_dev * heads * 3)
    head_of = position // 3 % heads
    tile_of = (seq_of[None, :] * per_dev + requests % per_dev) * heads + head_of[None, :]
    send_index = jnp.sum(jnp.where(select, tile_of[:, None, :], 0), 2)
    own_requests = lax.dynamic_slice_in_dim(rand_blocks, my_index * per_dev, per_dev, 1).reshape(
        count
    )
    own_owner = own_requests // per_dev
    onehot = (own_owner[:, None] == jnp.arange(n_dev, dtype=jnp.int32)[None, :]).astype(jnp.int32)
    own_rank = jnp.sum((jnp.cumsum(onehot, 0) - 1) * onehot, 1)
    recv_index = own_owner * capacity + own_rank
    return (capacity, send_index, filled, recv_index)


def pick_tiles(incoming, recv_index, seqs, per_dev, heads, block, hsize):
    stacked = incoming.reshape(-1, block, 2 * hsize)
    return jnp.take(stacked, recv_index, 0).reshape(seqs, per_dev, heads, 3, block, 2 * hsize)


def assemble(end_part, window_part, tile_part, seqs, per_dev, heads, block, hsize):
    ends_wide = jnp.broadcast_to(end_part[:, None], (seqs, per_dev, heads, 2 * block, hsize))
    return jnp.concatenate(
        [ends_wide, window_part, tile_part.reshape(seqs, per_dev, heads, 3 * block, hsize)], 3
    )


def split_sequences(
    tokens,
    rand_blocks,
    query_weight,
    query_bias,
    key_weight,
    value_weight,
    value_bias,
    output_weight,
    output_bias,
    attn_gain,
    attn_shift,
    up_weight,
    up_bias,
    down_weight,
    down_bias,
    ffn_gain,
    ffn_shift,
    cotangent,
):
    seqs, rows, width = tokens.shape
    block = BLOCK
    hsize = HD
    per_dev = rows // block
    n_dev = lax.axis_size("seq")
    my_index = lax.axis_index("seq")
    n_blocks = per_dev * n_dev
    heads = query_weight.shape[1] // hsize
    hidden = heads * hsize
    n_tok = seqs * rows
    is_first = my_index == 0
    is_last = my_index == n_dev - 1
    flat = tokens.reshape(n_tok, width)
    query_low = (plain_dot(flat, query_weight) + query_bias).astype(jnp.bfloat16)
    key_low = plain_dot(flat, key_weight).astype(jnp.bfloat16)
    value_low = (plain_dot(flat, value_weight) + value_bias).astype(jnp.bfloat16)
    keyval = jnp.concatenate([key_low, value_low], 1).reshape(seqs, rows, 2 * hidden)
    extended = with_halo(keyval, (("seq", 1),), block)
    windows = jnp.stack(
        [extended[:, offset * block : (offset + 3) * block] for offset in range(per_dev)], 1
    )
    windows = windows.reshape(seqs, per_dev, 3 * block, 2, heads, hsize)
    win_key = windows[:, :, :, 0].transpose(0, 1, 3, 2, 4)
    win_value = windows[:, :, :, 1].transpose(0, 1, 3, 2, 4)
    triple = jnp.concatenate([query_low.reshape(seqs, rows, hidden), keyval], 2).astype(jnp.float32)
    own_ends = jnp.stack(
        [
            jnp.where(is_first, triple[:, :block], 0.0),
            jnp.where(is_last, triple[:, rows - block :], 0.0),
        ],
        1,
    )
    ends = lax.psum(own_ends.astype(jnp.bfloat16), "seq").reshape(seqs, 2, block, 3, heads, hsize)
    end_query = ends[:, :, :, 0].transpose(0, 3, 1, 2, 4).reshape(seqs, heads, 2 * block, hsize)
    end_key = ends[:, :, :, 1].transpose(0, 3, 1, 2, 4).reshape(seqs, heads, 2 * block, hsize)
    end_value = ends[:, :, :, 2].transpose(0, 3, 1, 2, 4).reshape(seqs, heads, 2 * block, hsize)
    capacity, send_index, filled, recv_index = tile_plan(
        rand_blocks, my_index, n_dev, per_dev, seqs, heads
    )
    table = (
        keyval.reshape(seqs, per_dev, block, 2, heads, hsize)
        .transpose(0, 1, 4, 2, 3, 5)
        .reshape(seqs * per_dev * heads, block, 2 * hsize)
    )
    outgoing = jnp.take(table, send_index.reshape(-1), 0).reshape(n_dev, capacity, block, 2 * hsize)
    outgoing = jnp.where(filled[:, :, None, None], outgoing, jnp.zeros((), jnp.bfloat16))
    incoming = lax.all_to_all(outgoing, "seq", split_axis=0, concat_axis=0, tiled=True)
    tiles = pick_tiles(incoming, recv_index, seqs, per_dev, heads, block, hsize)
    q_blocks = query_low.reshape(seqs, per_dev, block, heads, hsize).transpose(0, 1, 3, 2, 4)
    keys_all = assemble(end_key, win_key, tiles[..., :hsize], seqs, per_dev, heads, block, hsize)
    values_all = assemble(
        end_value, win_value, tiles[..., hsize:], seqs, per_dev, heads, block, hsize
    )
    block_ids = my_index * per_dev + jnp.arange(per_dev, dtype=jnp.int32)
    slot_ids = jnp.arange(8 * block, dtype=jnp.int32) // block
    dropped = (slot_ids == 2)[None, :] & (block_ids == 1)[:, None] | (slot_ids == 4)[None, :] & (
        block_ids == n_blocks - 2
    )[:, None]
    unscaled_scores = (
        jnp.einsum("sbhqd,sbhkd->sbhqk", q_blocks, keys_all, preferred_element_type=jnp.float32)
        * 0.125
    )
    unscaled_scores = jnp.where(dropped[None, :, None, None, :], masked_score, unscaled_scores)
    weights = softmax_row_probs(unscaled_scores)
    sparse_attention = jnp.einsum(
        "sbhqk,sbhkd->sbhqd",
        weights,
        values_all.astype(jnp.float32),
        precision=highest_precision,
        preferred_element_type=jnp.float32,
    )
    key_local = key_low.reshape(seqs, rows, heads, hsize).transpose(0, 2, 1, 3)
    value_local = value_low.reshape(seqs, rows, heads, hsize).transpose(0, 2, 1, 3)
    end_raw = (
        jnp.einsum("shqd,shkd->shqk", end_query, key_local, preferred_element_type=jnp.float32)
        * 0.125
    )
    end_top = jnp.max(end_raw, -1)
    end_expo = jnp.exp(end_raw - end_top[..., None])
    end_total = jnp.sum(end_expo, -1)
    end_acc = jnp.einsum(
        "shqk,shkd->shqd",
        end_expo,
        value_local.astype(jnp.float32),
        precision=highest_precision,
        preferred_element_type=jnp.float32,
    )
    merged_top, merged_total, merged_acc = joined((end_top, end_total, end_acc), "seq", merge_rows)
    end_out = merged_acc / merged_total[..., None]
    end_lse = merged_top + jnp.log(merged_total)
    end_split = end_out.reshape(seqs, heads, 2, block, hsize)
    first_rows = block_ids == 0
    last_rows = block_ids == n_blocks - 1
    attn = jnp.where(
        first_rows[None, :, None, None, None], end_split[:, None, :, 0], sparse_attention
    )
    attn = jnp.where(last_rows[None, :, None, None, None], end_split[:, None, :, 1], attn)
    attn_low = attn.transpose(0, 1, 3, 2, 4).reshape(n_tok, hidden).astype(jnp.bfloat16)
    branch = head_sum_fwd(plain_dot(attn_low, output_weight)) + output_bias
    resid = flat.astype(jnp.float32) + branch
    normed = layer_norm(resid, attn_gain, attn_shift)
    normed_low = normed.astype(jnp.bfloat16)
    pre_act = plain_dot(normed_low, up_weight) + up_bias
    act_low = gelu_exact(pre_act).astype(jnp.bfloat16)
    ffn = head_sum_fwd(plain_dot(act_low, down_weight)) + down_bias
    resid_two = normed + ffn
    layer_output = (
        layer_norm(resid_two, ffn_gain, ffn_shift).astype(jnp.bfloat16).reshape(seqs, rows, width)
    )
    cot_flat = cotangent.reshape(n_tok, width).astype(jnp.float32)
    norm_two, pull_two = jax.vjp(layer_norm, resid_two, ffn_gain, ffn_shift)
    grad_resid2, grad_ffngain, grad_ffnshift = pull_two(cot_flat)
    grad_ffn = grad_resid2.astype(jnp.bfloat16)
    grad_downbias = jnp.sum(grad_ffn.astype(jnp.float32), 0)
    grad_downweight = rows_dot(act_low, grad_ffn)
    grad_act = back_dot(grad_ffn, down_weight)
    gelu_out, pull_gelu = jax.vjp(gelu_exact, pre_act)
    grad_pre = pull_gelu(grad_act)[0].astype(jnp.bfloat16)
    grad_upbias = jnp.sum(grad_pre.astype(jnp.float32), 0)
    grad_upweight = rows_dot(normed_low, grad_pre)
    grad_normed = grad_resid2 + head_sum_back(back_dot(grad_pre, up_weight))
    norm_one, pull_one = jax.vjp(layer_norm, resid, attn_gain, attn_shift)
    grad_resid, grad_attngain, grad_attnshift = pull_one(grad_normed)
    grad_branch = grad_resid.astype(jnp.bfloat16)
    grad_obias = jnp.sum(grad_branch.astype(jnp.float32), 0)
    grad_oweight = rows_dot(attn_low, grad_branch)
    grad_attn = back_dot(grad_branch, output_weight).astype(jnp.bfloat16)
    grad_heads = grad_attn.reshape(seqs, per_dev, block, heads, hsize).transpose(0, 1, 3, 2, 4)
    global_mask = (first_rows | last_rows)[None, :, None, None, None]
    grad_sparse = jnp.where(global_mask, jnp.zeros((), jnp.bfloat16), grad_heads)
    own_dout = jnp.stack(
        [
            jnp.where(is_first, grad_heads[:, 0].astype(jnp.float32), 0.0),
            jnp.where(is_last, grad_heads[:, per_dev - 1].astype(jnp.float32), 0.0),
        ],
        2,
    ).reshape(seqs, heads, 2 * block, hsize)
    own_delta = jnp.sum(own_dout * end_out, -1)
    end_dout, end_delta = lax.psum((own_dout, own_delta), "seq")
    end_dlow = end_dout.astype(jnp.bfloat16)
    end_prob = jnp.exp(end_raw - end_lse[..., None])
    end_dprob = jnp.einsum(
        "shqd,shkd->shqk", end_dlow, value_local, preferred_element_type=jnp.float32
    )
    end_dscore = (end_prob * (end_dprob - end_delta[..., None]) * 0.125).astype(jnp.bfloat16)
    end_dquery_part = jnp.einsum(
        "shqk,shkd->shqd", end_dscore, key_local, preferred_element_type=jnp.float32
    )
    local_dkey = jnp.einsum(
        "shqk,shqd->shkd", end_dscore, end_query, preferred_element_type=jnp.float32
    )
    local_dvalue = jnp.einsum(
        "shqk,shqd->shkd",
        end_prob,
        end_dout,
        precision=highest_precision,
        preferred_element_type=jnp.float32,
    )
    again = lax.all_to_all(outgoing, "seq", split_axis=0, concat_axis=0, tiled=True)
    back_tiles = pick_tiles(again, recv_index, seqs, per_dev, heads, block, hsize)
    keys_back = assemble(
        end_key, win_key, back_tiles[..., :hsize], seqs, per_dev, heads, block, hsize
    )
    values_back = assemble(
        end_value, win_value, back_tiles[..., hsize:], seqs, per_dev, heads, block, hsize
    )
    grad_prob = jnp.einsum(
        "sbhqd,sbhkd->sbhqk", grad_sparse, values_back, preferred_element_type=jnp.float32
    )
    row_delta = jnp.sum(weights * grad_prob, -1, keepdims=True)
    grad_score = (weights * (grad_prob - row_delta) * 0.125).astype(jnp.bfloat16)
    grad_qblocks = jnp.einsum(
        "sbhqk,sbhkd->sbhqd", grad_score, keys_back, preferred_element_type=jnp.float32
    )
    grad_keysall = jnp.einsum(
        "sbhqk,sbhqd->sbhkd", grad_score, q_blocks, preferred_element_type=jnp.float32
    )
    grad_valsall = jnp.einsum(
        "sbhqk,sbhqd->sbhkd",
        weights,
        grad_sparse.astype(jnp.float32),
        precision=highest_precision,
        preferred_element_type=jnp.float32,
    )
    end_dkey = jnp.sum(grad_keysall[:, :, :, : 2 * block], 1)
    end_dvalue = jnp.sum(grad_valsall[:, :, :, : 2 * block], 1)
    win_grad = jnp.stack(
        [
            grad_keysall[:, :, :, 2 * block : 5 * block].transpose(0, 1, 3, 2, 4),
            grad_valsall[:, :, :, 2 * block : 5 * block].transpose(0, 1, 3, 2, 4),
        ],
        3,
    ).reshape(seqs, per_dev, 3 * block, 2 * hidden)
    rand_grad = (
        jnp.concatenate(
            [
                grad_keysall[:, :, :, 5 * block :].reshape(seqs, per_dev, heads, 3, block, hsize),
                grad_valsall[:, :, :, 5 * block :].reshape(seqs, per_dev, heads, 3, block, hsize),
            ],
            5,
        )
        .reshape(-1, block, 2 * hsize)
        .astype(jnp.bfloat16)
    )
    ext_grad = jnp.zeros((seqs, rows + 2 * block, 2 * hidden), jnp.float32)
    for offset in range(per_dev):
        ext_grad = ext_grad.at[:, offset * block : (offset + 3) * block].add(win_grad[:, offset])
    rims = jnp.concatenate([ext_grad[:, :block], ext_grad[:, rows + block :]], 1)
    returned_rims = with_halo(rims.astype(jnp.bfloat16), (("seq", 1),), block).astype(rims.dtype)
    middle_zero = jnp.zeros((seqs, rows - 2 * block, 2 * hidden), jnp.float32)
    kv_grad = ext_grad[:, block : rows + block] + jnp.concatenate(
        [returned_rims[:, :block], middle_zero, returned_rims[:, 3 * block :]], 1
    )
    sent_back = (
        jnp.zeros((n_dev * capacity, block, 2 * hsize), jnp.bfloat16)
        .at[recv_index]
        .set(rand_grad)
        .reshape(n_dev, capacity, block, 2 * hsize)
    )
    arrived = lax.all_to_all(sent_back, "seq", split_axis=0, concat_axis=0, tiled=True)
    arrived = jnp.where(filled[:, :, None, None], arrived.astype(jnp.float32), 0.0)
    table_grad = (
        jnp.zeros((seqs * per_dev * heads, block, 2 * hsize), jnp.float32)
        .at[send_index.reshape(-1)]
        .add(arrived.reshape(-1, block, 2 * hsize))
    )
    kv_grad = kv_grad + table_grad.reshape(seqs, per_dev, heads, block, 2, hsize).transpose(
        0, 1, 3, 4, 2, 5
    ).reshape(seqs, rows, 2 * hidden)
    kv_grad = kv_grad + jnp.stack(
        [local_dkey.transpose(0, 2, 1, 3), local_dvalue.transpose(0, 2, 1, 3)], 2
    ).reshape(seqs, rows, 2 * hidden)
    end_dquery, end_dkey_all, end_dvalue_all = (
        lax.psum(end_dquery_part.astype(jnp.bfloat16), "seq").astype(jnp.float32),
        lax.psum(end_dkey.astype(jnp.bfloat16), "seq").astype(jnp.float32),
        lax.psum(end_dvalue.astype(jnp.bfloat16), "seq").astype(jnp.float32),
    )
    end_kv = jnp.stack(
        [end_dkey_all.transpose(0, 2, 1, 3), end_dvalue_all.transpose(0, 2, 1, 3)], 2
    ).reshape(seqs, 2 * block, 2 * hidden)
    kv_grad = kv_grad + jnp.concatenate(
        [
            jnp.where(is_first, end_kv[:, :block], 0.0),
            middle_zero,
            jnp.where(is_last, end_kv[:, block:], 0.0),
        ],
        1,
    )
    end_q = end_dquery.transpose(0, 2, 1, 3).reshape(seqs, 2 * block, hidden)
    query_zero = jnp.zeros((seqs, rows - 2 * block, hidden), jnp.float32)
    grad_query = grad_qblocks.transpose(0, 1, 3, 2, 4).reshape(seqs, rows, hidden)
    grad_query = grad_query + jnp.concatenate(
        [
            jnp.where(is_first, end_q[:, :block], 0.0),
            query_zero,
            jnp.where(is_last, end_q[:, block:], 0.0),
        ],
        1,
    )
    query_glow = grad_query.reshape(n_tok, hidden).astype(jnp.bfloat16)
    kv_glow = kv_grad.reshape(n_tok, 2 * hidden).astype(jnp.bfloat16)
    key_glow = kv_glow[:, :hidden]
    value_glow = kv_glow[:, hidden:]
    grad_qbias = jnp.sum(query_glow.astype(jnp.float32), 0)
    grad_vbias = jnp.sum(value_glow.astype(jnp.float32), 0)
    grad_qweight = rows_dot(flat, query_glow)
    grad_kweight = rows_dot(flat, key_glow)
    grad_vweight = rows_dot(flat, value_glow)
    into_tokens = (
        back_dot(query_glow, query_weight)
        + back_dot(key_glow, key_weight)
        + back_dot(value_glow, value_weight)
    )
    input_grad = (grad_resid + head_sum_back(into_tokens)).reshape(seqs, rows, width)
    totals = lax.psum(
        (
            grad_qweight,
            grad_qbias,
            grad_kweight,
            grad_vweight,
            grad_vbias,
            grad_oweight,
            grad_obias,
            grad_attngain,
            grad_attnshift,
            grad_upweight,
            grad_upbias,
            grad_downweight,
            grad_downbias,
            grad_ffngain,
            grad_ffnshift,
        ),
        "seq",
    )
    return (
        layer_output,
        input_grad,
        totals[0],
        totals[1],
        totals[2],
        totals[3],
        totals[4],
        totals[5],
        totals[6],
        totals[7],
        totals[8],
        totals[9],
        totals[10],
        totals[11],
        totals[12],
        totals[13],
        totals[14],
    )


HALF_ROOT = 0.7071067811865476
PDF_SCALE = 0.3989422804014327


MESH = pl.DeviceIdType.MESH


def place():
    me, t = lax.axis_index("seq"), lax.axis_index("tp")
    side, core = lax.div(t, 2), lax.rem(t, 2)
    return me, t, side, core


def tp_peer(side, core, bits):
    there = 1 - side if bits & 2 else side
    return there * 2 + (1 - core if bits & 1 else core)


def greet(peers):
    barrier = pltpu.get_barrier_semaphore()
    for peer in peers:
        pl.semaphore_signal(barrier, inc=1, device_id=peer, device_id_type=MESH)
    pl.semaphore_wait(barrier, len(peers))


def remote(src, dst, sends, recvs, at, peer):
    return pltpu.make_async_remote_copy(
        src_ref=src,
        dst_ref=dst,
        send_sem=sends.at[at],
        recv_sem=recvs.at[at],
        device_id=peer,
        device_id_type=MESH,
    )


class Piece:
    def __init__(self, at, bit, own, held, spots, sems):
        me, t, side, core = spots
        self.at, self.own, self.far = at, own, partial(held, 2 + core)
        mate, self.half = flip(me, bit)
        self.mate = (mate, t)
        self.near, self.across = (me, tp_peer(side, core, 1)), (me, tp_peer(side, core, 2))
        self.sems = sems

    def move(self, n):
        h = 1 - self.half if n == 3 else self.half
        src = self.own(h) if n == 0 else self.far(h)
        peer = (self.across, self.mate, self.near, self.near)[n]
        return remote(src, self.far(h), *self.sems, (self.at, n), peer)

    def start(self):
        self.move(0).start()

    def pass_on(self):
        self.move(0).wait_recv()
        self.move(1).start()
        self.move(2).start()

    def pass_side(self):
        self.move(1).wait_recv()
        self.move(3).start()

    def arrive(self):
        self.move(2).wait_recv()
        self.move(3).wait_recv()

    def sent(self):
        for n in range(4):
            self.move(n).wait_send()


def enter_kernel(
    n_dev, tok, cot, rand, wq, wk, wv, qb, vb, ub, wo, up, down,
    x, q, ko, kf, vo, vf, attn, lse, ids, ubs, wt_out, cot_out, wo_out, up_out, down_out,
    wt, qbs, vbs, ids_for,
    tok_send, tok_recv, cot_send, cot_recv, p_send, p_recv, o_send, o_recv, s_send, s_recv, kv_send, kv_recv, local,
):
    spots = me, t, side, core = place()
    near = (me, tp_peer(side, core, 1))
    hidden, width = wq.shape
    units = down.shape[0]
    span = x.shape[0]
    heads = hidden // HD
    pairs = width // (2 * HD)
    part = hidden // 2
    n_part = units // 2 // part

    holds = [(w, lambda j, m=m: wt.at[m, j]) for m, w in ((1, wk), (2, wv), (0, wq))]
    holds += [
        (wo, lambda j: wo_out.at[pl.ds(j * hidden, hidden), :]),
        (up, lambda j: up_out.at[:, pl.ds(j * units, units)]),
        (down, lambda j: down_out.at[pl.ds(j * units, units), :]),
    ]
    pieces = []
    for n, (ref, block) in enumerate(holds):
        for i in range(1 if n < 4 else n_part):
            count = 1 if n < 4 else n_part

            def rows(r, h, i=i, count=count):
                return r.at[pl.ds((h * count + i) * part, part), :]

            at = len(pieces)
            pieces.append(
                Piece(
                    at, (1, 2)[at % 2],
                    lambda h, ref=ref, rows=rows: rows(ref, h),
                    lambda j, h, block=block, rows=rows: rows(block(j), h),
                    spots, (p_send, p_recv),
                )
            )

    def own_near(n):
        return remote(holds[n][0], holds[n][1](core), o_send, o_recv, n, near)

    def own_here(n):
        return pltpu.make_async_copy(holds[n][0], holds[n][1](core), local.at[n])

    def spread(src, dst, sends, recvs):
        return [
            remote(
                src.at[2 * lax.rem(me + k, n_dev) + side, pl.ds(core * BLOCK, BLOCK), :],
                dst.at[pl.ds(k * BLOCK, BLOCK), :],
                sends, recvs, k - 1, (lax.rem(me + k, n_dev), t),
            )
            for k in range(1, n_dev)
        ]

    def kept(n):
        src, dst = ((tok, x), (cot, cot_out))[n]
        return pltpu.make_async_copy(
            src.at[2 * me + side, pl.ds(core * BLOCK, BLOCK), :], dst.at[pl.ds(0, BLOCK), :], local.at[6 + n]
        )

    def shared(bits, which=(0, 1, 2, 3)):
        slot = (bits & 2) + core
        to = tp_peer(side, core, bits)
        moves = (
            (qb, qbs.at[slot]), (vb, vbs.at[slot]), (ub, ubs.at[slot]),
            (ids_for.at[to], ids.at[pl.ds(slot * heads, heads)]),
        )
        return [
            remote(*moves[n], s_send, s_recv, (bits - 1, n), (me, to)) for n in which
        ]

    greet(all_peers(n_dev, *spots) + [(me, tp_peer(side, core, 3))])
    for move in spread(tok, x, tok_send, tok_recv):
        move.start()
    for piece in pieces[:3]:
        piece.start()
    kept(0).start()
    for n in range(3):
        own_near(n).start()
        own_here(n).start()
    qbs[core], vbs[core], ubs[core] = qb[...], vb[...], ub[...]
    for bits in (1, 2, 3):
        for move in shared(bits, (0, 1, 2)):
            move.start()
    for piece in pieces[3:]:
        piece.start()
    for n in range(3, 6):
        own_near(n).start()
        own_here(n).start()

    lane = lax.broadcasted_iota(jnp.int32, (1, span), 1)
    for y in range(2):
        for c in range(2):
            block = 2 * lax.rem(me - lane // BLOCK + n_dev, n_dev) + c
            for h in range(heads):
                for r in range(3):
                    line = rand[h, r, pl.ds(2 * me + y, 1), :]
                    row = jnp.zeros((1, span), jnp.int32)
                    for b in range(c, 2 * n_dev, 2):
                        row = jnp.where(block == b, line[:, b : b + 1], row)
                    ids_for[2 * y + c, h, r : r + 1, :] = row
    ids[pl.ds(core * heads, heads)] = ids_for[t]
    for bits in (1, 2, 3):
        shared(bits, (3,))[0].start()

    for piece in pieces[:3]:
        piece.pass_on()
    for piece in pieces[:3]:
        piece.pass_side()
    for move in spread(tok, x, tok_send, tok_recv):
        move.wait_recv()
    kept(0).wait()
    for move in spread(cot, cot_out, cot_send, cot_recv):
        move.start()
    kept(1).start()
    for bits in (1, 2, 3):
        for move in shared(bits):
            move.wait_recv()

    def bias_of(ref):
        return jnp.concatenate([ref[j] for j in range(4)], 1)

    def project(n, m):
        own_near(n).wait_recv()
        own_here(n).wait()
        pieces[n].arrive()
        return back_dot(x[...], wt[m].reshape(width, width))

    def swap_kv(n):
        src, dst = ((ko, kf), (vo, vf))[n]
        return remote(src, dst, kv_send, kv_recv, n, near)

    ko[...] = project(0, 1).astype(jnp.bfloat16)
    swap_kv(0).start()
    vo[...] = (project(1, 2) + bias_of(vbs)).astype(jnp.bfloat16)
    swap_kv(1).start()
    q[...] = (project(2, 0) + bias_of(qbs)).astype(jnp.bfloat16)
    keep = pltpu.make_async_copy(wt, wt_out, local.at[8])
    keep.start()
    for n in (3, 4):
        pieces[n].pass_on()
    pieces[3].pass_side()
    swap_kv(0).wait_recv()
    swap_kv(1).wait_recv()

    def pair(p, carry):
        lanes = pl.ds(pl.multiple_of(p * 2 * HD, 2 * HD), 2 * HD)
        attend_pair(n_dev, p, lanes, q, ko, kf, vo, vf, ids, attn, lse, me, core)
        for k in range(5):

            @pl.when(p == k)
            def _():
                pieces[5 + k].pass_on()
                pieces[4 + k].pass_side()

        return carry

    lax.fori_loop(0, pairs, pair, 0)
    for n in range(10, len(pieces)):
        pieces[n].pass_on()
        pieces[n - 1].pass_side()
    pieces[-1].pass_side()
    for n in range(3, len(pieces)):
        pieces[n].arrive()
    for move in spread(cot, cot_out, cot_send, cot_recv):
        move.wait()
    kept(1).wait()
    keep.wait()
    for move in spread(tok, x, tok_send, tok_recv):
        move.wait_send()
    for piece in pieces:
        piece.sent()
    for n in range(6):
        own_near(n).wait_send()
        if n > 2:
            own_near(n).wait_recv()
            own_here(n).wait()
    for bits in (1, 2, 3):
        for move in shared(bits):
            move.wait_send()
    for n in range(2):
        swap_kv(n).wait_send()


def enter(tok, cot, rand, wq, wk, wv, qb, vb, ub, wo, up, down, n_dev):
    hidden, width = wq.shape
    units = down.shape[0]
    span = n_dev * BLOCK
    heads = hidden // HD
    pieces = 4 + 2 * (units // hidden)
    vmem = pl.BlockSpec(memory_space=pltpu.VMEM)
    hbm = pl.BlockSpec(memory_space=pl.ANY)
    shape = lambda dtype, *dims: jax.ShapeDtypeStruct(dims, dtype)
    low = partial(shape, jnp.bfloat16)
    dma = pltpu.SemaphoreType.DMA
    return pl.pallas_call(
        partial(enter_kernel, n_dev),
        in_specs=[hbm, hbm, vmem] + [hbm] * 3 + [vmem] * 3 + [hbm] * 3,
        out_specs=[vmem] * 10 + [hbm] * 5,
        out_shape=[low(span, width)] * 7
        + [
            shape(jnp.float32, 2 * heads, 2, span),
            shape(jnp.int32, 4 * heads, 3, span),
            shape(jnp.float32, 4, 1, units),
            low(3, 4, hidden, width),
            low(span, width),
            low(width, width),
            low(width, 4 * units),
            low(4 * units, width),
        ],
        scratch_shapes=[
            pltpu.VMEM((3, 4, hidden, width), jnp.bfloat16),
            pltpu.VMEM((4, 1, hidden), jnp.float32),
            pltpu.VMEM((4, 1, hidden), jnp.float32),
            pltpu.VMEM((4, heads, 3, span), jnp.int32),
            dma((n_dev - 1,)),
            dma((n_dev - 1,)),
            dma((n_dev - 1,)),
            dma((n_dev - 1,)),
            dma((pieces, 4)),
            dma((pieces, 4)),
            dma((6,)),
            dma((6,)),
            dma((3, 4)),
            dma((3, 4)),
            dma((2,)),
            dma((2,)),
            dma((9,)),
        ],
        compiler_params=pltpu.CompilerParams(
            collective_id=0, has_side_effects=True, vmem_limit_bytes=56 * 2**20
        ),
    )(tok, cot, rand, wq, wk, wv, qb, vb, ub, wo, up, down)


def list_bias(ids_ref, h, key_shift, me, core, n_dev, span):
    n_blocks = 2 * n_dev
    row = lax.broadcasted_iota(jnp.int32, (n_dev, span), 0)
    lane = lax.broadcasted_iota(jnp.int32, (n_dev, span), 1)
    wrap = lambda i: lax.rem(me - i + n_dev, n_dev)
    k = 2 * wrap(row) + (1 - core if key_shift else core)
    b = 2 * wrap(lane // BLOCK) + core
    one = lambda flag: jnp.where(flag, 1.0, 0.0)
    count = (
        one(k == 0)
        + one(k == n_blocks - 1)
        + one((k == b - 1) & (b != 1))
        + one(k == b)
        + one((k == b + 1) & (b != n_blocks - 2))
    )
    for r in range(3):
        count = count + one(ids_ref[h, r : r + 1, :] == k)
    count = jnp.where((b == 0) | (b == n_blocks - 1), 1.0, count)
    return jnp.where(count > 0.5, jnp.log(jnp.maximum(count, 1.0)), masked_score)


def attend_pair(n_dev, p, lanes, q_ref, ko, kf, vo, vf, ids, attn, lse, me, core):
    span = q_ref.shape[0]
    blocks = span // BLOCK
    lane = lax.broadcasted_iota(jnp.int32, (1, 2 * HD), 1) // HD
    q = q_ref[:, lanes]
    keys = (ko[:, lanes], kf[:, lanes])
    values = (vo[:, lanes].T, vf[:, lanes].T)
    outs = []
    for h in range(2):
        qh = (jnp.where(lane == h, q, 0.0) * 0.125).astype(jnp.bfloat16)
        scores = []
        for far in range(2):
            bias = list_bias(ids, 2 * p + h, far == 1, me, core, n_dev, span)
            raw = back_dot(keys[far], qh).reshape(blocks, BLOCK, span)
            scores.append((raw + bias[:, None, :]).reshape(span, span))
        top = jnp.maximum(*(jnp.max(s, 0, keepdims=True) for s in scores))
        expo = [jnp.exp(s - top) for s in scores]
        total = sum(jnp.sum(e, 0, keepdims=True) for e in expo)
        rows = slice(h * HD, (h + 1) * HD)
        acc = sum(plain_dot(v[rows], e.astype(jnp.bfloat16)) for v, e in zip(values, expo))
        outs.append(acc / total)
        lse[p, h : h + 1, :] = top + jnp.log(total)
    attn[:, lanes] = jnp.concatenate(outs, 0).T.astype(jnp.bfloat16)


def flip(index, bit):
    value = lax.rem(lax.div(index, bit), 2)
    return index + bit - 2 * bit * value, value


class Reduction:
    def __init__(self, parts, mine, spots, bufs, sems):
        self.parts, self.mine = parts, mine
        self.me, self.t, self.side, self.core = spots
        self.b0, self.b1, self.acc, self.halves, self.got, self.f = bufs
        self.send, self.recv, self.send0, self.recv0 = sems
        self.near = (self.me, tp_peer(self.side, self.core, 1))
        self.across = (self.me, tp_peer(self.side, self.core, 2))
        self.mates = []
        self.bits = []
        for bit in (1, 2, 4):
            mate, value = flip(self.me, bit)
            self.mates.append((mate, self.t))
            self.bits.append(value)

    def span(self, ref, start, size):
        return ref.at[pl.ds(pl.multiple_of(start, 16), size), :]

    def rows(self, depth):
        start, size, inner = 0, self.f.shape[1], 0
        for level in range(depth):
            size //= 2
            start = start + self.bits[level] * size
            inner = inner + (self.bits[level] * size if level else 0)
        return start, inner, size

    def first(self, ch):
        moves = []
        for y in range(2):
            at = 0
            for ref in self.parts(ch, 2 * y + 1 - self.core):
                rows = pl.ds(at, ref.shape[0])
                at += ref.shape[0]
                n = len(moves)
                moves.append(
                    remote(ref, self.b0.at[ch, y, rows, :], self.send0, self.recv0, (ch, n), self.near)
                )
        return moves

    def over_y(self, ch):
        return remote(self.mine(ch, 1), self.b1.at[ch], self.send, self.recv, (ch, 0), self.across)

    def halving(self, ch, level):
        size = self.rows(level + 1)[2]
        return remote(
            self.halves.at[ch, pl.ds(size, size), :],
            self.got.at[ch, pl.ds(size, size), :],
            self.send, self.recv, (ch, 1 + level), self.mates[level],
        )

    def gather(self, ch, level):
        start, _, size = self.rows(level + 1)
        held = self.span(self.f.at[ch], start, size)
        return remote(held, held, self.send, self.recv, (ch, 4 + level), self.mates[level])

    def stage(self, ch, s):
        full = jnp.float32
        if s == 0:
            for move in self.first(ch):
                move.start()
        elif s == 1:
            for move in self.first(ch):
                move.wait_recv()
            out = self.mine(ch, 1)
            out[...] = (out[...].astype(full) + self.b0[ch, 1].astype(full)).astype(jnp.bfloat16)
            self.over_y(ch).start()
        elif s == 2:
            self.over_y(ch).wait_recv()
            size = self.rows(1)[2]

            def total(start):
                terms = (self.mine(ch, 0), self.b0.at[ch, 0], self.b1.at[ch])
                one, two, three = (self.span(ref, start, size)[...].astype(full) for ref in terms)
                return one + two + three

            self.halves[ch, pl.ds(size, size), :] = total((1 - self.bits[0]) * size).astype(jnp.bfloat16)
            self.halving(ch, 0).start()
            self.acc[ch] = total(self.bits[0] * size)
        elif s <= 5:
            level = s - 3
            _, inner, size = self.rows(level + 1)
            self.halving(ch, level).wait_recv()
            total = self.span(self.acc.at[ch], inner, size)[...] + self.got[ch, pl.ds(size, size), :].astype(full)
            if s == 5:
                self.span(self.f.at[ch], self.rows(3)[0], size)[...] = total.astype(jnp.bfloat16)
                self.gather(ch, 2).start()
            else:
                self.span(self.acc.at[ch], inner, size)[...] = total
                small = size // 2
                other = self.span(self.acc.at[ch], inner + (1 - self.bits[level + 1]) * small, small)
                self.halves[ch, pl.ds(small, small), :] = other[...].astype(jnp.bfloat16)
                self.halving(ch, level + 1).start()
        elif s <= 7:
            self.gather(ch, 8 - s).wait_recv()
            self.gather(ch, 7 - s).start()
        else:
            self.gather(ch, 0).wait_recv()

    def finish(self, ch):
        for move in self.first(ch):
            move.wait_send()
        self.over_y(ch).wait_send()
        for level in range(3):
            self.halving(ch, level).wait_send()
            self.gather(ch, level).wait_send()


class Return:
    def __init__(self, at, n_dev, src, dst, spots, sems):
        self.at, self.n_dev, self.src, self.dst = at, n_dev, src, dst
        self.me, self.t, self.side, self.core = spots
        self.send, self.recv, self.local = sems
        self.near = (self.me, tp_peer(self.side, self.core, 1))
        self.across = (self.me, tp_peer(self.side, self.core, 2))

    def block(self, s, side):
        return self.dst.at[s, side, pl.ds(self.core * BLOCK, BLOCK), :]

    def keep(self):
        return pltpu.make_async_copy(
            self.src.at[pl.ds(0, BLOCK), :], self.block(self.me, self.side), self.local.at[self.at]
        )

    def out(self, k):
        to = lax.rem(self.me - k + self.n_dev, self.n_dev)
        return remote(
            self.src.at[pl.ds(k * BLOCK, BLOCK), :], self.block(self.me, self.side),
            self.send, self.recv, (self.at, k - 1), (to, self.t),
        )

    def pass_on(self, n):
        side = 1 - self.side if n == 2 else self.side
        held = self.dst.at[:, side, pl.ds(self.core * BLOCK, BLOCK), :]
        peer = self.across if n == 0 else self.near
        return remote(held, held, self.send, self.recv, (self.at, self.n_dev - 1 + n), peer)

    def stage(self, s):
        if s == 0:
            self.keep().start()
            for k in range(1, self.n_dev):
                self.out(k).start()
        elif s == 1:
            self.keep().wait()
            for k in range(1, self.n_dev):
                self.out(k).wait_recv()
            self.pass_on(0).start()
            self.pass_on(1).start()
        elif s == 2:
            self.pass_on(0).wait_recv()
            self.pass_on(2).start()
        else:
            for k in range(1, self.n_dev):
                self.out(k).wait_send()
            self.pass_on(0).wait_send()
            self.pass_on(1).wait()
            self.pass_on(2).wait()


class SmallSum:
    def __init__(self, out, came, spots, sems):
        self.out, self.came = out, came
        me, t, side, core = spots
        self.send, self.recv = sems
        self.peers = [(me, tp_peer(side, core, 1)), (me, tp_peer(side, core, 2))]
        self.peers += [(flip(me, bit)[0], t) for bit in (1, 2, 4)]

    def move(self, n):
        held = self.out.at[n]
        return remote(held, self.came.at[n], self.send, self.recv, n, self.peers[n])

    def stage(self, n):
        if n:
            self.move(n - 1).wait_recv()
            self.out[n] = self.out[n - 1] + self.came[n - 1]
        if n < len(self.peers):
            self.move(n).start()

    def finish(self):
        for n in range(len(self.peers)):
            self.move(n).wait_send()


def all_peers(n_dev, me, t, side, core):
    return [(lax.rem(me + k, n_dev), t) for k in range(1, n_dev)] + [
        (me, tp_peer(side, core, bits)) for bits in (1, 2)
    ]


def tail_kernel(
    n_dev, q, ko, kf, vo, vf, ids, lse, attn, gat, x, gres, early, gd, gu, go, low, wt_hbm,
    f, out, iout, total,
    load, p2, wt, b0, b1, acc, halves, got, came, dq, own, far, far_in, ig,
    send, recv, send0, recv0, local, x_send, x_recv, r_send, r_recv, r_local, s_send, s_recv,
):
    spots = me, t, side, core = place()
    units, hidden = gd.shape[0] // 4, go.shape[0] // 4
    span, width = q.shape
    rows = f.shape[1]
    n_down = units // rows
    n_ffn = n_down + gu.shape[0] // rows
    count = f.shape[0]
    pairs = width // (2 * HD)
    near = (me, tp_peer(side, core, 1))

    def parts(ch, block):
        if ch < n_down:
            return [gd.at[pl.ds(block * units + ch * rows, rows), :]]
        if ch < n_ffn:
            return [gu.at[pl.ds((ch - n_down) * rows, rows), pl.ds(block * units, units)]]
        return [p2.at[ch - n_ffn, block]]

    def mine(ch, y):
        return load.at[ch, y] if ch < n_ffn else p2.at[ch - n_ffn, 2 * y + core]

    red = Reduction(parts, mine, spots, (b0, b1, acc, halves, got, f), (send, recv, send0, recv0))
    back = [
        Return(n, n_dev, src, dst, spots, (r_send, r_recv, r_local))
        for n, (src, dst) in enumerate(((low, out), (ig, iout)))
    ]
    tiny = SmallSum(total, came, spots, (s_send, s_recv))

    def loads(ch):
        return [
            pltpu.make_async_copy(parts(ch, 2 * y + core)[0], mine(ch, y), local.at[2 * ch + y])
            for y in range(2)
        ]

    def others():
        pieces = [(wt_hbm, wt)] + [
            (go.at[pl.ds(j * hidden, hidden), :], p2.at[0, j, pl.ds(0, hidden), :]) for j in range(4)
        ]
        return [
            pltpu.make_async_copy(a, b, local.at[2 * n_ffn + n]) for n, (a, b) in enumerate(pieces)
        ]

    def swap_far(p, n):
        return remote(far.at[n, p], far_in.at[n, p], x_send, x_recv, (p, n), near)

    greet(all_peers(n_dev, *spots))
    for ch in range(n_ffn):
        red.stage(ch, 0)
        for move in loads(ch):
            move.start()
    back[0].stage(0)
    for move in others():
        move.start()

    def pair(p, carry):
        lanes = pl.ds(pl.multiple_of(p * 2 * HD, 2 * HD), 2 * HD)
        attend_pair_back(n_dev, p, lanes, q, ko, kf, vo, vf, ids, lse, attn, gat, dq, own, far, me, core)
        for n in range(2):
            swap_far(p, n).start()
        for k in range(2):

            @pl.when(p == k)
            def _():
                for ch in range(k * n_ffn // 2, (k + 1) * n_ffn // 2):
                    for move in loads(ch):
                        move.wait()
                    red.stage(ch, 1)

        return carry

    lax.fori_loop(0, pairs, pair, 0)

    for p in range(pairs):
        for n in range(2):
            swap_far(p, n).wait_recv()

    def joined_low(n):
        cat = jnp.concatenate([far_in[n, p] for p in range(pairs)], 1)
        return (own[n] + cat.astype(jnp.float32)).astype(jnp.bfloat16)

    def weight_grad(low_grad, ch, at):
        grad = plain_dot(low_grad.T, x[...]).astype(jnp.bfloat16)
        for j in range(4):
            p2[ch, j, pl.ds(at, hidden), :] = grad[j * hidden : (j + 1) * hidden]

    def column_sum(low_grad):
        sums = jnp.sum(low_grad.astype(jnp.float32), 0, keepdims=True)
        turned = jnp.concatenate([sums[:, width // 2 :], sums[:, : width // 2]], 1)
        return jnp.where(side == 0, sums, turned)

    red.stage(0, 2)
    weight_grad(dq[...], 0, hidden)
    for move in others():
        move.wait()
    red.stage(n_ffn, 0)
    dk = joined_low(0)
    weight_grad(dk, 1, 0)
    dv = joined_low(1)
    weight_grad(dv, 1, hidden)
    red.stage(n_ffn + 1, 0)
    total[0] = early[...]
    total[0, 0:1, :] = column_sum(dq[...])
    total[0, 1:2, :] = column_sum(dv)
    tiny.stage(0)
    red.stage(n_ffn, 1)
    matrix = lambda m: wt[m].reshape(width, width)
    into = gres[...] + plain_dot(dq[...], matrix(0))
    into = into + plain_dot(dk, matrix(1))
    ig[...] = (into + plain_dot(dv, matrix(2))).astype(jnp.bfloat16)
    red.stage(n_ffn + 1, 1)
    back[1].stage(0)
    back[0].stage(1)

    events = []
    for ch in range(count):
        for s in range(2, 9):
            if (ch, s) != (0, 2):
                events.append((17 + 12.6 * ch + (0, 0, 0, 8, 13, 18, 23, 28, 35)[s], red, (ch, s)))
    for n in range(1, 6):
        events.append(((36, 84, 88, 92, 98)[n - 1], tiny, (n,)))
    events += [(55, back[1], (1,)), (96, back[0], (2,)), (114, back[1], (2,))]
    for _, who, what in sorted(events, key=lambda e: e[0]):
        who.stage(*what)
    for b in back:
        b.stage(3)
    for ch in range(count):
        red.finish(ch)
    tiny.finish()
    for p in range(pairs):
        for n in range(2):
            swap_far(p, n).wait_send()


def attend_pair_back(n_dev, p, lanes, q_ref, ko, kf, vo, vf, ids, lse_ref, attn, gat, dq, own, far, me, core):
    span = q_ref.shape[0]
    blocks = span // BLOCK
    lane = lax.broadcasted_iota(jnp.int32, (1, 2 * HD), 1) // HD
    q, g = q_ref[:, lanes], gat[:, lanes]
    weighted = (attn[:, lanes].astype(jnp.float32) * g.astype(jnp.float32)).T
    parts = ((ko[:, lanes], vo[:, lanes]), (kf[:, lanes], vf[:, lanes]))
    k_ts = [k.T for k, _ in parts]
    dks = [None, None]
    dvs = [None, None]
    dq_ts = []
    for h in range(2):
        rows = slice(h * HD, (h + 1) * HD)
        qh = (jnp.where(lane == h, q, 0.0) * 0.125).astype(jnp.bfloat16)
        gh = jnp.where(lane == h, g, 0.0).astype(jnp.bfloat16)
        delta = jnp.sum(weighted[rows], 0, keepdims=True)
        lse = lse_ref[p, h : h + 1, :]
        dq_t = None
        for at, (k, v) in enumerate(parts):
            bias = list_bias(ids, 2 * p + h, at == 1, me, core, n_dev, span)
            raw = back_dot(k, qh).reshape(blocks, BLOCK, span)
            raw = (raw + bias[:, None, :]).reshape(span, span)
            prob = jnp.exp(raw - lse)
            dprob = back_dot(v, gh)
            dscore = (prob * (dprob - delta)).astype(jnp.bfloat16)
            dv = plain_dot(prob.astype(jnp.bfloat16), gh)
            dk = plain_dot(dscore, qh)
            dvs[at] = dv if dvs[at] is None else dvs[at] + dv
            dks[at] = dk if dks[at] is None else dks[at] + dk
            piece = plain_dot(k_ts[at][rows], dscore)
            dq_t = piece if dq_t is None else dq_t + piece
        dq_ts.append(dq_t * 0.125)
    dq[:, lanes] = jnp.concatenate(dq_ts, 0).T.astype(jnp.bfloat16)
    for n, grads in enumerate((dks, dvs)):
        own[n, :, lanes] = grads[0]
        far[n, p] = grads[1].astype(jnp.bfloat16)


def tail(q, ko, kf, vo, vf, ids, lse, attn, gat, x, gres, early, gd, gu, go, low, wt, n_dev):
    span, width = q.shape
    hidden = go.shape[0] // 4
    rows = 2 * hidden
    n_ffn = (gd.shape[0] // 4 + gu.shape[0]) // rows
    count = n_ffn + 2
    pairs = width // (2 * HD)
    vmem = pl.BlockSpec(memory_space=pltpu.VMEM)
    hbm = pl.BlockSpec(memory_space=pl.ANY)
    dma = pltpu.SemaphoreType.DMA
    landed = jax.ShapeDtypeStruct((n_dev, 2, 2 * BLOCK, width), jnp.bfloat16)
    low_buf = lambda *shape: pltpu.VMEM(shape + (width,), jnp.bfloat16)
    pair_buf = pltpu.VMEM((2, pairs, span, 2 * HD), jnp.bfloat16)
    return pl.pallas_call(
        partial(tail_kernel, n_dev),
        in_specs=[vmem] * 12 + [hbm] * 5,
        out_specs=[vmem, hbm, hbm, vmem],
        out_shape=[
            jax.ShapeDtypeStruct((count, rows, width), jnp.bfloat16),
            landed,
            landed,
            jax.ShapeDtypeStruct((6,) + early.shape, jnp.float32),
        ],
        scratch_shapes=[
            low_buf(n_ffn, 2, rows),
            low_buf(2, 4, rows),
            pltpu.VMEM(wt.shape, jnp.bfloat16),
            low_buf(count, 2, rows),
            low_buf(count, rows),
            pltpu.VMEM((count, rows // 2, width), jnp.float32),
            low_buf(count, rows),
            low_buf(count, rows),
            pltpu.VMEM((5,) + early.shape, jnp.float32),
            low_buf(span),
            pltpu.VMEM((2, span, width), jnp.float32),
            pair_buf,
            pair_buf,
            low_buf(span),
            dma((count, 7)),
            dma((count, 7)),
            dma((count, 2)),
            dma((count, 2)),
            dma((2 * n_ffn + 5,)),
            dma((pairs, 2)),
            dma((pairs, 2)),
            dma((2, n_dev + 2)),
            dma((2, n_dev + 2)),
            dma((2,)),
            dma((5,)),
            dma((5,)),
        ],
        compiler_params=pltpu.CompilerParams(
            collective_id=2, has_side_effects=True, vmem_limit_bytes=60 * 2**20
        ),
    )(q, ko, kf, vo, vf, ids, lse, attn, gat, x, gres, early, gd, gu, go, low, wt)


def norm_parts(resid):
    centre = resid - jnp.mean(resid, -1, keepdims=True)
    inverse = lax.rsqrt(jnp.mean(centre * centre, -1, keepdims=True) + norm_eps)
    return centre * inverse, inverse


def norm_back(grad, unit, inverse, gain):
    scaled = grad * gain
    pull = scaled - jnp.mean(scaled, -1, keepdims=True)
    pull = pull - unit * jnp.mean(scaled * unit, -1, keepdims=True)
    return pull * inverse, jnp.sum(grad * unit, 0), jnp.sum(grad, 0)


def whole_sequences(
    tokens,
    rand_blocks,
    query_weight,
    query_bias,
    key_weight,
    value_weight,
    value_bias,
    output_weight,
    output_bias,
    attn_gain,
    attn_shift,
    up_weight,
    up_bias,
    down_weight,
    down_bias,
    ffn_gain,
    ffn_shift,
    cotangent,
):
    seqs, rows, width = tokens.shape
    n_dev = lax.axis_size("seq")
    me = lax.axis_index("seq")
    t = lax.axis_index("tp")
    side, core = t // 2, t % 2
    n_blocks = rows // BLOCK * n_dev
    hidden = query_weight.shape[1]
    units = up_weight.shape[1]
    span = n_dev * BLOCK

    (
        x, q, k_own, k_far, v_own, v_far, attn_low, lse, ids, u_bias, wt, cot, wo, w_up, w_down,
    ) = enter(
        tokens, cotangent, rand_blocks.transpose(2, 3, 0, 1), query_weight.T, key_weight.T, value_weight.T,
        query_bias[None], value_bias[None], up_bias[None], output_weight, up_weight, down_weight, n_dev,
    )
    u_bias = u_bias.reshape(4 * units)
    branch = plain_dot(attn_low, wo) + output_bias
    unit_one, inverse_one = norm_parts(x.astype(jnp.float32) + branch)
    normed = unit_one * attn_gain + attn_shift
    normed_low = normed.astype(jnp.bfloat16)
    pre_act = plain_dot(normed_low, w_up) + u_bias
    cdf = 0.5 * (1.0 + lax.erf(pre_act * HALF_ROOT))
    act_low = (pre_act * cdf).astype(jnp.bfloat16)
    slope = (cdf + pre_act * (PDF_SCALE * jnp.exp(-0.5 * pre_act * pre_act))).astype(jnp.bfloat16)
    ffn = plain_dot(act_low, w_down) + down_bias
    unit_two, inverse_two = norm_parts(normed + ffn)
    out_low = (unit_two * ffn_gain + ffn_shift).astype(jnp.bfloat16)

    g_resid2, grad_ffngain, grad_ffnshift = norm_back(
        cot.astype(jnp.float32), unit_two, inverse_two, ffn_gain
    )
    g_ffn = g_resid2.astype(jnp.bfloat16)
    grad_downbias = jnp.sum(g_ffn.astype(jnp.float32), 0)
    grad_down = rows_dot(act_low, g_ffn).astype(jnp.bfloat16)
    g_pre = (back_dot(g_ffn, w_down) * slope.astype(jnp.float32)).astype(jnp.bfloat16)
    grad_upbias = jnp.sum(g_pre.astype(jnp.float32), 0)
    grad_up = rows_dot(normed_low, g_pre).astype(jnp.bfloat16)
    g_normed = g_resid2 + back_dot(g_pre, w_up)
    g_resid, grad_attngain, grad_attnshift = norm_back(g_normed, unit_one, inverse_one, attn_gain)
    g_branch = g_resid.astype(jnp.bfloat16)
    grad_obias = jnp.sum(g_branch.astype(jnp.float32), 0)
    grad_o = rows_dot(attn_low, g_branch).astype(jnp.bfloat16)
    g_attn = back_dot(g_branch, wo).astype(jnp.bfloat16)

    ups = grad_upbias.reshape(2, 2, units)
    ups = jnp.where(side == 0, ups, ups[::-1]).reshape(4, width)
    late = jnp.zeros((2, width), jnp.float32)
    lines = [grad_obias, grad_attngain, grad_attnshift, grad_downbias, grad_ffngain, grad_ffnshift]
    early = jnp.concatenate([late, ups, jnp.stack(lines), late, late], 0)
    sums, layer_output, input_out, small = tail(
        q, k_own, k_far, v_own, v_far, ids, lse, attn_low, g_attn, x, g_resid, early,
        grad_down, grad_up, grad_o, out_low, wt, n_dev,
    )
    small = small[5]

    def share(first, size):
        whole = small[first : first + 4 * size // width].reshape(4, size)
        return lax.dynamic_index_in_dim(whole, t, 0, False)

    sums = sums.astype(jnp.float32)
    half = units // sums.shape[1]
    g_down = sums[:half].reshape(units, width)
    g_up = sums[half : half + width // sums.shape[1]].reshape(width, units)
    g_o, g_q = sums[-2, :hidden], sums[-2, hidden:]
    g_k, g_v = sums[-1, :hidden], sums[-1, hidden:]
    return (
        layer_output.reshape(seqs, rows, width),
        input_out.astype(jnp.float32).reshape(seqs, rows, width),
        g_q.T,
        share(0, hidden),
        g_k.T,
        g_v.T,
        share(1, hidden),
        g_o,
        small[6],
        small[7],
        small[8],
        g_up,
        share(2, units),
        g_down,
        small[9],
        small[10],
        small[11],
    )


def per_device(tokens, *rest):
    seqs, rows, _ = tokens.shape
    n_dev = lax.axis_size("seq")
    if lax.axis_size("tp") == 4 and n_dev == 8 and seqs == 2 * n_dev and rows == 2 * BLOCK:
        return whole_sequences(tokens, *rest)
    return split_sequences(tokens, *rest)


def solution(mesh):
    placed = (
        P(None, "seq", None),
        P(None, None, "tp", None),
        P(None, "tp"),
        P("tp"),
        P(None, "tp"),
        P(None, "tp"),
        P("tp"),
        P("tp", None),
        P(),
        P(),
        P(),
        P(None, "tp"),
        P("tp"),
        P("tp", None),
        P(),
        P(),
        P(),
        P(None, "seq", None),
    )
    return jax.shard_map(
        per_device,
        mesh=mesh,
        in_specs=placed,
        out_specs=(
            P(None, "seq", None),
            P(None, "seq", None),
            P(None, "tp"),
            P("tp"),
            P(None, "tp"),
            P(None, "tp"),
            P("tp"),
            P("tp", None),
            P(),
            P(),
            P(),
            P(None, "tp"),
            P("tp"),
            P("tp", None),
            P(),
            P(),
            P(),
        ),
        check_vma=False,
    )
```

```python
from functools import partial

import jax
import jax.numpy as jnp
from jax import lax
from jax.sharding import PartitionSpec as P
from jax.experimental import pallas as pl
from jax.experimental.pallas import tpu as pltpu

HD = 64
BLOCK = 64


norm_eps = 1e-06
masked_score = -1e30
highest_precision = lax.Precision.HIGHEST


def with_halo(shard, sides, width):
    for axis, dim in sides:
        size, length = (lax.axis_size(axis), shard.shape[dim])
        up = [(i, (i + 1) % size) for i in range(size - 1)]
        down = [(j, i) for i, j in up]
        last = lax.slice_in_dim(shard, length - width, length, axis=dim)
        first = lax.slice_in_dim(shard, 0, width, axis=dim)
        before = lax.ppermute(last, axis, up)
        after = lax.ppermute(first, axis, down)
        shard = jnp.concatenate([before, shard, after], axis=dim)
    return shard


def joined(shard, axis, combine):
    everything = jax.tree.map(lambda part: lax.all_gather(part, axis), shard)
    first = jax.tree.map(lambda part: part[0], everything)

    def hop(k, so_far):
        return combine(so_far, jax.tree.map(lambda part: part[k], everything))

    return lax.fori_loop(1, lax.axis_size(axis), hop, first)


def layer_norm(resid, gain, shift):
    centre = resid - jnp.mean(resid, -1, keepdims=True)
    spread = jnp.mean(centre * centre, -1, keepdims=True)
    return centre * lax.rsqrt(spread + norm_eps) * gain + shift


def gelu_exact(values):
    return jax.nn.gelu(values, approximate=False)


def plain_dot(left, right):
    return jnp.dot(left, right, preferred_element_type=jnp.float32)


def rows_dot(left, right):
    return lax.dot_general(
        left, right, (((0,), (0,)), ((), ())), preferred_element_type=jnp.float32
    )


def back_dot(left, right):
    return lax.dot_general(
        left, right, (((1,), (1,)), ((), ())), preferred_element_type=jnp.float32
    )


def softmax_row_probs(scores):
    top_score = jnp.max(scores, -1, keepdims=True)
    expo = jnp.exp(scores - top_score)
    return expo / jnp.sum(expo, -1, keepdims=True)


def head_sum_fwd(pieces):
    return lax.psum(pieces, "tp")


def head_sum_back(pieces):
    return lax.psum(pieces, "tp")


def merge_rows(first, second):
    top_score = jnp.maximum(first[0], second[0])
    scale_one = jnp.exp(first[0] - top_score)
    scale_two = jnp.exp(second[0] - top_score)
    return (
        top_score,
        first[1] * scale_one + second[1] * scale_two,
        first[2] * scale_one[..., None] + second[2] * scale_two[..., None],
    )


def tile_plan(rand_blocks, my_index, n_dev, per_dev, seqs, heads):
    count = seqs * per_dev * heads * 3
    capacity = max(2, 2 * count // n_dev)
    requests = (
        rand_blocks.reshape(seqs, n_dev, per_dev, heads, 3)
        .transpose(1, 0, 2, 3, 4)
        .reshape(n_dev, count)
    )
    is_mine = requests // per_dev == my_index
    ranking = jnp.cumsum(is_mine.astype(jnp.int32), 1) - 1
    slot_ids = jnp.arange(capacity, dtype=jnp.int32)
    select = is_mine[:, None, :] & (ranking[:, None, :] == slot_ids[None, :, None])
    filled = jnp.any(select, 2)
    position = jnp.arange(count, dtype=jnp.int32)
    seq_of = position // (per_dev * heads * 3)
    head_of = position // 3 % heads
    tile_of = (seq_of[None, :] * per_dev + requests % per_dev) * heads + head_of[None, :]
    send_index = jnp.sum(jnp.where(select, tile_of[:, None, :], 0), 2)
    own_requests = lax.dynamic_slice_in_dim(rand_blocks, my_index * per_dev, per_dev, 1).reshape(
        count
    )
    own_owner = own_requests // per_dev
    onehot = (own_owner[:, None] == jnp.arange(n_dev, dtype=jnp.int32)[None, :]).astype(jnp.int32)
    own_rank = jnp.sum((jnp.cumsum(onehot, 0) - 1) * onehot, 1)
    recv_index = own_owner * capacity + own_rank
    return (capacity, send_index, filled, recv_index)


def pick_tiles(incoming, recv_index, seqs, per_dev, heads, block, hsize):
    stacked = incoming.reshape(-1, block, 2 * hsize)
    return jnp.take(stacked, recv_index, 0).reshape(seqs, per_dev, heads, 3, block, 2 * hsize)


def assemble(end_part, window_part, tile_part, seqs, per_dev, heads, block, hsize):
    ends_wide = jnp.broadcast_to(end_part[:, None], (seqs, per_dev, heads, 2 * block, hsize))
    return jnp.concatenate(
        [ends_wide, window_part, tile_part.reshape(seqs, per_dev, heads, 3 * block, hsize)], 3
    )


def split_sequences(
    tokens,
    rand_blocks,
    query_weight,
    query_bias,
    key_weight,
    value_weight,
    value_bias,
    output_weight,
    output_bias,
    attn_gain,
    attn_shift,
    up_weight,
    up_bias,
    down_weight,
    down_bias,
    ffn_gain,
    ffn_shift,
    cotangent,
):
    seqs, rows, width = tokens.shape
    block = BLOCK
    hsize = HD
    per_dev = rows // block
    n_dev = lax.axis_size("seq")
    my_index = lax.axis_index("seq")
    n_blocks = per_dev * n_dev
    heads = query_weight.shape[1] // hsize
    hidden = heads * hsize
    n_tok = seqs * rows
    is_first = my_index == 0
    is_last = my_index == n_dev - 1
    flat = tokens.reshape(n_tok, width)
    query_low = (plain_dot(flat, query_weight) + query_bias).astype(jnp.bfloat16)
    key_low = plain_dot(flat, key_weight).astype(jnp.bfloat16)
    value_low = (plain_dot(flat, value_weight) + value_bias).astype(jnp.bfloat16)
    keyval = jnp.concatenate([key_low, value_low], 1).reshape(seqs, rows, 2 * hidden)
    extended = with_halo(keyval, (("seq", 1),), block)
    windows = jnp.stack(
        [extended[:, offset * block : (offset + 3) * block] for offset in range(per_dev)], 1
    )
    windows = windows.reshape(seqs, per_dev, 3 * block, 2, heads, hsize)
    win_key = windows[:, :, :, 0].transpose(0, 1, 3, 2, 4)
    win_value = windows[:, :, :, 1].transpose(0, 1, 3, 2, 4)
    triple = jnp.concatenate([query_low.reshape(seqs, rows, hidden), keyval], 2).astype(jnp.float32)
    own_ends = jnp.stack(
        [
            jnp.where(is_first, triple[:, :block], 0.0),
            jnp.where(is_last, triple[:, rows - block :], 0.0),
        ],
        1,
    )
    ends = lax.psum(own_ends.astype(jnp.bfloat16), "seq").reshape(seqs, 2, block, 3, heads, hsize)
    end_query = ends[:, :, :, 0].transpose(0, 3, 1, 2, 4).reshape(seqs, heads, 2 * block, hsize)
    end_key = ends[:, :, :, 1].transpose(0, 3, 1, 2, 4).reshape(seqs, heads, 2 * block, hsize)
    end_value = ends[:, :, :, 2].transpose(0, 3, 1, 2, 4).reshape(seqs, heads, 2 * block, hsize)
    capacity, send_index, filled, recv_index = tile_plan(
        rand_blocks, my_index, n_dev, per_dev, seqs, heads
    )
    table = (
        keyval.reshape(seqs, per_dev, block, 2, heads, hsize)
        .transpose(0, 1, 4, 2, 3, 5)
        .reshape(seqs * per_dev * heads, block, 2 * hsize)
    )
    outgoing = jnp.take(table, send_index.reshape(-1), 0).reshape(n_dev, capacity, block, 2 * hsize)
    outgoing = jnp.where(filled[:, :, None, None], outgoing, jnp.zeros((), jnp.bfloat16))
    incoming = lax.all_to_all(outgoing, "seq", split_axis=0, concat_axis=0, tiled=True)
    tiles = pick_tiles(incoming, recv_index, seqs, per_dev, heads, block, hsize)
    q_blocks = query_low.reshape(seqs, per_dev, block, heads, hsize).transpose(0, 1, 3, 2, 4)
    keys_all = assemble(end_key, win_key, tiles[..., :hsize], seqs, per_dev, heads, block, hsize)
    values_all = assemble(
        end_value, win_value, tiles[..., hsize:], seqs, per_dev, heads, block, hsize
    )
    block_ids = my_index * per_dev + jnp.arange(per_dev, dtype=jnp.int32)
    slot_ids = jnp.arange(8 * block, dtype=jnp.int32) // block
    dropped = (slot_ids == 2)[None, :] & (block_ids == 1)[:, None] | (slot_ids == 4)[None, :] & (
        block_ids == n_blocks - 2
    )[:, None]
    unscaled_scores = (
        jnp.einsum("sbhqd,sbhkd->sbhqk", q_blocks, keys_all, preferred_element_type=jnp.float32)
        * 0.125
    )
    unscaled_scores = jnp.where(dropped[None, :, None, None, :], masked_score, unscaled_scores)
    weights = softmax_row_probs(unscaled_scores)
    sparse_attention = jnp.einsum(
        "sbhqk,sbhkd->sbhqd",
        weights,
        values_all.astype(jnp.float32),
        precision=highest_precision,
        preferred_element_type=jnp.float32,
    )
    key_local = key_low.reshape(seqs, rows, heads, hsize).transpose(0, 2, 1, 3)
    value_local = value_low.reshape(seqs, rows, heads, hsize).transpose(0, 2, 1, 3)
    end_raw = (
        jnp.einsum("shqd,shkd->shqk", end_query, key_local, preferred_element_type=jnp.float32)
        * 0.125
    )
    end_top = jnp.max(end_raw, -1)
    end_expo = jnp.exp(end_raw - end_top[..., None])
    end_total = jnp.sum(end_expo, -1)
    end_acc = jnp.einsum(
        "shqk,shkd->shqd",
        end_expo,
        value_local.astype(jnp.float32),
        precision=highest_precision,
        preferred_element_type=jnp.float32,
    )
    merged_top, merged_total, merged_acc = joined((end_top, end_total, end_acc), "seq", merge_rows)
    end_out = merged_acc / merged_total[..., None]
    end_lse = merged_top + jnp.log(merged_total)
    end_split = end_out.reshape(seqs, heads, 2, block, hsize)
    first_rows = block_ids == 0
    last_rows = block_ids == n_blocks - 1
    attn = jnp.where(
        first_rows[None, :, None, None, None], end_split[:, None, :, 0], sparse_attention
    )
    attn = jnp.where(last_rows[None, :, None, None, None], end_split[:, None, :, 1], attn)
    attn_low = attn.transpose(0, 1, 3, 2, 4).reshape(n_tok, hidden).astype(jnp.bfloat16)
    branch = head_sum_fwd(plain_dot(attn_low, output_weight)) + output_bias
    resid = flat.astype(jnp.float32) + branch
    normed = layer_norm(resid, attn_gain, attn_shift)
    normed_low = normed.astype(jnp.bfloat16)
    pre_act = plain_dot(normed_low, up_weight) + up_bias
    act_low = gelu_exact(pre_act).astype(jnp.bfloat16)
    ffn = head_sum_fwd(plain_dot(act_low, down_weight)) + down_bias
    resid_two = normed + ffn
    layer_output = (
        layer_norm(resid_two, ffn_gain, ffn_shift).astype(jnp.bfloat16).reshape(seqs, rows, width)
    )
    cot_flat = cotangent.reshape(n_tok, width).astype(jnp.float32)
    norm_two, pull_two = jax.vjp(layer_norm, resid_two, ffn_gain, ffn_shift)
    grad_resid2, grad_ffngain, grad_ffnshift = pull_two(cot_flat)
    grad_ffn = grad_resid2.astype(jnp.bfloat16)
    grad_downbias = jnp.sum(grad_ffn.astype(jnp.float32), 0)
    grad_downweight = rows_dot(act_low, grad_ffn)
    grad_act = back_dot(grad_ffn, down_weight)
    gelu_out, pull_gelu = jax.vjp(gelu_exact, pre_act)
    grad_pre = pull_gelu(grad_act)[0].astype(jnp.bfloat16)
    grad_upbias = jnp.sum(grad_pre.astype(jnp.float32), 0)
    grad_upweight = rows_dot(normed_low, grad_pre)
    grad_normed = grad_resid2 + head_sum_back(back_dot(grad_pre, up_weight))
    norm_one, pull_one = jax.vjp(layer_norm, resid, attn_gain, attn_shift)
    grad_resid, grad_attngain, grad_attnshift = pull_one(grad_normed)
    grad_branch = grad_resid.astype(jnp.bfloat16)
    grad_obias = jnp.sum(grad_branch.astype(jnp.float32), 0)
    grad_oweight = rows_dot(attn_low, grad_branch)
    grad_attn = back_dot(grad_branch, output_weight).astype(jnp.bfloat16)
    grad_heads = grad_attn.reshape(seqs, per_dev, block, heads, hsize).transpose(0, 1, 3, 2, 4)
    global_mask = (first_rows | last_rows)[None, :, None, None, None]
    grad_sparse = jnp.where(global_mask, jnp.zeros((), jnp.bfloat16), grad_heads)
    own_dout = jnp.stack(
        [
            jnp.where(is_first, grad_heads[:, 0].astype(jnp.float32), 0.0),
            jnp.where(is_last, grad_heads[:, per_dev - 1].astype(jnp.float32), 0.0),
        ],
        2,
    ).reshape(seqs, heads, 2 * block, hsize)
    own_delta = jnp.sum(own_dout * end_out, -1)
    end_dout, end_delta = lax.psum((own_dout, own_delta), "seq")
    end_dlow = end_dout.astype(jnp.bfloat16)
    end_prob = jnp.exp(end_raw - end_lse[..., None])
    end_dprob = jnp.einsum(
        "shqd,shkd->shqk", end_dlow, value_local, preferred_element_type=jnp.float32
    )
    end_dscore = (end_prob * (end_dprob - end_delta[..., None]) * 0.125).astype(jnp.bfloat16)
    end_dquery_part = jnp.einsum(
        "shqk,shkd->shqd", end_dscore, key_local, preferred_element_type=jnp.float32
    )
    local_dkey = jnp.einsum(
        "shqk,shqd->shkd", end_dscore, end_query, preferred_element_type=jnp.float32
    )
    local_dvalue = jnp.einsum(
        "shqk,shqd->shkd",
        end_prob,
        end_dout,
        precision=highest_precision,
        preferred_element_type=jnp.float32,
    )
    again = lax.all_to_all(outgoing, "seq", split_axis=0, concat_axis=0, tiled=True)
    back_tiles = pick_tiles(again, recv_index, seqs, per_dev, heads, block, hsize)
    keys_back = assemble(
        end_key, win_key, back_tiles[..., :hsize], seqs, per_dev, heads, block, hsize
    )
    values_back = assemble(
        end_value, win_value, back_tiles[..., hsize:], seqs, per_dev, heads, block, hsize
    )
    grad_prob = jnp.einsum(
        "sbhqd,sbhkd->sbhqk", grad_sparse, values_back, preferred_element_type=jnp.float32
    )
    row_delta = jnp.sum(weights * grad_prob, -1, keepdims=True)
    grad_score = (weights * (grad_prob - row_delta) * 0.125).astype(jnp.bfloat16)
    grad_qblocks = jnp.einsum(
        "sbhqk,sbhkd->sbhqd", grad_score, keys_back, preferred_element_type=jnp.float32
    )
    grad_keysall = jnp.einsum(
        "sbhqk,sbhqd->sbhkd", grad_score, q_blocks, preferred_element_type=jnp.float32
    )
    grad_valsall = jnp.einsum(
        "sbhqk,sbhqd->sbhkd",
        weights,
        grad_sparse.astype(jnp.float32),
        precision=highest_precision,
        preferred_element_type=jnp.float32,
    )
    end_dkey = jnp.sum(grad_keysall[:, :, :, : 2 * block], 1)
    end_dvalue = jnp.sum(grad_valsall[:, :, :, : 2 * block], 1)
    win_grad = jnp.stack(
        [
            grad_keysall[:, :, :, 2 * block : 5 * block].transpose(0, 1, 3, 2, 4),
            grad_valsall[:, :, :, 2 * block : 5 * block].transpose(0, 1, 3, 2, 4),
        ],
        3,
    ).reshape(seqs, per_dev, 3 * block, 2 * hidden)
    rand_grad = (
        jnp.concatenate(
            [
                grad_keysall[:, :, :, 5 * block :].reshape(seqs, per_dev, heads, 3, block, hsize),
                grad_valsall[:, :, :, 5 * block :].reshape(seqs, per_dev, heads, 3, block, hsize),
            ],
            5,
        )
        .reshape(-1, block, 2 * hsize)
        .astype(jnp.bfloat16)
    )
    ext_grad = jnp.zeros((seqs, rows + 2 * block, 2 * hidden), jnp.float32)
    for offset in range(per_dev):
        ext_grad = ext_grad.at[:, offset * block : (offset + 3) * block].add(win_grad[:, offset])
    rims = jnp.concatenate([ext_grad[:, :block], ext_grad[:, rows + block :]], 1)
    returned_rims = with_halo(rims.astype(jnp.bfloat16), (("seq", 1),), block).astype(rims.dtype)
    middle_zero = jnp.zeros((seqs, rows - 2 * block, 2 * hidden), jnp.float32)
    kv_grad = ext_grad[:, block : rows + block] + jnp.concatenate(
        [returned_rims[:, :block], middle_zero, returned_rims[:, 3 * block :]], 1
    )
    sent_back = (
        jnp.zeros((n_dev * capacity, block, 2 * hsize), jnp.bfloat16)
        .at[recv_index]
        .set(rand_grad)
        .reshape(n_dev, capacity, block, 2 * hsize)
    )
    arrived = lax.all_to_all(sent_back, "seq", split_axis=0, concat_axis=0, tiled=True)
    arrived = jnp.where(filled[:, :, None, None], arrived.astype(jnp.float32), 0.0)
    table_grad = (
        jnp.zeros((seqs * per_dev * heads, block, 2 * hsize), jnp.float32)
        .at[send_index.reshape(-1)]
        .add(arrived.reshape(-1, block, 2 * hsize))
    )
    kv_grad = kv_grad + table_grad.reshape(seqs, per_dev, heads, block, 2, hsize).transpose(
        0, 1, 3, 4, 2, 5
    ).reshape(seqs, rows, 2 * hidden)
    kv_grad = kv_grad + jnp.stack(
        [local_dkey.transpose(0, 2, 1, 3), local_dvalue.transpose(0, 2, 1, 3)], 2
    ).reshape(seqs, rows, 2 * hidden)
    end_dquery, end_dkey_all, end_dvalue_all = (
        lax.psum(end_dquery_part.astype(jnp.bfloat16), "seq").astype(jnp.float32),
        lax.psum(end_dkey.astype(jnp.bfloat16), "seq").astype(jnp.float32),
        lax.psum(end_dvalue.astype(jnp.bfloat16), "seq").astype(jnp.float32),
    )
    end_kv = jnp.stack(
        [end_dkey_all.transpose(0, 2, 1, 3), end_dvalue_all.transpose(0, 2, 1, 3)], 2
    ).reshape(seqs, 2 * block, 2 * hidden)
    kv_grad = kv_grad + jnp.concatenate(
        [
            jnp.where(is_first, end_kv[:, :block], 0.0),
            middle_zero,
            jnp.where(is_last, end_kv[:, block:], 0.0),
        ],
        1,
    )
    end_q = end_dquery.transpose(0, 2, 1, 3).reshape(seqs, 2 * block, hidden)
    query_zero = jnp.zeros((seqs, rows - 2 * block, hidden), jnp.float32)
    grad_query = grad_qblocks.transpose(0, 1, 3, 2, 4).reshape(seqs, rows, hidden)
    grad_query = grad_query + jnp.concatenate(
        [
            jnp.where(is_first, end_q[:, :block], 0.0),
            query_zero,
            jnp.where(is_last, end_q[:, block:], 0.0),
        ],
        1,
    )
    query_glow = grad_query.reshape(n_tok, hidden).astype(jnp.bfloat16)
    kv_glow = kv_grad.reshape(n_tok, 2 * hidden).astype(jnp.bfloat16)
    key_glow = kv_glow[:, :hidden]
    value_glow = kv_glow[:, hidden:]
    grad_qbias = jnp.sum(query_glow.astype(jnp.float32), 0)
    grad_vbias = jnp.sum(value_glow.astype(jnp.float32), 0)
    grad_qweight = rows_dot(flat, query_glow)
    grad_kweight = rows_dot(flat, key_glow)
    grad_vweight = rows_dot(flat, value_glow)
    into_tokens = (
        back_dot(query_glow, query_weight)
        + back_dot(key_glow, key_weight)
        + back_dot(value_glow, value_weight)
    )
    input_grad = (grad_resid + head_sum_back(into_tokens)).reshape(seqs, rows, width)
    totals = lax.psum(
        (
            grad_qweight,
            grad_qbias,
            grad_kweight,
            grad_vweight,
            grad_vbias,
            grad_oweight,
            grad_obias,
            grad_attngain,
            grad_attnshift,
            grad_upweight,
            grad_upbias,
            grad_downweight,
            grad_downbias,
            grad_ffngain,
            grad_ffnshift,
        ),
        "seq",
    )
    return (
        layer_output,
        input_grad,
        totals[0],
        totals[1],
        totals[2],
        totals[3],
        totals[4],
        totals[5],
        totals[6],
        totals[7],
        totals[8],
        totals[9],
        totals[10],
        totals[11],
        totals[12],
        totals[13],
        totals[14],
    )


HALF_ROOT = 0.7071067811865476
PDF_SCALE = 0.3989422804014327


MESH = pl.DeviceIdType.MESH


def place():
    me, t = lax.axis_index("seq"), lax.axis_index("tp")
    side, core = lax.div(t, 2), lax.rem(t, 2)
    return me, t, side, core


def tp_peer(side, core, bits):
    there = 1 - side if bits & 2 else side
    return there * 2 + (1 - core if bits & 1 else core)


def greet(peers):
    barrier = pltpu.get_barrier_semaphore()
    for peer in peers:
        pl.semaphore_signal(barrier, inc=1, device_id=peer, device_id_type=MESH)
    pl.semaphore_wait(barrier, len(peers))


def remote(src, dst, sends, recvs, at, peer):
    return pltpu.make_async_remote_copy(
        src_ref=src,
        dst_ref=dst,
        send_sem=sends.at[at],
        recv_sem=recvs.at[at],
        device_id=peer,
        device_id_type=MESH,
    )


class Piece:
    def __init__(self, at, bit, own, held, spots, sems):
        me, t, side, core = spots
        self.at, self.own, self.far = at, own, partial(held, 2 + core)
        mate, self.half = flip(me, bit)
        self.mate = (mate, t)
        self.near, self.across = (me, tp_peer(side, core, 1)), (me, tp_peer(side, core, 2))
        self.sems = sems
        self.then = []

    def move(self, n):
        h = 1 - self.half if n == 3 else self.half
        src = self.own(h) if n == 0 else self.far(h)
        peer = (self.across, self.mate, self.near, self.near)[n]
        return remote(src, self.far(h), *self.sems, (self.at, n), peer)

    def start(self):
        self.move(0).start()

    def pass_on(self):
        self.move(0).wait_recv()
        for piece in self.then:
            piece.start()
        self.move(1).start()
        self.move(2).start()

    def pass_side(self):
        self.move(1).wait_recv()
        self.move(3).start()

    def arrive(self):
        self.move(2).wait_recv()
        self.move(3).wait_recv()

    def sent(self):
        for n in range(4):
            self.move(n).wait_send()


def enter_kernel(
    n_dev, tok, cot, rand, wq, wk, wv, qb, vb, ub, wo, up, down,
    x, q, ko, kf, vo, vf, attn, lse, ids, ubs, wt_out, cot_out, wo_out, up_out, down_out,
    wt, qbs, vbs, ids_for, own_wo, own_up, own_down,
    tok_send, tok_recv, cot_send, cot_recv, p_send, p_recv, o_send, o_recv, s_send, s_recv, kv_send, kv_recv, local,
):
    spots = me, t, side, core = place()
    near = (me, tp_peer(side, core, 1))
    hidden, width = wq.shape
    units = down.shape[0]
    span = x.shape[0]
    heads = hidden // HD
    pairs = width // (2 * HD)
    part = hidden // 2
    n_part = units // 2 // part
    own_buf = (own_wo, own_up, own_down)

    holds = [(w, lambda j, m=m: wt.at[m, j]) for m, w in ((1, wk), (2, wv), (0, wq))]
    holds += [
        (wo, lambda j: wo_out.at[pl.ds(j * hidden, hidden), :]),
        (up, lambda j: up_out.at[:, pl.ds(j * units, units)]),
        (down, lambda j: down_out.at[pl.ds(j * units, units), :]),
    ]
    pieces = []
    for n, (ref, block) in enumerate(holds):
        for i in range(1 if n < 4 else n_part):
            count = 1 if n < 4 else n_part

            def rows(r, h, i=i, count=count):
                return r.at[pl.ds((h * count + i) * part, part), :]

            at = len(pieces)
            pieces.append(
                Piece(
                    at, (1, 2)[at % 2],
                    lambda h, ref=ref, rows=rows: rows(ref, h),
                    lambda j, h, block=block, rows=rows: rows(block(j), h),
                    spots, (p_send, p_recv),
                )
            )

    ahead = 4
    for piece, later in zip(pieces, pieces[ahead:]):
        piece.then = [later]

    def own_near(n):
        return remote(holds[n][0], holds[n][1](core), o_send, o_recv, n, near)

    def own_here(n):
        src = holds[n][0] if n < 3 else own_buf[n - 3]
        return pltpu.make_async_copy(src, holds[n][1](core), local.at[n])

    def own_in(n):
        return pltpu.make_async_copy(holds[n][0], own_buf[n - 3], local.at[6 + n])

    def spread(src, dst, sends, recvs):
        return [
            remote(
                src.at[2 * lax.rem(me + k, n_dev) + side, pl.ds(core * BLOCK, BLOCK), :],
                dst.at[pl.ds(k * BLOCK, BLOCK), :],
                sends, recvs, k - 1, (lax.rem(me + k, n_dev), t),
            )
            for k in range(1, n_dev)
        ]

    def kept(n):
        src, dst = ((tok, x), (cot, cot_out))[n]
        return pltpu.make_async_copy(
            src.at[2 * me + side, pl.ds(core * BLOCK, BLOCK), :], dst.at[pl.ds(0, BLOCK), :], local.at[12 + n]
        )

    def shared(bits, which=(0, 1, 2, 3)):
        slot = (bits & 2) + core
        to = tp_peer(side, core, bits)
        moves = (
            (qb, qbs.at[slot]), (vb, vbs.at[slot]), (ub, ubs.at[slot]),
            (ids_for.at[to], ids.at[pl.ds(slot * heads, heads)]),
        )
        return [
            remote(*moves[n], s_send, s_recv, (bits - 1, n), (me, to)) for n in which
        ]

    greet(all_peers(n_dev, *spots) + [(me, tp_peer(side, core, 3))])
    for move in spread(tok, x, tok_send, tok_recv):
        move.start()
    for piece in pieces[:ahead]:
        piece.start()
    kept(0).start()
    for n in range(3):
        own_near(n).start()
        own_here(n).start()
    qbs[core], vbs[core], ubs[core] = qb[...], vb[...], ub[...]
    for bits in (1, 2, 3):
        for move in shared(bits, (0, 1, 2)):
            move.start()
    for n in range(3, 6):
        own_in(n).start()

    lane = lax.broadcasted_iota(jnp.int32, (1, span), 1)
    for y in range(2):
        for c in range(2):
            block = 2 * lax.rem(me - lane // BLOCK + n_dev, n_dev) + c
            for h in range(heads):
                for r in range(3):
                    line = rand[h, r, pl.ds(2 * me + y, 1), :]
                    row = jnp.zeros((1, span), jnp.int32)
                    for b in range(c, 2 * n_dev, 2):
                        row = jnp.where(block == b, line[:, b : b + 1], row)
                    ids_for[2 * y + c, h, r : r + 1, :] = row
    ids[pl.ds(core * heads, heads)] = ids_for[t]
    for bits in (1, 2, 3):
        shared(bits, (3,))[0].start()

    def advance(n):
        pieces[n].pass_on()
        if n:
            pieces[n - 1].pass_side()

    for n in range(4):
        advance(n)
    for move in spread(tok, x, tok_send, tok_recv):
        move.wait_recv()
    kept(0).wait()
    for move in spread(cot, cot_out, cot_send, cot_recv):
        move.start()
    kept(1).start()
    for n in range(3, 6):
        own_near(n).start()
        own_in(n).wait()
        own_here(n).start()
    for bits in (1, 2, 3):
        for move in shared(bits):
            move.wait_recv()

    def bias_of(ref):
        return jnp.concatenate([ref[j] for j in range(4)], 1)

    def project(n, m):
        own_near(n).wait_recv()
        own_here(n).wait()
        pieces[n].arrive()
        return back_dot(x[...], wt[m].reshape(width, width))

    def swap_kv(n):
        src, dst = ((ko, kf), (vo, vf))[n]
        return remote(src, dst, kv_send, kv_recv, n, near)

    ko[...] = project(0, 1).astype(jnp.bfloat16)
    swap_kv(0).start()
    vo[...] = (project(1, 2) + bias_of(vbs)).astype(jnp.bfloat16)
    swap_kv(1).start()
    advance(4)
    q[...] = (project(2, 0) + bias_of(qbs)).astype(jnp.bfloat16)
    keep = pltpu.make_async_copy(wt, wt_out, local.at[14])
    keep.start()
    advance(5)
    swap_kv(0).wait_recv()
    swap_kv(1).wait_recv()

    def pair(p, carry):
        lanes = pl.ds(pl.multiple_of(p * 2 * HD, 2 * HD), 2 * HD)
        attend_pair(n_dev, p, lanes, q, ko, kf, vo, vf, ids, attn, lse, me, core)
        for k in range(3):

            @pl.when(p == 2 * k + 1)
            def _():
                advance(6 + k)

        return carry

    lax.fori_loop(0, pairs, pair, 0)
    for n in range(9, len(pieces)):
        advance(n)
    pieces[-1].pass_side()
    for n in range(3, len(pieces)):
        pieces[n].arrive()
    for move in spread(cot, cot_out, cot_send, cot_recv):
        move.wait()
    kept(1).wait()
    keep.wait()
    for move in spread(tok, x, tok_send, tok_recv):
        move.wait_send()
    for piece in pieces:
        piece.sent()
    for n in range(6):
        own_near(n).wait_send()
        if n > 2:
            own_near(n).wait_recv()
            own_here(n).wait()
    for bits in (1, 2, 3):
        for move in shared(bits):
            move.wait_send()
    for n in range(2):
        swap_kv(n).wait_send()


def enter(tok, cot, rand, wq, wk, wv, qb, vb, ub, wo, up, down, n_dev):
    hidden, width = wq.shape
    units = down.shape[0]
    span = n_dev * BLOCK
    heads = hidden // HD
    pieces = 4 + 2 * (units // hidden)
    vmem = pl.BlockSpec(memory_space=pltpu.VMEM)
    hbm = pl.BlockSpec(memory_space=pl.ANY)
    shape = lambda dtype, *dims: jax.ShapeDtypeStruct(dims, dtype)
    low = partial(shape, jnp.bfloat16)
    dma = pltpu.SemaphoreType.DMA
    return pl.pallas_call(
        partial(enter_kernel, n_dev),
        in_specs=[hbm, hbm, vmem] + [hbm] * 3 + [vmem] * 3 + [hbm] * 3,
        out_specs=[vmem] * 10 + [hbm] * 5,
        out_shape=[low(span, width)] * 7
        + [
            shape(jnp.float32, 2 * heads, 2, span),
            shape(jnp.int32, 4 * heads, 3, span),
            shape(jnp.float32, 4, 1, units),
            low(3, 4, hidden, width),
            low(span, width),
            low(width, width),
            low(width, 4 * units),
            low(4 * units, width),
        ],
        scratch_shapes=[
            pltpu.VMEM((3, 4, hidden, width), jnp.bfloat16),
            pltpu.VMEM((4, 1, hidden), jnp.float32),
            pltpu.VMEM((4, 1, hidden), jnp.float32),
            pltpu.VMEM((4, heads, 3, span), jnp.int32),
            pltpu.VMEM(wo.shape, jnp.bfloat16),
            pltpu.VMEM(up.shape, jnp.bfloat16),
            pltpu.VMEM(down.shape, jnp.bfloat16),
            dma((n_dev - 1,)),
            dma((n_dev - 1,)),
            dma((n_dev - 1,)),
            dma((n_dev - 1,)),
            dma((pieces, 4)),
            dma((pieces, 4)),
            dma((6,)),
            dma((6,)),
            dma((3, 4)),
            dma((3, 4)),
            dma((2,)),
            dma((2,)),
            dma((15,)),
        ],
        compiler_params=pltpu.CompilerParams(
            collective_id=0, has_side_effects=True, vmem_limit_bytes=56 * 2**20
        ),
    )(tok, cot, rand, wq, wk, wv, qb, vb, ub, wo, up, down)


def list_bias(ids_ref, h, key_shift, me, core, n_dev, span):
    n_blocks = 2 * n_dev
    row = lax.broadcasted_iota(jnp.int32, (n_dev, span), 0)
    lane = lax.broadcasted_iota(jnp.int32, (n_dev, span), 1)
    wrap = lambda i: lax.rem(me - i + n_dev, n_dev)
    k = 2 * wrap(row) + (1 - core if key_shift else core)
    b = 2 * wrap(lane // BLOCK) + core
    one = lambda flag: jnp.where(flag, 1.0, 0.0)
    count = (
        one(k == 0)
        + one(k == n_blocks - 1)
        + one((k == b - 1) & (b != 1))
        + one(k == b)
        + one((k == b + 1) & (b != n_blocks - 2))
    )
    for r in range(3):
        count = count + one(ids_ref[h, r : r + 1, :] == k)
    count = jnp.where((b == 0) | (b == n_blocks - 1), 1.0, count)
    return jnp.where(count > 0.5, jnp.log(jnp.maximum(count, 1.0)), masked_score)


def attend_pair(n_dev, p, lanes, q_ref, ko, kf, vo, vf, ids, attn, lse, me, core):
    span = q_ref.shape[0]
    blocks = span // BLOCK
    lane = lax.broadcasted_iota(jnp.int32, (1, 2 * HD), 1) // HD
    q = q_ref[:, lanes]
    keys = (ko[:, lanes], kf[:, lanes])
    values = (vo[:, lanes].T, vf[:, lanes].T)
    outs = []
    for h in range(2):
        qh = (jnp.where(lane == h, q, 0.0) * 0.125).astype(jnp.bfloat16)
        scores = []
        for far in range(2):
            bias = list_bias(ids, 2 * p + h, far == 1, me, core, n_dev, span)
            raw = back_dot(keys[far], qh).reshape(blocks, BLOCK, span)
            scores.append((raw + bias[:, None, :]).reshape(span, span))
        top = jnp.maximum(*(jnp.max(s, 0, keepdims=True) for s in scores))
        expo = [jnp.exp(s - top) for s in scores]
        total = sum(jnp.sum(e, 0, keepdims=True) for e in expo)
        rows = slice(h * HD, (h + 1) * HD)
        acc = sum(plain_dot(v[rows], e.astype(jnp.bfloat16)) for v, e in zip(values, expo))
        outs.append(acc / total)
        lse[p, h : h + 1, :] = top + jnp.log(total)
    attn[:, lanes] = jnp.concatenate(outs, 0).T.astype(jnp.bfloat16)


def flip(index, bit):
    value = lax.rem(lax.div(index, bit), 2)
    return index + bit - 2 * bit * value, value


class Reduction:
    def __init__(self, parts, mine, spots, bufs, sems):
        self.parts, self.mine = parts, mine
        self.jobs, self.ahead = [], 3
        self.me, self.t, self.side, self.core = spots
        self.b0, self.b1, self.acc, self.halves, self.got, self.f = bufs
        self.send, self.recv, self.send0, self.recv0 = sems
        self.near = (self.me, tp_peer(self.side, self.core, 1))
        self.across = (self.me, tp_peer(self.side, self.core, 2))
        self.mates = []
        self.bits = []
        for bit in (1, 2, 4):
            mate, value = flip(self.me, bit)
            self.mates.append((mate, self.t))
            self.bits.append(value)

    def span(self, ref, start, size):
        return ref.at[pl.ds(pl.multiple_of(start, 16), size), :]

    def rows(self, depth):
        start, size, inner = 0, self.f.shape[1], 0
        for level in range(depth):
            size //= 2
            start = start + self.bits[level] * size
            inner = inner + (self.bits[level] * size if level else 0)
        return start, inner, size

    def first(self, ch):
        moves = []
        for y in range(2):
            at = 0
            for ref in self.parts(ch, 2 * y + 1 - self.core):
                rows = pl.ds(at, ref.shape[0])
                at += ref.shape[0]
                n = len(moves)
                moves.append(
                    remote(ref, self.b0.at[ch, y, rows, :], self.send0, self.recv0, (ch, n), self.near)
                )
        return moves

    def over_y(self, ch):
        return remote(self.mine(ch, 1), self.b1.at[ch], self.send, self.recv, (ch, 0), self.across)

    def next_y(self, job):
        if job + self.ahead < len(self.jobs):
            self.jobs[job + self.ahead]().start()

    def halving(self, ch, level):
        size = self.rows(level + 1)[2]
        return remote(
            self.halves.at[ch, pl.ds(size, size), :],
            self.got.at[ch, pl.ds(size, size), :],
            self.send, self.recv, (ch, 1 + level), self.mates[level],
        )

    def gather(self, ch, level):
        start, _, size = self.rows(level + 1)
        held = self.span(self.f.at[ch], start, size)
        return remote(held, held, self.send, self.recv, (ch, 4 + level), self.mates[level])

    def stage(self, ch, s):
        full = jnp.float32
        if s == 0:
            for move in self.first(ch):
                move.start()
        elif s == 1:
            for move in self.first(ch):
                move.wait_recv()
            out = self.mine(ch, 1)
            out[...] = (out[...].astype(full) + self.b0[ch, 1].astype(full)).astype(jnp.bfloat16)
            if ch < self.ahead:
                self.over_y(ch).start()
        elif s == 2:
            self.over_y(ch).wait_recv()
            self.next_y(ch)
            size = self.rows(1)[2]

            def total(start):
                terms = (self.mine(ch, 0), self.b0.at[ch, 0], self.b1.at[ch])
                one, two, three = (self.span(ref, start, size)[...].astype(full) for ref in terms)
                return one + two + three

            self.halves[ch, pl.ds(size, size), :] = total((1 - self.bits[0]) * size).astype(jnp.bfloat16)
            self.halving(ch, 0).start()
            self.acc[ch] = total(self.bits[0] * size)
        elif s <= 5:
            level = s - 3
            _, inner, size = self.rows(level + 1)
            self.halving(ch, level).wait_recv()
            total = self.span(self.acc.at[ch], inner, size)[...] + self.got[ch, pl.ds(size, size), :].astype(full)
            if s == 5:
                self.span(self.f.at[ch], self.rows(3)[0], size)[...] = total.astype(jnp.bfloat16)
                self.gather(ch, 2).start()
            else:
                self.span(self.acc.at[ch], inner, size)[...] = total
                small = size // 2
                other = self.span(self.acc.at[ch], inner + (1 - self.bits[level + 1]) * small, small)
                self.halves[ch, pl.ds(small, small), :] = other[...].astype(jnp.bfloat16)
                self.halving(ch, level + 1).start()
        elif s <= 7:
            self.gather(ch, 8 - s).wait_recv()
            self.gather(ch, 7 - s).start()
        else:
            self.gather(ch, 0).wait_recv()

    def finish(self, ch):
        for move in self.first(ch):
            move.wait_send()
        self.over_y(ch).wait_send()
        for level in range(3):
            self.halving(ch, level).wait_send()
            self.gather(ch, level).wait_send()


class Return:
    def __init__(self, at, n_dev, src, dst, spots, sems):
        self.at, self.n_dev, self.src, self.dst = at, n_dev, src, dst
        self.me, self.t, self.side, self.core = spots
        self.send, self.recv, self.local = sems
        self.near = (self.me, tp_peer(self.side, self.core, 1))
        self.across = (self.me, tp_peer(self.side, self.core, 2))

    def block(self, s, side):
        return self.dst.at[s, side, pl.ds(self.core * BLOCK, BLOCK), :]

    def keep(self):
        return pltpu.make_async_copy(
            self.src.at[pl.ds(0, BLOCK), :], self.block(self.me, self.side), self.local.at[self.at]
        )

    def out(self, k):
        to = lax.rem(self.me - k + self.n_dev, self.n_dev)
        return remote(
            self.src.at[pl.ds(k * BLOCK, BLOCK), :], self.block(self.me, self.side),
            self.send, self.recv, (self.at, k - 1), (to, self.t),
        )

    def pass_on(self, n):
        side = 1 - self.side if n == 2 else self.side
        held = self.dst.at[:, side, pl.ds(self.core * BLOCK, BLOCK), :]
        peer = self.across if n == 0 else self.near
        return remote(held, held, self.send, self.recv, (self.at, self.n_dev - 1 + n), peer)

    def stage(self, s):
        if s == 0:
            self.keep().start()
            for k in range(1, self.n_dev):
                self.out(k).start()
        elif s == 1:
            self.keep().wait()
            for k in range(1, self.n_dev):
                self.out(k).wait_recv()
            self.pass_on(1).start()
        elif s == 2:
            self.pass_on(0).wait_recv()
            self.then()
            self.pass_on(2).start()
        else:
            for k in range(1, self.n_dev):
                self.out(k).wait_send()
            self.pass_on(0).wait_send()
            self.pass_on(1).wait()
            self.pass_on(2).wait()


class SmallSum:
    def __init__(self, out, came, spots, sems):
        self.out, self.came = out, came
        me, t, side, core = spots
        self.send, self.recv = sems
        self.peers = [(me, tp_peer(side, core, 1)), (me, tp_peer(side, core, 2))]
        self.peers += [(flip(me, bit)[0], t) for bit in (1, 2, 4)]

    def move(self, n):
        held = self.out.at[n]
        return remote(held, self.came.at[n], self.send, self.recv, n, self.peers[n])

    def stage(self, n):
        if n:
            self.move(n - 1).wait_recv()
            self.out[n] = self.out[n - 1] + self.came[n - 1]
        if n < len(self.peers):
            self.move(n).start()

    def finish(self):
        for n in range(len(self.peers)):
            self.move(n).wait_send()


def all_peers(n_dev, me, t, side, core):
    return [(lax.rem(me + k, n_dev), t) for k in range(1, n_dev)] + [
        (me, tp_peer(side, core, bits)) for bits in (1, 2)
    ]


def tail_kernel(
    n_dev, q, ko, kf, vo, vf, ids, lse, attn, gat, x, gres, early, gd, gu, go, low, wt_hbm,
    f, out, iout, total,
    load, p2, wt, b0, b1, acc, halves, got, came, dq, own, far, far_in, ig,
    send, recv, send0, recv0, local, x_send, x_recv, r_send, r_recv, r_local, s_send, s_recv,
):
    spots = me, t, side, core = place()
    units, hidden = gd.shape[0] // 4, go.shape[0] // 4
    span, width = q.shape
    rows = f.shape[1]
    n_down = units // rows
    n_ffn = n_down + gu.shape[0] // rows
    count = f.shape[0]
    pairs = width // (2 * HD)
    near = (me, tp_peer(side, core, 1))

    def parts(ch, block):
        if ch < n_down:
            return [gd.at[pl.ds(block * units + ch * rows, rows), :]]
        if ch < n_ffn:
            return [gu.at[pl.ds((ch - n_down) * rows, rows), pl.ds(block * units, units)]]
        return [p2.at[block, pl.ds((ch - n_ffn) * rows, rows), :]]

    def mine(ch, y):
        return load.at[ch, y] if ch < n_ffn else parts(ch, 2 * y + core)[0]

    red = Reduction(parts, mine, spots, (b0, b1, acc, halves, got, f), (send, recv, send0, recv0))
    back = [
        Return(n, n_dev, src, dst, spots, (r_send, r_recv, r_local))
        for n, (src, dst) in enumerate(((low, out), (ig, iout)))
    ]
    tiny = SmallSum(total, came, spots, (s_send, s_recv))

    def loads(ch):
        return [
            pltpu.make_async_copy(parts(ch, 2 * y + core)[0], mine(ch, y), local.at[2 * ch + y])
            for y in range(2)
        ]

    def others():
        pieces = [(wt_hbm, wt)] + [
            (go.at[pl.ds(j * hidden, hidden), :], p2.at[j, pl.ds(0, hidden), :]) for j in range(4)
        ]
        return [
            pltpu.make_async_copy(a, b, local.at[2 * n_ffn + n]) for n, (a, b) in enumerate(pieces)
        ]

    def swap_far(p, n):
        return remote(far.at[n, p], far_in.at[n, p], x_send, x_recv, (p, n), near)

    red.jobs = [partial(red.over_y, ch) for ch in range(count)]
    red.jobs += [partial(b.pass_on, 0) for b in back]
    back[0].then, back[1].then = partial(red.next_y, count), partial(red.next_y, count + 1)

    def begin(ch):
        red.stage(ch, 0)
        for move in loads(ch):
            move.start()

    def second(ch):
        for move in loads(ch):
            move.wait()
        red.stage(ch, 1)

    greet(all_peers(n_dev, *spots))
    for ch in range(n_ffn // 2):
        begin(ch)
    back[0].stage(0)
    for move in others():
        move.start()

    def pair(p, carry):
        lanes = pl.ds(pl.multiple_of(p * 2 * HD, 2 * HD), 2 * HD)
        attend_pair_back(n_dev, p, lanes, q, ko, kf, vo, vf, ids, lse, attn, gat, dq, own, far, me, core)
        for n in range(2):
            swap_far(p, n).start()
        for k in range(2):

            @pl.when(p == k)
            def _():
                for ch in range(k * n_ffn // 2, (k + 1) * n_ffn // 2):
                    second(ch)
                for ch in range(n_ffn // 2, (1 - k) * n_ffn):
                    begin(ch)

        return carry

    lax.fori_loop(0, pairs, pair, 0)

    for p in range(pairs):
        for n in range(2):
            swap_far(p, n).wait_recv()

    def joined_low(n):
        cat = jnp.concatenate([far_in[n, p] for p in range(pairs)], 1)
        return (own[n] + cat.astype(jnp.float32)).astype(jnp.bfloat16)

    def weight_grad(low_grad, at):
        grad = plain_dot(low_grad.T, x[...]).astype(jnp.bfloat16)
        for j in range(4):
            p2[j, pl.ds(at * hidden, hidden), :] = grad[j * hidden : (j + 1) * hidden]

    def column_sum(low_grad):
        sums = jnp.sum(low_grad.astype(jnp.float32), 0, keepdims=True)
        turned = jnp.concatenate([sums[:, width // 2 :], sums[:, : width // 2]], 1)
        return jnp.where(side == 0, sums, turned)

    red.stage(0, 2)
    weight_grad(dq[...], 1)
    for move in others():
        move.wait()
    red.stage(n_ffn, 0)
    dk = joined_low(0)
    weight_grad(dk, 2)
    red.stage(n_ffn + 1, 0)
    red.stage(1, 2)
    dv = joined_low(1)
    weight_grad(dv, 3)
    for ch in range(n_ffn + 2, count):
        red.stage(ch, 0)
    red.stage(0, 3)
    total[0] = early[...]
    total[0, 0:1, :] = column_sum(dq[...])
    total[0, 1:2, :] = column_sum(dv)
    tiny.stage(0)
    matrix = lambda m: wt[m].reshape(width, width)
    into = gres[...] + plain_dot(dq[...], matrix(0))
    into = into + plain_dot(dk, matrix(1))
    ig[...] = (into + plain_dot(dv, matrix(2))).astype(jnp.bfloat16)
    back[1].stage(0)
    for ch in range(n_ffn, count):
        red.stage(ch, 1)
    back[0].stage(1)

    events = []
    done = [(0, 2), (0, 3), (1, 2)]
    for ch in range(count):
        for s in range(2, 9):
            if (ch, s) not in done:
                events.append((10 + 8 * (ch + 1) + (0, 10, 18, 26, 34, 42, 51)[s - 2], red, (ch, s)))
    events += [(33 + 7 * n, tiny, (n,)) for n in range(1, 6)]
    events += [(58, back[1], (1,)), (106, back[0], (2,)), (123, back[1], (2,))]
    for _, who, what in sorted(events, key=lambda e: e[0]):
        who.stage(*what)
    for b in back:
        b.stage(3)
    for ch in range(count):
        red.finish(ch)
    tiny.finish()
    for p in range(pairs):
        for n in range(2):
            swap_far(p, n).wait_send()


def attend_pair_back(n_dev, p, lanes, q_ref, ko, kf, vo, vf, ids, lse_ref, attn, gat, dq, own, far, me, core):
    span = q_ref.shape[0]
    blocks = span // BLOCK
    lane = lax.broadcasted_iota(jnp.int32, (1, 2 * HD), 1) // HD
    q, g = q_ref[:, lanes], gat[:, lanes]
    weighted = (attn[:, lanes].astype(jnp.float32) * g.astype(jnp.float32)).T
    parts = ((ko[:, lanes], vo[:, lanes]), (kf[:, lanes], vf[:, lanes]))
    k_ts = [k.T for k, _ in parts]
    dks = [None, None]
    dvs = [None, None]
    dq_ts = []
    for h in range(2):
        rows = slice(h * HD, (h + 1) * HD)
        qh = (jnp.where(lane == h, q, 0.0) * 0.125).astype(jnp.bfloat16)
        gh = jnp.where(lane == h, g, 0.0).astype(jnp.bfloat16)
        delta = jnp.sum(weighted[rows], 0, keepdims=True)
        lse = lse_ref[p, h : h + 1, :]
        dq_t = None
        for at, (k, v) in enumerate(parts):
            bias = list_bias(ids, 2 * p + h, at == 1, me, core, n_dev, span)
            raw = back_dot(k, qh).reshape(blocks, BLOCK, span)
            raw = (raw + bias[:, None, :]).reshape(span, span)
            prob = jnp.exp(raw - lse)
            dprob = back_dot(v, gh)
            dscore = (prob * (dprob - delta)).astype(jnp.bfloat16)
            dv = plain_dot(prob.astype(jnp.bfloat16), gh)
            dk = plain_dot(dscore, qh)
            dvs[at] = dv if dvs[at] is None else dvs[at] + dv
            dks[at] = dk if dks[at] is None else dks[at] + dk
            piece = plain_dot(k_ts[at][rows], dscore)
            dq_t = piece if dq_t is None else dq_t + piece
        dq_ts.append(dq_t * 0.125)
    dq[:, lanes] = jnp.concatenate(dq_ts, 0).T.astype(jnp.bfloat16)
    for n, grads in enumerate((dks, dvs)):
        own[n, :, lanes] = grads[0]
        far[n, p] = grads[1].astype(jnp.bfloat16)


def tail(q, ko, kf, vo, vf, ids, lse, attn, gat, x, gres, early, gd, gu, go, low, wt, n_dev):
    span, width = q.shape
    hidden = go.shape[0] // 4
    rows = 256
    n_ffn = (gd.shape[0] // 4 + gu.shape[0]) // rows
    count = n_ffn + go.shape[0] // rows
    pairs = width // (2 * HD)
    vmem = pl.BlockSpec(memory_space=pltpu.VMEM)
    hbm = pl.BlockSpec(memory_space=pl.ANY)
    dma = pltpu.SemaphoreType.DMA
    landed = jax.ShapeDtypeStruct((n_dev, 2, 2 * BLOCK, width), jnp.bfloat16)
    low_buf = lambda *shape: pltpu.VMEM(shape + (width,), jnp.bfloat16)
    pair_buf = pltpu.VMEM((2, pairs, span, 2 * HD), jnp.bfloat16)
    return pl.pallas_call(
        partial(tail_kernel, n_dev),
        in_specs=[vmem] * 12 + [hbm] * 5,
        out_specs=[vmem, hbm, hbm, vmem],
        out_shape=[
            jax.ShapeDtypeStruct((count, rows, width), jnp.bfloat16),
            landed,
            landed,
            jax.ShapeDtypeStruct((6,) + early.shape, jnp.float32),
        ],
        scratch_shapes=[
            low_buf(n_ffn, 2, rows),
            low_buf(4, 4 * hidden),
            pltpu.VMEM(wt.shape, jnp.bfloat16),
            low_buf(count, 2, rows),
            low_buf(count, rows),
            pltpu.VMEM((count, rows // 2, width), jnp.float32),
            low_buf(count, rows),
            low_buf(count, rows),
            pltpu.VMEM((5,) + early.shape, jnp.float32),
            low_buf(span),
            pltpu.VMEM((2, span, width), jnp.float32),
            pair_buf,
            pair_buf,
            low_buf(span),
            dma((count, 7)),
            dma((count, 7)),
            dma((count, 2)),
            dma((count, 2)),
            dma((2 * n_ffn + 5,)),
            dma((pairs, 2)),
            dma((pairs, 2)),
            dma((2, n_dev + 2)),
            dma((2, n_dev + 2)),
            dma((2,)),
            dma((5,)),
            dma((5,)),
        ],
        compiler_params=pltpu.CompilerParams(
            collective_id=2, has_side_effects=True, vmem_limit_bytes=60 * 2**20
        ),
    )(q, ko, kf, vo, vf, ids, lse, attn, gat, x, gres, early, gd, gu, go, low, wt)


def norm_parts(resid):
    centre = resid - jnp.mean(resid, -1, keepdims=True)
    inverse = lax.rsqrt(jnp.mean(centre * centre, -1, keepdims=True) + norm_eps)
    return centre * inverse, inverse


def norm_back(grad, unit, inverse, gain):
    scaled = grad * gain
    pull = scaled - jnp.mean(scaled, -1, keepdims=True)
    pull = pull - unit * jnp.mean(scaled * unit, -1, keepdims=True)
    return pull * inverse, jnp.sum(grad * unit, 0), jnp.sum(grad, 0)


def whole_sequences(
    tokens,
    rand_blocks,
    query_weight,
    query_bias,
    key_weight,
    value_weight,
    value_bias,
    output_weight,
    output_bias,
    attn_gain,
    attn_shift,
    up_weight,
    up_bias,
    down_weight,
    down_bias,
    ffn_gain,
    ffn_shift,
    cotangent,
):
    seqs, rows, width = tokens.shape
    n_dev = lax.axis_size("seq")
    me = lax.axis_index("seq")
    t = lax.axis_index("tp")
    side, core = t // 2, t % 2
    n_blocks = rows // BLOCK * n_dev
    hidden = query_weight.shape[1]
    units = up_weight.shape[1]
    span = n_dev * BLOCK

    (
        x, q, k_own, k_far, v_own, v_far, attn_low, lse, ids, u_bias, wt, cot, wo, w_up, w_down,
    ) = enter(
        tokens, cotangent, rand_blocks.transpose(2, 3, 0, 1), query_weight.T, key_weight.T, value_weight.T,
        query_bias[None], value_bias[None], up_bias[None], output_weight, up_weight, down_weight, n_dev,
    )
    u_bias = u_bias.reshape(4 * units)
    branch = plain_dot(attn_low, wo) + output_bias
    unit_one, inverse_one = norm_parts(x.astype(jnp.float32) + branch)
    normed = unit_one * attn_gain + attn_shift
    normed_low = normed.astype(jnp.bfloat16)
    pre_act = plain_dot(normed_low, w_up) + u_bias
    cdf = 0.5 * (1.0 + lax.erf(pre_act * HALF_ROOT))
    act_low = (pre_act * cdf).astype(jnp.bfloat16)
    slope = (cdf + pre_act * (PDF_SCALE * jnp.exp(-0.5 * pre_act * pre_act))).astype(jnp.bfloat16)
    ffn = plain_dot(act_low, w_down) + down_bias
    unit_two, inverse_two = norm_parts(normed + ffn)
    out_low = (unit_two * ffn_gain + ffn_shift).astype(jnp.bfloat16)

    g_resid2, grad_ffngain, grad_ffnshift = norm_back(
        cot.astype(jnp.float32), unit_two, inverse_two, ffn_gain
    )
    g_ffn = g_resid2.astype(jnp.bfloat16)
    grad_downbias = jnp.sum(g_ffn.astype(jnp.float32), 0)
    grad_down = rows_dot(act_low, g_ffn).astype(jnp.bfloat16)
    g_pre = (back_dot(g_ffn, w_down) * slope.astype(jnp.float32)).astype(jnp.bfloat16)
    grad_upbias = jnp.sum(g_pre.astype(jnp.float32), 0)
    grad_up = rows_dot(normed_low, g_pre).astype(jnp.bfloat16)
    g_normed = g_resid2 + back_dot(g_pre, w_up)
    g_resid, grad_attngain, grad_attnshift = norm_back(g_normed, unit_one, inverse_one, attn_gain)
    g_branch = g_resid.astype(jnp.bfloat16)
    grad_obias = jnp.sum(g_branch.astype(jnp.float32), 0)
    grad_o = rows_dot(attn_low, g_branch).astype(jnp.bfloat16)
    g_attn = back_dot(g_branch, wo).astype(jnp.bfloat16)

    ups = grad_upbias.reshape(2, 2, units)
    ups = jnp.where(side == 0, ups, ups[::-1]).reshape(4, width)
    late = jnp.zeros((2, width), jnp.float32)
    lines = [grad_obias, grad_attngain, grad_attnshift, grad_downbias, grad_ffngain, grad_ffnshift]
    early = jnp.concatenate([late, ups, jnp.stack(lines), late, late], 0)
    sums, layer_output, input_out, small = tail(
        q, k_own, k_far, v_own, v_far, ids, lse, attn_low, g_attn, x, g_resid, early,
        grad_down, grad_up, grad_o, out_low, wt, n_dev,
    )
    small = small[5]

    def share(first, size):
        whole = small[first : first + 4 * size // width].reshape(4, size)
        return lax.dynamic_index_in_dim(whole, t, 0, False)

    sums = sums.astype(jnp.float32)
    half = units // sums.shape[1]
    g_down = sums[:half].reshape(units, width)
    g_up = sums[half : half + width // sums.shape[1]].reshape(width, units)
    rest = sums[half + width // sums.shape[1] :].reshape(4, hidden, width)
    g_o, g_q, g_k, g_v = rest
    return (
        layer_output.reshape(seqs, rows, width),
        input_out.astype(jnp.float32).reshape(seqs, rows, width),
        g_q.T,
        share(0, hidden),
        g_k.T,
        g_v.T,
        share(1, hidden),
        g_o,
        small[6],
        small[7],
        small[8],
        g_up,
        share(2, units),
        g_down,
        small[9],
        small[10],
        small[11],
    )


def per_device(tokens, *rest):
    seqs, rows, _ = tokens.shape
    n_dev = lax.axis_size("seq")
    if lax.axis_size("tp") == 4 and n_dev == 8 and seqs == 2 * n_dev and rows == 2 * BLOCK:
        return whole_sequences(tokens, *rest)
    return split_sequences(tokens, *rest)


def solution(mesh):
    placed = (
        P(None, "seq", None),
        P(None, None, "tp", None),
        P(None, "tp"),
        P("tp"),
        P(None, "tp"),
        P(None, "tp"),
        P("tp"),
        P("tp", None),
        P(),
        P(),
        P(),
        P(None, "tp"),
        P("tp"),
        P("tp", None),
        P(),
        P(),
        P(),
        P(None, "seq", None),
    )
    return jax.shard_map(
        per_device,
        mesh=mesh,
        in_specs=placed,
        out_specs=(
            P(None, "seq", None),
            P(None, "seq", None),
            P(None, "tp"),
            P("tp"),
            P(None, "tp"),
            P(None, "tp"),
            P("tp"),
            P("tp", None),
            P(),
            P(),
            P(),
            P(None, "tp"),
            P("tp"),
            P("tp", None),
            P(),
            P(),
            P(),
        ),
        check_vma=False,
    )
```

```python
from functools import partial

import jax
import jax.numpy as jnp
from jax import lax
from jax.sharding import PartitionSpec as P
from jax.experimental import pallas as pl
from jax.experimental.pallas import tpu as pltpu

HD = 64
BLOCK = 64


norm_eps = 1e-06
masked_score = -1e30
highest_precision = lax.Precision.HIGHEST


def with_halo(shard, sides, width):
    for axis, dim in sides:
        size, length = (lax.axis_size(axis), shard.shape[dim])
        up = [(i, (i + 1) % size) for i in range(size - 1)]
        down = [(j, i) for i, j in up]
        last = lax.slice_in_dim(shard, length - width, length, axis=dim)
        first = lax.slice_in_dim(shard, 0, width, axis=dim)
        before = lax.ppermute(last, axis, up)
        after = lax.ppermute(first, axis, down)
        shard = jnp.concatenate([before, shard, after], axis=dim)
    return shard


def joined(shard, axis, combine):
    everything = jax.tree.map(lambda part: lax.all_gather(part, axis), shard)
    first = jax.tree.map(lambda part: part[0], everything)

    def hop(k, so_far):
        return combine(so_far, jax.tree.map(lambda part: part[k], everything))

    return lax.fori_loop(1, lax.axis_size(axis), hop, first)


def layer_norm(resid, gain, shift):
    centre = resid - jnp.mean(resid, -1, keepdims=True)
    spread = jnp.mean(centre * centre, -1, keepdims=True)
    return centre * lax.rsqrt(spread + norm_eps) * gain + shift


def gelu_exact(values):
    return jax.nn.gelu(values, approximate=False)


def plain_dot(left, right):
    return jnp.dot(left, right, preferred_element_type=jnp.float32)


def rows_dot(left, right):
    return lax.dot_general(
        left, right, (((0,), (0,)), ((), ())), preferred_element_type=jnp.float32
    )


def back_dot(left, right):
    return lax.dot_general(
        left, right, (((1,), (1,)), ((), ())), preferred_element_type=jnp.float32
    )


def softmax_row_probs(scores):
    top_score = jnp.max(scores, -1, keepdims=True)
    expo = jnp.exp(scores - top_score)
    return expo / jnp.sum(expo, -1, keepdims=True)


def head_sum_fwd(pieces):
    return lax.psum(pieces, "tp")


def head_sum_back(pieces):
    return lax.psum(pieces, "tp")


def merge_rows(first, second):
    top_score = jnp.maximum(first[0], second[0])
    scale_one = jnp.exp(first[0] - top_score)
    scale_two = jnp.exp(second[0] - top_score)
    return (
        top_score,
        first[1] * scale_one + second[1] * scale_two,
        first[2] * scale_one[..., None] + second[2] * scale_two[..., None],
    )


def tile_plan(rand_blocks, my_index, n_dev, per_dev, seqs, heads):
    count = seqs * per_dev * heads * 3
    capacity = max(2, 2 * count // n_dev)
    requests = (
        rand_blocks.reshape(seqs, n_dev, per_dev, heads, 3)
        .transpose(1, 0, 2, 3, 4)
        .reshape(n_dev, count)
    )
    is_mine = requests // per_dev == my_index
    ranking = jnp.cumsum(is_mine.astype(jnp.int32), 1) - 1
    slot_ids = jnp.arange(capacity, dtype=jnp.int32)
    select = is_mine[:, None, :] & (ranking[:, None, :] == slot_ids[None, :, None])
    filled = jnp.any(select, 2)
    position = jnp.arange(count, dtype=jnp.int32)
    seq_of = position // (per_dev * heads * 3)
    head_of = position // 3 % heads
    tile_of = (seq_of[None, :] * per_dev + requests % per_dev) * heads + head_of[None, :]
    send_index = jnp.sum(jnp.where(select, tile_of[:, None, :], 0), 2)
    own_requests = lax.dynamic_slice_in_dim(rand_blocks, my_index * per_dev, per_dev, 1).reshape(
        count
    )
    own_owner = own_requests // per_dev
    onehot = (own_owner[:, None] == jnp.arange(n_dev, dtype=jnp.int32)[None, :]).astype(jnp.int32)
    own_rank = jnp.sum((jnp.cumsum(onehot, 0) - 1) * onehot, 1)
    recv_index = own_owner * capacity + own_rank
    return (capacity, send_index, filled, recv_index)


def pick_tiles(incoming, recv_index, seqs, per_dev, heads, block, hsize):
    stacked = incoming.reshape(-1, block, 2 * hsize)
    return jnp.take(stacked, recv_index, 0).reshape(seqs, per_dev, heads, 3, block, 2 * hsize)


def assemble(end_part, window_part, tile_part, seqs, per_dev, heads, block, hsize):
    ends_wide = jnp.broadcast_to(end_part[:, None], (seqs, per_dev, heads, 2 * block, hsize))
    return jnp.concatenate(
        [ends_wide, window_part, tile_part.reshape(seqs, per_dev, heads, 3 * block, hsize)], 3
    )


def split_sequences(
    tokens,
    rand_blocks,
    query_weight,
    query_bias,
    key_weight,
    value_weight,
    value_bias,
    output_weight,
    output_bias,
    attn_gain,
    attn_shift,
    up_weight,
    up_bias,
    down_weight,
    down_bias,
    ffn_gain,
    ffn_shift,
    cotangent,
):
    seqs, rows, width = tokens.shape
    block = BLOCK
    hsize = HD
    per_dev = rows // block
    n_dev = lax.axis_size("seq")
    my_index = lax.axis_index("seq")
    n_blocks = per_dev * n_dev
    heads = query_weight.shape[1] // hsize
    hidden = heads * hsize
    n_tok = seqs * rows
    is_first = my_index == 0
    is_last = my_index == n_dev - 1
    flat = tokens.reshape(n_tok, width)
    query_low = (plain_dot(flat, query_weight) + query_bias).astype(jnp.bfloat16)
    key_low = plain_dot(flat, key_weight).astype(jnp.bfloat16)
    value_low = (plain_dot(flat, value_weight) + value_bias).astype(jnp.bfloat16)
    keyval = jnp.concatenate([key_low, value_low], 1).reshape(seqs, rows, 2 * hidden)
    extended = with_halo(keyval, (("seq", 1),), block)
    windows = jnp.stack(
        [extended[:, offset * block : (offset + 3) * block] for offset in range(per_dev)], 1
    )
    windows = windows.reshape(seqs, per_dev, 3 * block, 2, heads, hsize)
    win_key = windows[:, :, :, 0].transpose(0, 1, 3, 2, 4)
    win_value = windows[:, :, :, 1].transpose(0, 1, 3, 2, 4)
    triple = jnp.concatenate([query_low.reshape(seqs, rows, hidden), keyval], 2).astype(jnp.float32)
    own_ends = jnp.stack(
        [
            jnp.where(is_first, triple[:, :block], 0.0),
            jnp.where(is_last, triple[:, rows - block :], 0.0),
        ],
        1,
    )
    ends = lax.psum(own_ends.astype(jnp.bfloat16), "seq").reshape(seqs, 2, block, 3, heads, hsize)
    end_query = ends[:, :, :, 0].transpose(0, 3, 1, 2, 4).reshape(seqs, heads, 2 * block, hsize)
    end_key = ends[:, :, :, 1].transpose(0, 3, 1, 2, 4).reshape(seqs, heads, 2 * block, hsize)
    end_value = ends[:, :, :, 2].transpose(0, 3, 1, 2, 4).reshape(seqs, heads, 2 * block, hsize)
    capacity, send_index, filled, recv_index = tile_plan(
        rand_blocks, my_index, n_dev, per_dev, seqs, heads
    )
    table = (
        keyval.reshape(seqs, per_dev, block, 2, heads, hsize)
        .transpose(0, 1, 4, 2, 3, 5)
        .reshape(seqs * per_dev * heads, block, 2 * hsize)
    )
    outgoing = jnp.take(table, send_index.reshape(-1), 0).reshape(n_dev, capacity, block, 2 * hsize)
    outgoing = jnp.where(filled[:, :, None, None], outgoing, jnp.zeros((), jnp.bfloat16))
    incoming = lax.all_to_all(outgoing, "seq", split_axis=0, concat_axis=0, tiled=True)
    tiles = pick_tiles(incoming, recv_index, seqs, per_dev, heads, block, hsize)
    q_blocks = query_low.reshape(seqs, per_dev, block, heads, hsize).transpose(0, 1, 3, 2, 4)
    keys_all = assemble(end_key, win_key, tiles[..., :hsize], seqs, per_dev, heads, block, hsize)
    values_all = assemble(
        end_value, win_value, tiles[..., hsize:], seqs, per_dev, heads, block, hsize
    )
    block_ids = my_index * per_dev + jnp.arange(per_dev, dtype=jnp.int32)
    slot_ids = jnp.arange(8 * block, dtype=jnp.int32) // block
    dropped = (slot_ids == 2)[None, :] & (block_ids == 1)[:, None] | (slot_ids == 4)[None, :] & (
        block_ids == n_blocks - 2
    )[:, None]
    unscaled_scores = (
        jnp.einsum("sbhqd,sbhkd->sbhqk", q_blocks, keys_all, preferred_element_type=jnp.float32)
        * 0.125
    )
    unscaled_scores = jnp.where(dropped[None, :, None, None, :], masked_score, unscaled_scores)
    weights = softmax_row_probs(unscaled_scores)
    sparse_attention = jnp.einsum(
        "sbhqk,sbhkd->sbhqd",
        weights,
        values_all.astype(jnp.float32),
        precision=highest_precision,
        preferred_element_type=jnp.float32,
    )
    key_local = key_low.reshape(seqs, rows, heads, hsize).transpose(0, 2, 1, 3)
    value_local = value_low.reshape(seqs, rows, heads, hsize).transpose(0, 2, 1, 3)
    end_raw = (
        jnp.einsum("shqd,shkd->shqk", end_query, key_local, preferred_element_type=jnp.float32)
        * 0.125
    )
    end_top = jnp.max(end_raw, -1)
    end_expo = jnp.exp(end_raw - end_top[..., None])
    end_total = jnp.sum(end_expo, -1)
    end_acc = jnp.einsum(
        "shqk,shkd->shqd",
        end_expo,
        value_local.astype(jnp.float32),
        precision=highest_precision,
        preferred_element_type=jnp.float32,
    )
    merged_top, merged_total, merged_acc = joined((end_top, end_total, end_acc), "seq", merge_rows)
    end_out = merged_acc / merged_total[..., None]
    end_lse = merged_top + jnp.log(merged_total)
    end_split = end_out.reshape(seqs, heads, 2, block, hsize)
    first_rows = block_ids == 0
    last_rows = block_ids == n_blocks - 1
    attn = jnp.where(
        first_rows[None, :, None, None, None], end_split[:, None, :, 0], sparse_attention
    )
    attn = jnp.where(last_rows[None, :, None, None, None], end_split[:, None, :, 1], attn)
    attn_low = attn.transpose(0, 1, 3, 2, 4).reshape(n_tok, hidden).astype(jnp.bfloat16)
    branch = head_sum_fwd(plain_dot(attn_low, output_weight)) + output_bias
    resid = flat.astype(jnp.float32) + branch
    normed = layer_norm(resid, attn_gain, attn_shift)
    normed_low = normed.astype(jnp.bfloat16)
    pre_act = plain_dot(normed_low, up_weight) + up_bias
    act_low = gelu_exact(pre_act).astype(jnp.bfloat16)
    ffn = head_sum_fwd(plain_dot(act_low, down_weight)) + down_bias
    resid_two = normed + ffn
    layer_output = (
        layer_norm(resid_two, ffn_gain, ffn_shift).astype(jnp.bfloat16).reshape(seqs, rows, width)
    )
    cot_flat = cotangent.reshape(n_tok, width).astype(jnp.float32)
    norm_two, pull_two = jax.vjp(layer_norm, resid_two, ffn_gain, ffn_shift)
    grad_resid2, grad_ffngain, grad_ffnshift = pull_two(cot_flat)
    grad_ffn = grad_resid2.astype(jnp.bfloat16)
    grad_downbias = jnp.sum(grad_ffn.astype(jnp.float32), 0)
    grad_downweight = rows_dot(act_low, grad_ffn)
    grad_act = back_dot(grad_ffn, down_weight)
    gelu_out, pull_gelu = jax.vjp(gelu_exact, pre_act)
    grad_pre = pull_gelu(grad_act)[0].astype(jnp.bfloat16)
    grad_upbias = jnp.sum(grad_pre.astype(jnp.float32), 0)
    grad_upweight = rows_dot(normed_low, grad_pre)
    grad_normed = grad_resid2 + head_sum_back(back_dot(grad_pre, up_weight))
    norm_one, pull_one = jax.vjp(layer_norm, resid, attn_gain, attn_shift)
    grad_resid, grad_attngain, grad_attnshift = pull_one(grad_normed)
    grad_branch = grad_resid.astype(jnp.bfloat16)
    grad_obias = jnp.sum(grad_branch.astype(jnp.float32), 0)
    grad_oweight = rows_dot(attn_low, grad_branch)
    grad_attn = back_dot(grad_branch, output_weight).astype(jnp.bfloat16)
    grad_heads = grad_attn.reshape(seqs, per_dev, block, heads, hsize).transpose(0, 1, 3, 2, 4)
    global_mask = (first_rows | last_rows)[None, :, None, None, None]
    grad_sparse = jnp.where(global_mask, jnp.zeros((), jnp.bfloat16), grad_heads)
    own_dout = jnp.stack(
        [
            jnp.where(is_first, grad_heads[:, 0].astype(jnp.float32), 0.0),
            jnp.where(is_last, grad_heads[:, per_dev - 1].astype(jnp.float32), 0.0),
        ],
        2,
    ).reshape(seqs, heads, 2 * block, hsize)
    own_delta = jnp.sum(own_dout * end_out, -1)
    end_dout, end_delta = lax.psum((own_dout, own_delta), "seq")
    end_dlow = end_dout.astype(jnp.bfloat16)
    end_prob = jnp.exp(end_raw - end_lse[..., None])
    end_dprob = jnp.einsum(
        "shqd,shkd->shqk", end_dlow, value_local, preferred_element_type=jnp.float32
    )
    end_dscore = (end_prob * (end_dprob - end_delta[..., None]) * 0.125).astype(jnp.bfloat16)
    end_dquery_part = jnp.einsum(
        "shqk,shkd->shqd", end_dscore, key_local, preferred_element_type=jnp.float32
    )
    local_dkey = jnp.einsum(
        "shqk,shqd->shkd", end_dscore, end_query, preferred_element_type=jnp.float32
    )
    local_dvalue = jnp.einsum(
        "shqk,shqd->shkd",
        end_prob,
        end_dout,
        precision=highest_precision,
        preferred_element_type=jnp.float32,
    )
    again = lax.all_to_all(outgoing, "seq", split_axis=0, concat_axis=0, tiled=True)
    back_tiles = pick_tiles(again, recv_index, seqs, per_dev, heads, block, hsize)
    keys_back = assemble(
        end_key, win_key, back_tiles[..., :hsize], seqs, per_dev, heads, block, hsize
    )
    values_back = assemble(
        end_value, win_value, back_tiles[..., hsize:], seqs, per_dev, heads, block, hsize
    )
    grad_prob = jnp.einsum(
        "sbhqd,sbhkd->sbhqk", grad_sparse, values_back, preferred_element_type=jnp.float32
    )
    row_delta = jnp.sum(weights * grad_prob, -1, keepdims=True)
    grad_score = (weights * (grad_prob - row_delta) * 0.125).astype(jnp.bfloat16)
    grad_qblocks = jnp.einsum(
        "sbhqk,sbhkd->sbhqd", grad_score, keys_back, preferred_element_type=jnp.float32
    )
    grad_keysall = jnp.einsum(
        "sbhqk,sbhqd->sbhkd", grad_score, q_blocks, preferred_element_type=jnp.float32
    )
    grad_valsall = jnp.einsum(
        "sbhqk,sbhqd->sbhkd",
        weights,
        grad_sparse.astype(jnp.float32),
        precision=highest_precision,
        preferred_element_type=jnp.float32,
    )
    end_dkey = jnp.sum(grad_keysall[:, :, :, : 2 * block], 1)
    end_dvalue = jnp.sum(grad_valsall[:, :, :, : 2 * block], 1)
    win_grad = jnp.stack(
        [
            grad_keysall[:, :, :, 2 * block : 5 * block].transpose(0, 1, 3, 2, 4),
            grad_valsall[:, :, :, 2 * block : 5 * block].transpose(0, 1, 3, 2, 4),
        ],
        3,
    ).reshape(seqs, per_dev, 3 * block, 2 * hidden)
    rand_grad = (
        jnp.concatenate(
            [
                grad_keysall[:, :, :, 5 * block :].reshape(seqs, per_dev, heads, 3, block, hsize),
                grad_valsall[:, :, :, 5 * block :].reshape(seqs, per_dev, heads, 3, block, hsize),
            ],
            5,
        )
        .reshape(-1, block, 2 * hsize)
        .astype(jnp.bfloat16)
    )
    ext_grad = jnp.zeros((seqs, rows + 2 * block, 2 * hidden), jnp.float32)
    for offset in range(per_dev):
        ext_grad = ext_grad.at[:, offset * block : (offset + 3) * block].add(win_grad[:, offset])
    rims = jnp.concatenate([ext_grad[:, :block], ext_grad[:, rows + block :]], 1)
    returned_rims = with_halo(rims.astype(jnp.bfloat16), (("seq", 1),), block).astype(rims.dtype)
    middle_zero = jnp.zeros((seqs, rows - 2 * block, 2 * hidden), jnp.float32)
    kv_grad = ext_grad[:, block : rows + block] + jnp.concatenate(
        [returned_rims[:, :block], middle_zero, returned_rims[:, 3 * block :]], 1
    )
    sent_back = (
        jnp.zeros((n_dev * capacity, block, 2 * hsize), jnp.bfloat16)
        .at[recv_index]
        .set(rand_grad)
        .reshape(n_dev, capacity, block, 2 * hsize)
    )
    arrived = lax.all_to_all(sent_back, "seq", split_axis=0, concat_axis=0, tiled=True)
    arrived = jnp.where(filled[:, :, None, None], arrived.astype(jnp.float32), 0.0)
    table_grad = (
        jnp.zeros((seqs * per_dev * heads, block, 2 * hsize), jnp.float32)
        .at[send_index.reshape(-1)]
        .add(arrived.reshape(-1, block, 2 * hsize))
    )
    kv_grad = kv_grad + table_grad.reshape(seqs, per_dev, heads, block, 2, hsize).transpose(
        0, 1, 3, 4, 2, 5
    ).reshape(seqs, rows, 2 * hidden)
    kv_grad = kv_grad + jnp.stack(
        [local_dkey.transpose(0, 2, 1, 3), local_dvalue.transpose(0, 2, 1, 3)], 2
    ).reshape(seqs, rows, 2 * hidden)
    end_dquery, end_dkey_all, end_dvalue_all = (
        lax.psum(end_dquery_part.astype(jnp.bfloat16), "seq").astype(jnp.float32),
        lax.psum(end_dkey.astype(jnp.bfloat16), "seq").astype(jnp.float32),
        lax.psum(end_dvalue.astype(jnp.bfloat16), "seq").astype(jnp.float32),
    )
    end_kv = jnp.stack(
        [end_dkey_all.transpose(0, 2, 1, 3), end_dvalue_all.transpose(0, 2, 1, 3)], 2
    ).reshape(seqs, 2 * block, 2 * hidden)
    kv_grad = kv_grad + jnp.concatenate(
        [
            jnp.where(is_first, end_kv[:, :block], 0.0),
            middle_zero,
            jnp.where(is_last, end_kv[:, block:], 0.0),
        ],
        1,
    )
    end_q = end_dquery.transpose(0, 2, 1, 3).reshape(seqs, 2 * block, hidden)
    query_zero = jnp.zeros((seqs, rows - 2 * block, hidden), jnp.float32)
    grad_query = grad_qblocks.transpose(0, 1, 3, 2, 4).reshape(seqs, rows, hidden)
    grad_query = grad_query + jnp.concatenate(
        [
            jnp.where(is_first, end_q[:, :block], 0.0),
            query_zero,
            jnp.where(is_last, end_q[:, block:], 0.0),
        ],
        1,
    )
    query_glow = grad_query.reshape(n_tok, hidden).astype(jnp.bfloat16)
    kv_glow = kv_grad.reshape(n_tok, 2 * hidden).astype(jnp.bfloat16)
    key_glow = kv_glow[:, :hidden]
    value_glow = kv_glow[:, hidden:]
    grad_qbias = jnp.sum(query_glow.astype(jnp.float32), 0)
    grad_vbias = jnp.sum(value_glow.astype(jnp.float32), 0)
    grad_qweight = rows_dot(flat, query_glow)
    grad_kweight = rows_dot(flat, key_glow)
    grad_vweight = rows_dot(flat, value_glow)
    into_tokens = (
        back_dot(query_glow, query_weight)
        + back_dot(key_glow, key_weight)
        + back_dot(value_glow, value_weight)
    )
    input_grad = (grad_resid + head_sum_back(into_tokens)).reshape(seqs, rows, width)
    totals = lax.psum(
        (
            grad_qweight,
            grad_qbias,
            grad_kweight,
            grad_vweight,
            grad_vbias,
            grad_oweight,
            grad_obias,
            grad_attngain,
            grad_attnshift,
            grad_upweight,
            grad_upbias,
            grad_downweight,
            grad_downbias,
            grad_ffngain,
            grad_ffnshift,
        ),
        "seq",
    )
    return (
        layer_output,
        input_grad,
        totals[0],
        totals[1],
        totals[2],
        totals[3],
        totals[4],
        totals[5],
        totals[6],
        totals[7],
        totals[8],
        totals[9],
        totals[10],
        totals[11],
        totals[12],
        totals[13],
        totals[14],
    )


HALF_ROOT = 0.7071067811865476
PDF_SCALE = 0.3989422804014327


MESH = pl.DeviceIdType.MESH


def place():
    me, t = lax.axis_index("seq"), lax.axis_index("tp")
    side, core = lax.div(t, 2), lax.rem(t, 2)
    return me, t, side, core


def tp_peer(side, core, bits):
    there = 1 - side if bits & 2 else side
    return there * 2 + (1 - core if bits & 1 else core)


def greet(peers):
    barrier = pltpu.get_barrier_semaphore()
    for peer in peers:
        pl.semaphore_signal(barrier, inc=1, device_id=peer, device_id_type=MESH)
    pl.semaphore_wait(barrier, len(peers))


def remote(src, dst, sends, recvs, at, peer):
    return pltpu.make_async_remote_copy(
        src_ref=src,
        dst_ref=dst,
        send_sem=sends.at[at],
        recv_sem=recvs.at[at],
        device_id=peer,
        device_id_type=MESH,
    )


class Piece:
    def __init__(self, at, bit, own, held, spots, sems):
        me, t, side, core = spots
        self.at, self.own, self.far = at, own, partial(held, 2 + core)
        mate, self.half = flip(me, bit)
        self.mate = (mate, t)
        self.near, self.across = (me, tp_peer(side, core, 1)), (me, tp_peer(side, core, 2))
        self.sems = sems
        self.then = []

    def move(self, n):
        h = 1 - self.half if n == 3 else self.half
        src = self.own(h) if n == 0 else self.far(h)
        peer = (self.across, self.mate, self.near, self.near)[n]
        return remote(src, self.far(h), *self.sems, (self.at, n), peer)

    def start(self):
        self.move(0).start()

    def pass_on(self):
        self.move(0).wait_recv()
        for piece in self.then:
            piece.start()
        self.move(1).start()
        self.move(2).start()

    def pass_side(self):
        self.move(1).wait_recv()
        self.move(3).start()

    def arrive(self):
        self.move(2).wait_recv()
        self.move(3).wait_recv()

    def sent(self):
        for n in range(4):
            self.move(n).wait_send()


def enter_kernel(
    n_dev, tok, cot, rand, wq, wk, wv, qb, vb, ub, wo, up, down,
    x, q, ko, kf, vo, vf, attn, lse, ids, ubs, wt_out, cot_out, wo_out, up_out, down_out,
    wt, qbs, vbs, ids_for, own_wo, own_up, own_down,
    tok_send, tok_recv, cot_send, cot_recv, p_send, p_recv, o_send, o_recv, s_send, s_recv, kv_send, kv_recv, local,
):
    spots = me, t, side, core = place()
    near = (me, tp_peer(side, core, 1))
    hidden, width = wq.shape
    units = down.shape[0]
    span = x.shape[0]
    heads = hidden // HD
    pairs = width // (2 * HD)
    part = hidden // 2
    n_part = units // 2 // part
    own_buf = (own_wo, own_up, own_down)

    holds = [(w, lambda j, m=m: wt.at[m, j]) for m, w in ((1, wk), (2, wv), (0, wq))]
    holds += [
        (wo, lambda j: wo_out.at[pl.ds(j * hidden, hidden), :]),
        (up, lambda j: up_out.at[:, pl.ds(j * units, units)]),
        (down, lambda j: down_out.at[pl.ds(j * units, units), :]),
    ]
    pieces = []
    for n, (ref, block) in enumerate(holds):
        for i in range(1 if n < 4 else n_part):
            count = 1 if n < 4 else n_part

            def rows(r, h, i=i, count=count):
                return r.at[pl.ds((h * count + i) * part, part), :]

            at = len(pieces)
            pieces.append(
                Piece(
                    at, (1, 2)[at % 2],
                    lambda h, ref=ref, rows=rows: rows(ref, h),
                    lambda j, h, block=block, rows=rows: rows(block(j), h),
                    spots, (p_send, p_recv),
                )
            )

    ahead = 4
    for piece, later in zip(pieces, pieces[ahead:]):
        piece.then = [later]

    def own_near(n):
        return remote(holds[n][0], holds[n][1](core), o_send, o_recv, n, near)

    def own_here(n):
        src = holds[n][0] if n < 3 else own_buf[n - 3]
        return pltpu.make_async_copy(src, holds[n][1](core), local.at[n])

    def own_in(n):
        return pltpu.make_async_copy(holds[n][0], own_buf[n - 3], local.at[6 + n])

    def spread(src, dst, sends, recvs):
        return [
            remote(
                src.at[2 * lax.rem(me + k, n_dev) + side, pl.ds(core * BLOCK, BLOCK), :],
                dst.at[pl.ds(k * BLOCK, BLOCK), :],
                sends, recvs, k - 1, (lax.rem(me + k, n_dev), t),
            )
            for k in range(1, n_dev)
        ]

    def kept(n):
        src, dst = ((tok, x), (cot, cot_out))[n]
        return pltpu.make_async_copy(
            src.at[2 * me + side, pl.ds(core * BLOCK, BLOCK), :], dst.at[pl.ds(0, BLOCK), :], local.at[12 + n]
        )

    def shared(bits, which=(0, 1, 2, 3)):
        slot = (bits & 2) + core
        to = tp_peer(side, core, bits)
        moves = (
            (qb, qbs.at[slot]), (vb, vbs.at[slot]), (ub, ubs.at[slot]),
            (ids_for.at[to], ids.at[pl.ds(slot * heads, heads)]),
        )
        return [
            remote(*moves[n], s_send, s_recv, (bits - 1, n), (me, to)) for n in which
        ]

    greet(all_peers(n_dev, *spots) + [(me, tp_peer(side, core, 3))])
    for move in spread(tok, x, tok_send, tok_recv):
        move.start()
    for piece in pieces[:ahead]:
        piece.start()
    kept(0).start()
    for n in range(3):
        own_near(n).start()
        own_here(n).start()
    qbs[core], vbs[core], ubs[core] = qb[...], vb[...], ub[...]
    for bits in (1, 2, 3):
        for move in shared(bits, (0, 1, 2)):
            move.start()
    for n in range(3, 6):
        own_in(n).start()

    lane = lax.broadcasted_iota(jnp.int32, (1, span), 1)
    for y in range(2):
        for c in range(2):
            block = 2 * lax.rem(me - lane // BLOCK + n_dev, n_dev) + c
            for h in range(heads):
                for r in range(3):
                    line = rand[h, r, pl.ds(2 * me + y, 1), :]
                    row = jnp.zeros((1, span), jnp.int32)
                    for b in range(c, 2 * n_dev, 2):
                        row = jnp.where(block == b, line[:, b : b + 1], row)
                    ids_for[2 * y + c, h, r : r + 1, :] = row
    ids[pl.ds(core * heads, heads)] = ids_for[t]
    for bits in (1, 2, 3):
        shared(bits, (3,))[0].start()

    def advance(n):
        pieces[n].pass_on()
        if n:
            pieces[n - 1].pass_side()

    for n in range(4):
        advance(n)
    for move in spread(tok, x, tok_send, tok_recv):
        move.wait_recv()
    kept(0).wait()
    for move in spread(cot, cot_out, cot_send, cot_recv):
        move.start()
    kept(1).start()
    for n in range(3, 6):
        own_near(n).start()
        own_in(n).wait()
        own_here(n).start()
    for bits in (1, 2, 3):
        for move in shared(bits):
            move.wait_recv()

    def bias_of(ref):
        return jnp.concatenate([ref[j] for j in range(4)], 1)

    def project(n, m):
        own_near(n).wait_recv()
        own_here(n).wait()
        pieces[n].arrive()
        return back_dot(x[...], wt[m].reshape(width, width))

    def swap_kv(n):
        src, dst = ((ko, kf), (vo, vf))[n]
        return remote(src, dst, kv_send, kv_recv, n, near)

    ko[...] = project(0, 1).astype(jnp.bfloat16)
    swap_kv(0).start()
    vo[...] = (project(1, 2) + bias_of(vbs)).astype(jnp.bfloat16)
    swap_kv(1).start()
    advance(4)
    q[...] = (project(2, 0) + bias_of(qbs)).astype(jnp.bfloat16)
    keep = pltpu.make_async_copy(wt, wt_out, local.at[14])
    keep.start()
    advance(5)
    swap_kv(0).wait_recv()
    swap_kv(1).wait_recv()

    def pair(p, carry):
        lanes = pl.ds(pl.multiple_of(p * 2 * HD, 2 * HD), 2 * HD)
        attend_pair(n_dev, p, lanes, q, ko, kf, vo, vf, ids, attn, lse, me, core)
        for k in range(3):

            @pl.when(p == 2 * k + 1)
            def _():
                advance(6 + k)

        return carry

    lax.fori_loop(0, pairs, pair, 0)
    for n in range(9, len(pieces)):
        advance(n)
    pieces[-1].pass_side()
    for n in range(3, len(pieces)):
        pieces[n].arrive()
    for move in spread(cot, cot_out, cot_send, cot_recv):
        move.wait()
    kept(1).wait()
    keep.wait()
    for move in spread(tok, x, tok_send, tok_recv):
        move.wait_send()
    for piece in pieces:
        piece.sent()
    for n in range(6):
        own_near(n).wait_send()
        if n > 2:
            own_near(n).wait_recv()
            own_here(n).wait()
    for bits in (1, 2, 3):
        for move in shared(bits):
            move.wait_send()
    for n in range(2):
        swap_kv(n).wait_send()


def enter(tok, cot, rand, wq, wk, wv, qb, vb, ub, wo, up, down, n_dev):
    hidden, width = wq.shape
    units = down.shape[0]
    span = n_dev * BLOCK
    heads = hidden // HD
    pieces = 4 + 2 * (units // hidden)
    vmem = pl.BlockSpec(memory_space=pltpu.VMEM)
    hbm = pl.BlockSpec(memory_space=pl.ANY)
    shape = lambda dtype, *dims: jax.ShapeDtypeStruct(dims, dtype)
    low = partial(shape, jnp.bfloat16)
    dma = pltpu.SemaphoreType.DMA
    return pl.pallas_call(
        partial(enter_kernel, n_dev),
        in_specs=[hbm, hbm, vmem] + [hbm] * 3 + [vmem] * 3 + [hbm] * 3,
        out_specs=[vmem] * 10 + [hbm] * 5,
        out_shape=[low(span, width)] * 7
        + [
            shape(jnp.float32, 2 * heads, 2, span),
            shape(jnp.int32, 4 * heads, 3, span),
            shape(jnp.float32, 4, 1, units),
            low(3, 4, hidden, width),
            low(span, width),
            low(width, width),
            low(width, 4 * units),
            low(4 * units, width),
        ],
        scratch_shapes=[
            pltpu.VMEM((3, 4, hidden, width), jnp.bfloat16),
            pltpu.VMEM((4, 1, hidden), jnp.float32),
            pltpu.VMEM((4, 1, hidden), jnp.float32),
            pltpu.VMEM((4, heads, 3, span), jnp.int32),
            pltpu.VMEM(wo.shape, jnp.bfloat16),
            pltpu.VMEM(up.shape, jnp.bfloat16),
            pltpu.VMEM(down.shape, jnp.bfloat16),
            dma((n_dev - 1,)),
            dma((n_dev - 1,)),
            dma((n_dev - 1,)),
            dma((n_dev - 1,)),
            dma((pieces, 4)),
            dma((pieces, 4)),
            dma((6,)),
            dma((6,)),
            dma((3, 4)),
            dma((3, 4)),
            dma((2,)),
            dma((2,)),
            dma((15,)),
        ],
        compiler_params=pltpu.CompilerParams(
            collective_id=0, has_side_effects=True, vmem_limit_bytes=56 * 2**20
        ),
    )(tok, cot, rand, wq, wk, wv, qb, vb, ub, wo, up, down)


def list_bias(ids_ref, h, key_shift, me, core, n_dev, span):
    n_blocks = 2 * n_dev
    row = lax.broadcasted_iota(jnp.int32, (n_dev, span), 0)
    lane = lax.broadcasted_iota(jnp.int32, (n_dev, span), 1)
    wrap = lambda i: lax.rem(me - i + n_dev, n_dev)
    k = 2 * wrap(row) + (1 - core if key_shift else core)
    b = 2 * wrap(lane // BLOCK) + core
    one = lambda flag: jnp.where(flag, 1.0, 0.0)
    count = (
        one(k == 0)
        + one(k == n_blocks - 1)
        + one((k == b - 1) & (b != 1))
        + one(k == b)
        + one((k == b + 1) & (b != n_blocks - 2))
    )
    for r in range(3):
        count = count + one(ids_ref[h, r : r + 1, :] == k)
    count = jnp.where((b == 0) | (b == n_blocks - 1), 1.0, count)
    return jnp.where(count > 0.5, jnp.log(jnp.maximum(count, 1.0)), masked_score)


def attend_pair(n_dev, p, lanes, q_ref, ko, kf, vo, vf, ids, attn, lse, me, core):
    span = q_ref.shape[0]
    blocks = span // BLOCK
    lane = lax.broadcasted_iota(jnp.int32, (1, 2 * HD), 1) // HD
    q = q_ref[:, lanes]
    keys = (ko[:, lanes], kf[:, lanes])
    values = (vo[:, lanes].T, vf[:, lanes].T)
    outs = []
    for h in range(2):
        qh = (jnp.where(lane == h, q, 0.0) * 0.125).astype(jnp.bfloat16)
        scores = []
        for far in range(2):
            bias = list_bias(ids, 2 * p + h, far == 1, me, core, n_dev, span)
            raw = back_dot(keys[far], qh).reshape(blocks, BLOCK, span)
            scores.append((raw + bias[:, None, :]).reshape(span, span))
        top = jnp.maximum(*(jnp.max(s, 0, keepdims=True) for s in scores))
        expo = [jnp.exp(s - top) for s in scores]
        total = sum(jnp.sum(e, 0, keepdims=True) for e in expo)
        rows = slice(h * HD, (h + 1) * HD)
        acc = sum(plain_dot(v[rows], e.astype(jnp.bfloat16)) for v, e in zip(values, expo))
        outs.append(acc / total)
        lse[p, h : h + 1, :] = top + jnp.log(total)
    attn[:, lanes] = jnp.concatenate(outs, 0).T.astype(jnp.bfloat16)


def flip(index, bit):
    value = lax.rem(lax.div(index, bit), 2)
    return index + bit - 2 * bit * value, value


class Reduction:
    def __init__(self, away, mine, spots, bufs, sems):
        self.away, self.mine = away, mine
        self.jobs, self.ahead = [], 3
        self.me, self.t, self.side, self.core = spots
        self.b0, self.b1, self.acc, self.halves, self.got, self.f = bufs
        self.send, self.recv, self.send0, self.recv0 = sems
        self.near = (self.me, tp_peer(self.side, self.core, 1))
        self.across = (self.me, tp_peer(self.side, self.core, 2))
        self.mates = []
        self.bits = []
        for bit in (1, 2, 4):
            mate, value = flip(self.me, bit)
            self.mates.append((mate, self.t))
            self.bits.append(value)

    def span(self, ref, start, size):
        return ref.at[pl.ds(pl.multiple_of(start, 16), size), :]

    def rows(self, depth):
        start, size, inner = 0, self.f.shape[1], 0
        for level in range(depth):
            size //= 2
            start = start + self.bits[level] * size
            inner = inner + (self.bits[level] * size if level else 0)
        return start, inner, size

    def first(self, ch):
        return [
            remote(self.away(ch, y), self.b0.at[ch, y], self.send0, self.recv0, (ch, y), self.near)
            for y in range(2)
        ]

    def over_y(self, ch):
        return remote(self.mine(ch, 1), self.b1.at[ch], self.send, self.recv, (ch, 0), self.across)

    def next_y(self, job):
        if job + self.ahead < len(self.jobs):
            self.jobs[job + self.ahead]().start()

    def halving(self, ch, level):
        size = self.rows(level + 1)[2]
        return remote(
            self.halves.at[ch, pl.ds(size, size), :],
            self.got.at[ch, pl.ds(size, size), :],
            self.send, self.recv, (ch, 1 + level), self.mates[level],
        )

    def gather(self, ch, level):
        start, _, size = self.rows(level + 1)
        held = self.span(self.f.at[ch], start, size)
        return remote(held, held, self.send, self.recv, (ch, 4 + level), self.mates[level])

    def stage(self, ch, s):
        full = jnp.float32
        if s == 0:
            for move in self.first(ch):
                move.start()
        elif s == 1:
            for move in self.first(ch):
                move.wait()
            out = self.mine(ch, 1)
            out[...] = (out[...].astype(full) + self.b0[ch, 1].astype(full)).astype(jnp.bfloat16)
            if ch < self.ahead:
                self.over_y(ch).start()
        elif s == 2:
            self.over_y(ch).wait_recv()
            self.next_y(ch)
            size = self.rows(1)[2]

            def total(start):
                terms = (self.mine(ch, 0), self.b0.at[ch, 0], self.b1.at[ch])
                one, two, three = (self.span(ref, start, size)[...].astype(full) for ref in terms)
                return one + two + three

            self.halves[ch, pl.ds(size, size), :] = total((1 - self.bits[0]) * size).astype(jnp.bfloat16)
            self.halving(ch, 0).start()
            self.acc[ch] = total(self.bits[0] * size)
        elif s <= 5:
            level = s - 3
            _, inner, size = self.rows(level + 1)
            self.halving(ch, level).wait_recv()
            total = self.span(self.acc.at[ch], inner, size)[...] + self.got[ch, pl.ds(size, size), :].astype(full)
            if s == 5:
                self.span(self.f.at[ch], self.rows(3)[0], size)[...] = total.astype(jnp.bfloat16)
                self.gather(ch, 2).start()
            else:
                self.span(self.acc.at[ch], inner, size)[...] = total
                small = size // 2
                other = self.span(self.acc.at[ch], inner + (1 - self.bits[level + 1]) * small, small)
                self.halves[ch, pl.ds(small, small), :] = other[...].astype(jnp.bfloat16)
                self.halving(ch, level + 1).start()
        elif s <= 7:
            self.gather(ch, 8 - s).wait_recv()
            self.gather(ch, 7 - s).start()
        else:
            self.gather(ch, 0).wait_recv()

    def finish(self, ch):
        self.over_y(ch).wait_send()
        for level in range(3):
            self.halving(ch, level).wait_send()
            self.gather(ch, level).wait_send()


class Return:
    def __init__(self, at, n_dev, src, dst, spots, sems):
        self.at, self.n_dev, self.src, self.dst = at, n_dev, src, dst
        self.me, self.t, self.side, self.core = spots
        self.send, self.recv, self.local = sems
        self.near = (self.me, tp_peer(self.side, self.core, 1))
        self.across = (self.me, tp_peer(self.side, self.core, 2))

    def block(self, s, side):
        return self.dst.at[s, side, pl.ds(self.core * BLOCK, BLOCK), :]

    def keep(self):
        return pltpu.make_async_copy(
            self.src.at[pl.ds(0, BLOCK), :], self.block(self.me, self.side), self.local.at[self.at]
        )

    def out(self, k):
        to = lax.rem(self.me - k + self.n_dev, self.n_dev)
        return remote(
            self.src.at[pl.ds(k * BLOCK, BLOCK), :], self.block(self.me, self.side),
            self.send, self.recv, (self.at, k - 1), (to, self.t),
        )

    def pass_on(self, n):
        side = 1 - self.side if n == 2 else self.side
        held = self.dst.at[:, side, pl.ds(self.core * BLOCK, BLOCK), :]
        peer = self.across if n == 0 else self.near
        return remote(held, held, self.send, self.recv, (self.at, self.n_dev - 1 + n), peer)

    def stage(self, s):
        if s == 0:
            self.keep().start()
            for k in range(1, self.n_dev):
                self.out(k).start()
        elif s == 1:
            self.keep().wait()
            for k in range(1, self.n_dev):
                self.out(k).wait_recv()
            self.pass_on(1).start()
        elif s == 2:
            self.pass_on(0).wait_recv()
            self.then()
            self.pass_on(2).start()
        else:
            for k in range(1, self.n_dev):
                self.out(k).wait_send()
            self.pass_on(0).wait_send()
            self.pass_on(1).wait()
            self.pass_on(2).wait()


class SmallSum:
    def __init__(self, out, came, spots, sems):
        self.out, self.came = out, came
        me, t, side, core = spots
        self.send, self.recv = sems
        self.peers = [(me, tp_peer(side, core, 1)), (me, tp_peer(side, core, 2))]
        self.peers += [(flip(me, bit)[0], t) for bit in (1, 2, 4)]

    def move(self, n):
        held = self.out.at[n]
        return remote(held, self.came.at[n], self.send, self.recv, n, self.peers[n])

    def stage(self, n):
        if n:
            self.move(n - 1).wait_recv()
            self.out[n] = self.out[n - 1] + self.came[n - 1]
        if n < len(self.peers):
            self.move(n).start()

    def finish(self):
        for n in range(len(self.peers)):
            self.move(n).wait_send()


def all_peers(n_dev, me, t, side, core):
    return [(lax.rem(me + k, n_dev), t) for k in range(1, n_dev)] + [
        (me, tp_peer(side, core, bits)) for bits in (1, 2)
    ]


def tail_kernel(
    n_dev, q, ko, kf, vo, vf, ids, lse, attn, gat, x, gres, early, normed, g_ffn, act, g_pre, low, wt_hbm,
    f, out, iout, total,
    load, p2, wt, b0, b1, acc, halves, got, came, dq, own, far, far_in, ig,
    send, recv, send0, recv0, local, x_send, x_recv, r_send, r_recv, r_local, s_send, s_recv,
):
    spots = me, t, side, core = place()
    span, width = q.shape
    units, hidden = act.shape[1] // 4, width // 4
    rows = f.shape[1]
    n_down = units // rows
    n_ffn = n_down + width // rows
    count = f.shape[0]
    pairs = width // (2 * HD)
    near = (me, tp_peer(side, core, 1))

    def own_rows(ch, block):
        return p2.at[block, pl.ds((ch - n_ffn) * rows, rows), :]

    def away(ch, y):
        return halves.at[2 * (ch % 4) + y] if ch < n_ffn else own_rows(ch, 2 * y + 1 - core)

    def mine(ch, y):
        return load.at[ch, y] if ch < n_ffn else own_rows(ch, 2 * y + core)

    red = Reduction(away, mine, spots, (b0, b1, acc, halves, got, f), (send, recv, send0, recv0))
    back = [
        Return(n, n_dev, src, dst, spots, (r_send, r_recv, r_local))
        for n, (src, dst) in enumerate(((low, out), (ig, iout)))
    ]
    tiny = SmallSum(total, came, spots, (s_send, s_recv))

    def loads(n):
        src = (act, g_pre)[n]
        for j in range(4):
            dst = (p2.at[j, pl.ds(0, span), :], wt.at[pl.ds(j * span, span), :])[n]
            yield pltpu.make_async_copy(src.at[:, pl.ds(j * units, units)], dst, local.at[4 * n + j])
        yield pltpu.make_async_copy((g_ffn, normed)[n], (ig, dq)[n], local.at[9 + n])

    def weights_in():
        return pltpu.make_async_copy(wt_hbm, wt, local.at[8])

    def ffn_grad(ch, block):
        if ch < n_down:
            left, right = p2[block, 0:span, ch * rows : (ch + 1) * rows], ig[...]
        else:
            left = dq[:, (ch - n_down) * rows : (ch - n_down + 1) * rows]
            right = wt[pl.ds(pl.multiple_of(block * span, span), span), :]
        return plain_dot(left.T, right).astype(jnp.bfloat16)

    def swap_far(p, n):
        return remote(far.at[n, p], far_in.at[n, p], x_send, x_recv, (p, n), near)

    red.jobs = [partial(red.over_y, ch) for ch in range(count)]
    red.jobs += [partial(b.pass_on, 0) for b in back]
    back[0].then, back[1].then = partial(red.next_y, count), partial(red.next_y, count + 1)

    def begin(ch):
        for y in range(2):
            away(ch, y)[...] = ffn_grad(ch, 2 * y + 1 - core)
        red.stage(ch, 0)
        for y in range(2):
            load[ch, y] = ffn_grad(ch, 2 * y + core)

    for n in range(2):
        for move in loads(n):
            move.start()
    greet(all_peers(n_dev, *spots))
    back[0].stage(0)
    for n in range(2):
        for move in loads(n):
            move.wait()
        for ch in (range(n_down), range(n_down, n_ffn))[n]:
            if ch >= 4:
                red.stage(ch - 4, 1)
            begin(ch)
    weights_in().start()

    def pair(p, carry):
        lanes = pl.ds(pl.multiple_of(p * 2 * HD, 2 * HD), 2 * HD)
        attend_pair_back(n_dev, p, lanes, q, ko, kf, vo, vf, ids, lse, attn, gat, dq, own, far, me, core)
        for n in range(2):
            swap_far(p, n).start()
        for k in range(2):

            @pl.when(p == k)
            def _():
                for ch in range(n_ffn - 4 + 2 * k, n_ffn - 2 + 2 * k):
                    red.stage(ch, 1)

        return carry

    lax.fori_loop(0, pairs, pair, 0)

    for p in range(pairs):
        for n in range(2):
            swap_far(p, n).wait_recv()

    def joined_low(n):
        cat = jnp.concatenate([far_in[n, p] for p in range(pairs)], 1)
        return (own[n] + cat.astype(jnp.float32)).astype(jnp.bfloat16)

    def weight_grad(left, right, at):
        grad = plain_dot(left.T, right).astype(jnp.bfloat16)
        for j in range(4):
            p2[j, pl.ds(at * hidden, hidden), :] = grad[j * hidden : (j + 1) * hidden]

    def column_sum(low_grad):
        sums = jnp.sum(low_grad.astype(jnp.float32), 0, keepdims=True)
        turned = jnp.concatenate([sums[:, width // 2 :], sums[:, : width // 2]], 1)
        return jnp.where(side == 0, sums, turned)

    red.stage(0, 2)
    weight_grad(attn[...], gres[...].astype(jnp.bfloat16), 0)
    weight_grad(dq[...], x[...], 1)
    red.stage(n_ffn, 0)
    dk = joined_low(0)
    weight_grad(dk, x[...], 2)
    red.stage(n_ffn + 1, 0)
    red.stage(1, 2)
    dv = joined_low(1)
    weight_grad(dv, x[...], 3)
    for ch in range(n_ffn + 2, count):
        red.stage(ch, 0)
    red.stage(0, 3)
    total[0] = early[...]
    total[0, 0:1, :] = column_sum(dq[...])
    total[0, 1:2, :] = column_sum(dv)
    tiny.stage(0)
    weights_in().wait()
    matrix = lambda m: wt[m * width : (m + 1) * width]
    into = gres[...] + plain_dot(dq[...], matrix(0))
    into = into + plain_dot(dk, matrix(1))
    ig[...] = (into + plain_dot(dv, matrix(2))).astype(jnp.bfloat16)
    back[1].stage(0)
    for ch in range(n_ffn, count):
        red.stage(ch, 1)
    back[0].stage(1)

    events = []
    done = [(0, 2), (0, 3), (1, 2)]
    for ch in range(count):
        for s in range(2, 9):
            if (ch, s) not in done:
                events.append((10 + 8 * (ch + 1) + (0, 10, 18, 26, 34, 42, 51)[s - 2], red, (ch, s)))
    events += [(33 + 7 * n, tiny, (n,)) for n in range(1, 6)]
    events += [(68, back[1], (1,)), (106, back[0], (2,)), (123, back[1], (2,))]
    for _, who, what in sorted(events, key=lambda e: e[0]):
        who.stage(*what)
    for b in back:
        b.stage(3)
    for ch in range(count):
        red.finish(ch)
    tiny.finish()
    for p in range(pairs):
        for n in range(2):
            swap_far(p, n).wait_send()


def attend_pair_back(n_dev, p, lanes, q_ref, ko, kf, vo, vf, ids, lse_ref, attn, gat, dq, own, far, me, core):
    span = q_ref.shape[0]
    blocks = span // BLOCK
    lane = lax.broadcasted_iota(jnp.int32, (1, 2 * HD), 1) // HD
    q, g = q_ref[:, lanes], gat[:, lanes]
    weighted = (attn[:, lanes].astype(jnp.float32) * g.astype(jnp.float32)).T
    parts = ((ko[:, lanes], vo[:, lanes]), (kf[:, lanes], vf[:, lanes]))
    k_ts = [k.T for k, _ in parts]
    dks = [None, None]
    dvs = [None, None]
    dq_ts = []
    for h in range(2):
        rows = slice(h * HD, (h + 1) * HD)
        qh = (jnp.where(lane == h, q, 0.0) * 0.125).astype(jnp.bfloat16)
        gh = jnp.where(lane == h, g, 0.0).astype(jnp.bfloat16)
        delta = jnp.sum(weighted[rows], 0, keepdims=True)
        lse = lse_ref[p, h : h + 1, :]
        dq_t = None
        for at, (k, v) in enumerate(parts):
            bias = list_bias(ids, 2 * p + h, at == 1, me, core, n_dev, span)
            raw = back_dot(k, qh).reshape(blocks, BLOCK, span)
            raw = (raw + bias[:, None, :]).reshape(span, span)
            prob = jnp.exp(raw - lse)
            dprob = back_dot(v, gh)
            dscore = (prob * (dprob - delta)).astype(jnp.bfloat16)
            dv = plain_dot(prob.astype(jnp.bfloat16), gh)
            dk = plain_dot(dscore, qh)
            dvs[at] = dv if dvs[at] is None else dvs[at] + dv
            dks[at] = dk if dks[at] is None else dks[at] + dk
            piece = plain_dot(k_ts[at][rows], dscore)
            dq_t = piece if dq_t is None else dq_t + piece
        dq_ts.append(dq_t * 0.125)
    dq[:, lanes] = jnp.concatenate(dq_ts, 0).T.astype(jnp.bfloat16)
    for n, grads in enumerate((dks, dvs)):
        own[n, :, lanes] = grads[0]
        far[n, p] = grads[1].astype(jnp.bfloat16)


def tail(q, ko, kf, vo, vf, ids, lse, attn, gat, x, gres, early, normed, g_ffn, act, g_pre, low, wt, n_dev):
    span, width = q.shape
    rows = 256
    n_ffn = (act.shape[1] // 4 + width) // rows
    count = n_ffn + width // rows
    pairs = width // (2 * HD)
    vmem = pl.BlockSpec(memory_space=pltpu.VMEM)
    hbm = pl.BlockSpec(memory_space=pl.ANY)
    dma = pltpu.SemaphoreType.DMA
    landed = jax.ShapeDtypeStruct((n_dev, 2, 2 * BLOCK, width), jnp.bfloat16)
    low_buf = lambda *shape: pltpu.VMEM(shape + (width,), jnp.bfloat16)
    pair_buf = pltpu.VMEM((2, pairs, span, 2 * HD), jnp.bfloat16)
    return pl.pallas_call(
        partial(tail_kernel, n_dev),
        in_specs=[vmem] * 12 + [hbm] * 6,
        out_specs=[vmem, hbm, hbm, vmem],
        out_shape=[
            jax.ShapeDtypeStruct((count, rows, width), jnp.bfloat16),
            landed,
            landed,
            jax.ShapeDtypeStruct((6,) + early.shape, jnp.float32),
        ],
        scratch_shapes=[
            low_buf(n_ffn, 2, rows),
            low_buf(4, width),
            pltpu.VMEM(wt.shape, jnp.bfloat16),
            low_buf(count, 2, rows),
            low_buf(count, rows),
            pltpu.VMEM((count, rows // 2, width), jnp.float32),
            low_buf(count, rows),
            low_buf(count, rows),
            pltpu.VMEM((5,) + early.shape, jnp.float32),
            low_buf(span),
            pltpu.VMEM((2, span, width), jnp.float32),
            pair_buf,
            pair_buf,
            low_buf(span),
            dma((count, 7)),
            dma((count, 7)),
            dma((count, 2)),
            dma((count, 2)),
            dma((11,)),
            dma((pairs, 2)),
            dma((pairs, 2)),
            dma((2, n_dev + 2)),
            dma((2, n_dev + 2)),
            dma((2,)),
            dma((5,)),
            dma((5,)),
        ],
        compiler_params=pltpu.CompilerParams(
            collective_id=2, has_side_effects=True, vmem_limit_bytes=60 * 2**20
        ),
    )(q, ko, kf, vo, vf, ids, lse, attn, gat, x, gres, early, normed, g_ffn, act, g_pre, low, wt)


def norm_parts(resid):
    centre = resid - jnp.mean(resid, -1, keepdims=True)
    inverse = lax.rsqrt(jnp.mean(centre * centre, -1, keepdims=True) + norm_eps)
    return centre * inverse, inverse


def norm_back(grad, unit, inverse, gain):
    scaled = grad * gain
    pull = scaled - jnp.mean(scaled, -1, keepdims=True)
    pull = pull - unit * jnp.mean(scaled * unit, -1, keepdims=True)
    return pull * inverse, jnp.sum(grad * unit, 0), jnp.sum(grad, 0)


def whole_sequences(
    tokens,
    rand_blocks,
    query_weight,
    query_bias,
    key_weight,
    value_weight,
    value_bias,
    output_weight,
    output_bias,
    attn_gain,
    attn_shift,
    up_weight,
    up_bias,
    down_weight,
    down_bias,
    ffn_gain,
    ffn_shift,
    cotangent,
):
    seqs, rows, width = tokens.shape
    n_dev = lax.axis_size("seq")
    me = lax.axis_index("seq")
    t = lax.axis_index("tp")
    side, core = t // 2, t % 2
    n_blocks = rows // BLOCK * n_dev
    hidden = query_weight.shape[1]
    units = up_weight.shape[1]
    span = n_dev * BLOCK

    (
        x, q, k_own, k_far, v_own, v_far, attn_low, lse, ids, u_bias, wt, cot, wo, w_up, w_down,
    ) = enter(
        tokens, cotangent, rand_blocks.transpose(2, 3, 0, 1), query_weight.T, key_weight.T, value_weight.T,
        query_bias[None], value_bias[None], up_bias[None], output_weight, up_weight, down_weight, n_dev,
    )
    u_bias = u_bias.reshape(4 * units)
    branch = plain_dot(attn_low, wo) + output_bias
    unit_one, inverse_one = norm_parts(x.astype(jnp.float32) + branch)
    normed = unit_one * attn_gain + attn_shift
    normed_low = normed.astype(jnp.bfloat16)
    pre_act = plain_dot(normed_low, w_up) + u_bias
    cdf = 0.5 * (1.0 + lax.erf(pre_act * HALF_ROOT))
    act_low = (pre_act * cdf).astype(jnp.bfloat16)
    slope = (cdf + pre_act * (PDF_SCALE * jnp.exp(-0.5 * pre_act * pre_act))).astype(jnp.bfloat16)
    ffn = plain_dot(act_low, w_down) + down_bias
    unit_two, inverse_two = norm_parts(normed + ffn)
    out_low = (unit_two * ffn_gain + ffn_shift).astype(jnp.bfloat16)

    g_resid2, grad_ffngain, grad_ffnshift = norm_back(
        cot.astype(jnp.float32), unit_two, inverse_two, ffn_gain
    )
    g_ffn = g_resid2.astype(jnp.bfloat16)
    grad_downbias = jnp.sum(g_ffn.astype(jnp.float32), 0)
    g_pre = (back_dot(g_ffn, w_down) * slope.astype(jnp.float32)).astype(jnp.bfloat16)
    grad_upbias = jnp.sum(g_pre.astype(jnp.float32), 0)
    g_normed = g_resid2 + back_dot(g_pre, w_up)
    g_resid, grad_attngain, grad_attnshift = norm_back(g_normed, unit_one, inverse_one, attn_gain)
    g_branch = g_resid.astype(jnp.bfloat16)
    grad_obias = jnp.sum(g_branch.astype(jnp.float32), 0)
    g_attn = back_dot(g_branch, wo).astype(jnp.bfloat16)

    ups = grad_upbias.reshape(2, 2, units)
    ups = jnp.where(side == 0, ups, ups[::-1]).reshape(4, width)
    late = jnp.zeros((2, width), jnp.float32)
    lines = [grad_obias, grad_attngain, grad_attnshift, grad_downbias, grad_ffngain, grad_ffnshift]
    early = jnp.concatenate([late, ups, jnp.stack(lines), late, late], 0)
    sums, layer_output, input_out, small = tail(
        q, k_own, k_far, v_own, v_far, ids, lse, attn_low, g_attn, x, g_resid, early,
        normed_low, g_ffn, act_low, g_pre, out_low, wt.reshape(3 * width, width), n_dev,
    )
    small = small[5]

    def share(first, size):
        whole = small[first : first + 4 * size // width].reshape(4, size)
        return lax.dynamic_index_in_dim(whole, t, 0, False)

    sums = sums.astype(jnp.float32)
    half = units // sums.shape[1]
    g_down = sums[:half].reshape(units, width)
    g_up = sums[half : half + width // sums.shape[1]].reshape(width, units)
    rest = sums[half + width // sums.shape[1] :].reshape(4, hidden, width)
    g_o, g_q, g_k, g_v = rest
    return (
        layer_output.reshape(seqs, rows, width),
        input_out.astype(jnp.float32).reshape(seqs, rows, width),
        g_q.T,
        share(0, hidden),
        g_k.T,
        g_v.T,
        share(1, hidden),
        g_o,
        small[6],
        small[7],
        small[8],
        g_up,
        share(2, units),
        g_down,
        small[9],
        small[10],
        small[11],
    )


def per_device(tokens, *rest):
    seqs, rows, _ = tokens.shape
    n_dev = lax.axis_size("seq")
    if lax.axis_size("tp") == 4 and n_dev == 8 and seqs == 2 * n_dev and rows == 2 * BLOCK:
        return whole_sequences(tokens, *rest)
    return split_sequences(tokens, *rest)


def solution(mesh):
    placed = (
        P(None, "seq", None),
        P(None, None, "tp", None),
        P(None, "tp"),
        P("tp"),
        P(None, "tp"),
        P(None, "tp"),
        P("tp"),
        P("tp", None),
        P(),
        P(),
        P(),
        P(None, "tp"),
        P("tp"),
        P("tp", None),
        P(),
        P(),
        P(),
        P(None, "seq", None),
    )
    return jax.shard_map(
        per_device,
        mesh=mesh,
        in_specs=placed,
        out_specs=(
            P(None, "seq", None),
            P(None, "seq", None),
            P(None, "tp"),
            P("tp"),
            P(None, "tp"),
            P(None, "tp"),
            P("tp"),
            P("tp", None),
            P(),
            P(),
            P(),
            P(None, "tp"),
            P("tp"),
            P("tp", None),
            P(),
            P(),
            P(),
        ),
        check_vma=False,
    )
```

```python
from functools import partial

import jax
import jax.numpy as jnp
from jax import lax
from jax.sharding import PartitionSpec as P
from jax.experimental import pallas as pl
from jax.experimental.pallas import tpu as pltpu

HD = 64
BLOCK = 64


norm_eps = 1e-06
masked_score = -1e30
highest_precision = lax.Precision.HIGHEST


def with_halo(shard, sides, width):
    for axis, dim in sides:
        size, length = (lax.axis_size(axis), shard.shape[dim])
        up = [(i, (i + 1) % size) for i in range(size - 1)]
        down = [(j, i) for i, j in up]
        last = lax.slice_in_dim(shard, length - width, length, axis=dim)
        first = lax.slice_in_dim(shard, 0, width, axis=dim)
        before = lax.ppermute(last, axis, up)
        after = lax.ppermute(first, axis, down)
        shard = jnp.concatenate([before, shard, after], axis=dim)
    return shard


def joined(shard, axis, combine):
    everything = jax.tree.map(lambda part: lax.all_gather(part, axis), shard)
    first = jax.tree.map(lambda part: part[0], everything)

    def hop(k, so_far):
        return combine(so_far, jax.tree.map(lambda part: part[k], everything))

    return lax.fori_loop(1, lax.axis_size(axis), hop, first)


def layer_norm(resid, gain, shift):
    centre = resid - jnp.mean(resid, -1, keepdims=True)
    spread = jnp.mean(centre * centre, -1, keepdims=True)
    return centre * lax.rsqrt(spread + norm_eps) * gain + shift


def gelu_exact(values):
    return jax.nn.gelu(values, approximate=False)


def plain_dot(left, right):
    return jnp.dot(left, right, preferred_element_type=jnp.float32)


def rows_dot(left, right):
    return lax.dot_general(
        left, right, (((0,), (0,)), ((), ())), preferred_element_type=jnp.float32
    )


def back_dot(left, right):
    return lax.dot_general(
        left, right, (((1,), (1,)), ((), ())), preferred_element_type=jnp.float32
    )


def softmax_row_probs(scores):
    top_score = jnp.max(scores, -1, keepdims=True)
    expo = jnp.exp(scores - top_score)
    return expo / jnp.sum(expo, -1, keepdims=True)


def head_sum_fwd(pieces):
    return lax.psum(pieces, "tp")


def head_sum_back(pieces):
    return lax.psum(pieces, "tp")


def merge_rows(first, second):
    top_score = jnp.maximum(first[0], second[0])
    scale_one = jnp.exp(first[0] - top_score)
    scale_two = jnp.exp(second[0] - top_score)
    return (
        top_score,
        first[1] * scale_one + second[1] * scale_two,
        first[2] * scale_one[..., None] + second[2] * scale_two[..., None],
    )


def tile_plan(rand_blocks, my_index, n_dev, per_dev, seqs, heads):
    count = seqs * per_dev * heads * 3
    capacity = max(2, 2 * count // n_dev)
    requests = (
        rand_blocks.reshape(seqs, n_dev, per_dev, heads, 3)
        .transpose(1, 0, 2, 3, 4)
        .reshape(n_dev, count)
    )
    is_mine = requests // per_dev == my_index
    ranking = jnp.cumsum(is_mine.astype(jnp.int32), 1) - 1
    slot_ids = jnp.arange(capacity, dtype=jnp.int32)
    select = is_mine[:, None, :] & (ranking[:, None, :] == slot_ids[None, :, None])
    filled = jnp.any(select, 2)
    position = jnp.arange(count, dtype=jnp.int32)
    seq_of = position // (per_dev * heads * 3)
    head_of = position // 3 % heads
    tile_of = (seq_of[None, :] * per_dev + requests % per_dev) * heads + head_of[None, :]
    send_index = jnp.sum(jnp.where(select, tile_of[:, None, :], 0), 2)
    own_requests = lax.dynamic_slice_in_dim(rand_blocks, my_index * per_dev, per_dev, 1).reshape(
        count
    )
    own_owner = own_requests // per_dev
    onehot = (own_owner[:, None] == jnp.arange(n_dev, dtype=jnp.int32)[None, :]).astype(jnp.int32)
    own_rank = jnp.sum((jnp.cumsum(onehot, 0) - 1) * onehot, 1)
    recv_index = own_owner * capacity + own_rank
    return (capacity, send_index, filled, recv_index)


def pick_tiles(incoming, recv_index, seqs, per_dev, heads, block, hsize):
    stacked = incoming.reshape(-1, block, 2 * hsize)
    return jnp.take(stacked, recv_index, 0).reshape(seqs, per_dev, heads, 3, block, 2 * hsize)


def assemble(end_part, window_part, tile_part, seqs, per_dev, heads, block, hsize):
    ends_wide = jnp.broadcast_to(end_part[:, None], (seqs, per_dev, heads, 2 * block, hsize))
    return jnp.concatenate(
        [ends_wide, window_part, tile_part.reshape(seqs, per_dev, heads, 3 * block, hsize)], 3
    )


def split_sequences(
    tokens,
    rand_blocks,
    query_weight,
    query_bias,
    key_weight,
    value_weight,
    value_bias,
    output_weight,
    output_bias,
    attn_gain,
    attn_shift,
    up_weight,
    up_bias,
    down_weight,
    down_bias,
    ffn_gain,
    ffn_shift,
    cotangent,
):
    seqs, rows, width = tokens.shape
    block = BLOCK
    hsize = HD
    per_dev = rows // block
    n_dev = lax.axis_size("seq")
    my_index = lax.axis_index("seq")
    n_blocks = per_dev * n_dev
    heads = query_weight.shape[1] // hsize
    hidden = heads * hsize
    n_tok = seqs * rows
    is_first = my_index == 0
    is_last = my_index == n_dev - 1
    flat = tokens.reshape(n_tok, width)
    query_low = (plain_dot(flat, query_weight) + query_bias).astype(jnp.bfloat16)
    key_low = plain_dot(flat, key_weight).astype(jnp.bfloat16)
    value_low = (plain_dot(flat, value_weight) + value_bias).astype(jnp.bfloat16)
    keyval = jnp.concatenate([key_low, value_low], 1).reshape(seqs, rows, 2 * hidden)
    extended = with_halo(keyval, (("seq", 1),), block)
    windows = jnp.stack(
        [extended[:, offset * block : (offset + 3) * block] for offset in range(per_dev)], 1
    )
    windows = windows.reshape(seqs, per_dev, 3 * block, 2, heads, hsize)
    win_key = windows[:, :, :, 0].transpose(0, 1, 3, 2, 4)
    win_value = windows[:, :, :, 1].transpose(0, 1, 3, 2, 4)
    triple = jnp.concatenate([query_low.reshape(seqs, rows, hidden), keyval], 2).astype(jnp.float32)
    own_ends = jnp.stack(
        [
            jnp.where(is_first, triple[:, :block], 0.0),
            jnp.where(is_last, triple[:, rows - block :], 0.0),
        ],
        1,
    )
    ends = lax.psum(own_ends.astype(jnp.bfloat16), "seq").reshape(seqs, 2, block, 3, heads, hsize)
    end_query = ends[:, :, :, 0].transpose(0, 3, 1, 2, 4).reshape(seqs, heads, 2 * block, hsize)
    end_key = ends[:, :, :, 1].transpose(0, 3, 1, 2, 4).reshape(seqs, heads, 2 * block, hsize)
    end_value = ends[:, :, :, 2].transpose(0, 3, 1, 2, 4).reshape(seqs, heads, 2 * block, hsize)
    capacity, send_index, filled, recv_index = tile_plan(
        rand_blocks, my_index, n_dev, per_dev, seqs, heads
    )
    table = (
        keyval.reshape(seqs, per_dev, block, 2, heads, hsize)
        .transpose(0, 1, 4, 2, 3, 5)
        .reshape(seqs * per_dev * heads, block, 2 * hsize)
    )
    outgoing = jnp.take(table, send_index.reshape(-1), 0).reshape(n_dev, capacity, block, 2 * hsize)
    outgoing = jnp.where(filled[:, :, None, None], outgoing, jnp.zeros((), jnp.bfloat16))
    incoming = lax.all_to_all(outgoing, "seq", split_axis=0, concat_axis=0, tiled=True)
    tiles = pick_tiles(incoming, recv_index, seqs, per_dev, heads, block, hsize)
    q_blocks = query_low.reshape(seqs, per_dev, block, heads, hsize).transpose(0, 1, 3, 2, 4)
    keys_all = assemble(end_key, win_key, tiles[..., :hsize], seqs, per_dev, heads, block, hsize)
    values_all = assemble(
        end_value, win_value, tiles[..., hsize:], seqs, per_dev, heads, block, hsize
    )
    block_ids = my_index * per_dev + jnp.arange(per_dev, dtype=jnp.int32)
    slot_ids = jnp.arange(8 * block, dtype=jnp.int32) // block
    dropped = (slot_ids == 2)[None, :] & (block_ids == 1)[:, None] | (slot_ids == 4)[None, :] & (
        block_ids == n_blocks - 2
    )[:, None]
    unscaled_scores = (
        jnp.einsum("sbhqd,sbhkd->sbhqk", q_blocks, keys_all, preferred_element_type=jnp.float32)
        * 0.125
    )
    unscaled_scores = jnp.where(dropped[None, :, None, None, :], masked_score, unscaled_scores)
    weights = softmax_row_probs(unscaled_scores)
    sparse_attention = jnp.einsum(
        "sbhqk,sbhkd->sbhqd",
        weights,
        values_all.astype(jnp.float32),
        precision=highest_precision,
        preferred_element_type=jnp.float32,
    )
    key_local = key_low.reshape(seqs, rows, heads, hsize).transpose(0, 2, 1, 3)
    value_local = value_low.reshape(seqs, rows, heads, hsize).transpose(0, 2, 1, 3)
    end_raw = (
        jnp.einsum("shqd,shkd->shqk", end_query, key_local, preferred_element_type=jnp.float32)
        * 0.125
    )
    end_top = jnp.max(end_raw, -1)
    end_expo = jnp.exp(end_raw - end_top[..., None])
    end_total = jnp.sum(end_expo, -1)
    end_acc = jnp.einsum(
        "shqk,shkd->shqd",
        end_expo,
        value_local.astype(jnp.float32),
        precision=highest_precision,
        preferred_element_type=jnp.float32,
    )
    merged_top, merged_total, merged_acc = joined((end_top, end_total, end_acc), "seq", merge_rows)
    end_out = merged_acc / merged_total[..., None]
    end_lse = merged_top + jnp.log(merged_total)
    end_split = end_out.reshape(seqs, heads, 2, block, hsize)
    first_rows = block_ids == 0
    last_rows = block_ids == n_blocks - 1
    attn = jnp.where(
        first_rows[None, :, None, None, None], end_split[:, None, :, 0], sparse_attention
    )
    attn = jnp.where(last_rows[None, :, None, None, None], end_split[:, None, :, 1], attn)
    attn_low = attn.transpose(0, 1, 3, 2, 4).reshape(n_tok, hidden).astype(jnp.bfloat16)
    branch = head_sum_fwd(plain_dot(attn_low, output_weight)) + output_bias
    resid = flat.astype(jnp.float32) + branch
    normed = layer_norm(resid, attn_gain, attn_shift)
    normed_low = normed.astype(jnp.bfloat16)
    pre_act = plain_dot(normed_low, up_weight) + up_bias
    act_low = gelu_exact(pre_act).astype(jnp.bfloat16)
    ffn = head_sum_fwd(plain_dot(act_low, down_weight)) + down_bias
    resid_two = normed + ffn
    layer_output = (
        layer_norm(resid_two, ffn_gain, ffn_shift).astype(jnp.bfloat16).reshape(seqs, rows, width)
    )
    cot_flat = cotangent.reshape(n_tok, width).astype(jnp.float32)
    norm_two, pull_two = jax.vjp(layer_norm, resid_two, ffn_gain, ffn_shift)
    grad_resid2, grad_ffngain, grad_ffnshift = pull_two(cot_flat)
    grad_ffn = grad_resid2.astype(jnp.bfloat16)
    grad_downbias = jnp.sum(grad_ffn.astype(jnp.float32), 0)
    grad_downweight = rows_dot(act_low, grad_ffn)
    grad_act = back_dot(grad_ffn, down_weight)
    gelu_out, pull_gelu = jax.vjp(gelu_exact, pre_act)
    grad_pre = pull_gelu(grad_act)[0].astype(jnp.bfloat16)
    grad_upbias = jnp.sum(grad_pre.astype(jnp.float32), 0)
    grad_upweight = rows_dot(normed_low, grad_pre)
    grad_normed = grad_resid2 + head_sum_back(back_dot(grad_pre, up_weight))
    norm_one, pull_one = jax.vjp(layer_norm, resid, attn_gain, attn_shift)
    grad_resid, grad_attngain, grad_attnshift = pull_one(grad_normed)
    grad_branch = grad_resid.astype(jnp.bfloat16)
    grad_obias = jnp.sum(grad_branch.astype(jnp.float32), 0)
    grad_oweight = rows_dot(attn_low, grad_branch)
    grad_attn = back_dot(grad_branch, output_weight).astype(jnp.bfloat16)
    grad_heads = grad_attn.reshape(seqs, per_dev, block, heads, hsize).transpose(0, 1, 3, 2, 4)
    global_mask = (first_rows | last_rows)[None, :, None, None, None]
    grad_sparse = jnp.where(global_mask, jnp.zeros((), jnp.bfloat16), grad_heads)
    own_dout = jnp.stack(
        [
            jnp.where(is_first, grad_heads[:, 0].astype(jnp.float32), 0.0),
            jnp.where(is_last, grad_heads[:, per_dev - 1].astype(jnp.float32), 0.0),
        ],
        2,
    ).reshape(seqs, heads, 2 * block, hsize)
    own_delta = jnp.sum(own_dout * end_out, -1)
    end_dout, end_delta = lax.psum((own_dout, own_delta), "seq")
    end_dlow = end_dout.astype(jnp.bfloat16)
    end_prob = jnp.exp(end_raw - end_lse[..., None])
    end_dprob = jnp.einsum(
        "shqd,shkd->shqk", end_dlow, value_local, preferred_element_type=jnp.float32
    )
    end_dscore = (end_prob * (end_dprob - end_delta[..., None]) * 0.125).astype(jnp.bfloat16)
    end_dquery_part = jnp.einsum(
        "shqk,shkd->shqd", end_dscore, key_local, preferred_element_type=jnp.float32
    )
    local_dkey = jnp.einsum(
        "shqk,shqd->shkd", end_dscore, end_query, preferred_element_type=jnp.float32
    )
    local_dvalue = jnp.einsum(
        "shqk,shqd->shkd",
        end_prob,
        end_dout,
        precision=highest_precision,
        preferred_element_type=jnp.float32,
    )
    again = lax.all_to_all(outgoing, "seq", split_axis=0, concat_axis=0, tiled=True)
    back_tiles = pick_tiles(again, recv_index, seqs, per_dev, heads, block, hsize)
    keys_back = assemble(
        end_key, win_key, back_tiles[..., :hsize], seqs, per_dev, heads, block, hsize
    )
    values_back = assemble(
        end_value, win_value, back_tiles[..., hsize:], seqs, per_dev, heads, block, hsize
    )
    grad_prob = jnp.einsum(
        "sbhqd,sbhkd->sbhqk", grad_sparse, values_back, preferred_element_type=jnp.float32
    )
    row_delta = jnp.sum(weights * grad_prob, -1, keepdims=True)
    grad_score = (weights * (grad_prob - row_delta) * 0.125).astype(jnp.bfloat16)
    grad_qblocks = jnp.einsum(
        "sbhqk,sbhkd->sbhqd", grad_score, keys_back, preferred_element_type=jnp.float32
    )
    grad_keysall = jnp.einsum(
        "sbhqk,sbhqd->sbhkd", grad_score, q_blocks, preferred_element_type=jnp.float32
    )
    grad_valsall = jnp.einsum(
        "sbhqk,sbhqd->sbhkd",
        weights,
        grad_sparse.astype(jnp.float32),
        precision=highest_precision,
        preferred_element_type=jnp.float32,
    )
    end_dkey = jnp.sum(grad_keysall[:, :, :, : 2 * block], 1)
    end_dvalue = jnp.sum(grad_valsall[:, :, :, : 2 * block], 1)
    win_grad = jnp.stack(
        [
            grad_keysall[:, :, :, 2 * block : 5 * block].transpose(0, 1, 3, 2, 4),
            grad_valsall[:, :, :, 2 * block : 5 * block].transpose(0, 1, 3, 2, 4),
        ],
        3,
    ).reshape(seqs, per_dev, 3 * block, 2 * hidden)
    rand_grad = (
        jnp.concatenate(
            [
                grad_keysall[:, :, :, 5 * block :].reshape(seqs, per_dev, heads, 3, block, hsize),
                grad_valsall[:, :, :, 5 * block :].reshape(seqs, per_dev, heads, 3, block, hsize),
            ],
            5,
        )
        .reshape(-1, block, 2 * hsize)
        .astype(jnp.bfloat16)
    )
    ext_grad = jnp.zeros((seqs, rows + 2 * block, 2 * hidden), jnp.float32)
    for offset in range(per_dev):
        ext_grad = ext_grad.at[:, offset * block : (offset + 3) * block].add(win_grad[:, offset])
    rims = jnp.concatenate([ext_grad[:, :block], ext_grad[:, rows + block :]], 1)
    returned_rims = with_halo(rims.astype(jnp.bfloat16), (("seq", 1),), block).astype(rims.dtype)
    middle_zero = jnp.zeros((seqs, rows - 2 * block, 2 * hidden), jnp.float32)
    kv_grad = ext_grad[:, block : rows + block] + jnp.concatenate(
        [returned_rims[:, :block], middle_zero, returned_rims[:, 3 * block :]], 1
    )
    sent_back = (
        jnp.zeros((n_dev * capacity, block, 2 * hsize), jnp.bfloat16)
        .at[recv_index]
        .set(rand_grad)
        .reshape(n_dev, capacity, block, 2 * hsize)
    )
    arrived = lax.all_to_all(sent_back, "seq", split_axis=0, concat_axis=0, tiled=True)
    arrived = jnp.where(filled[:, :, None, None], arrived.astype(jnp.float32), 0.0)
    table_grad = (
        jnp.zeros((seqs * per_dev * heads, block, 2 * hsize), jnp.float32)
        .at[send_index.reshape(-1)]
        .add(arrived.reshape(-1, block, 2 * hsize))
    )
    kv_grad = kv_grad + table_grad.reshape(seqs, per_dev, heads, block, 2, hsize).transpose(
        0, 1, 3, 4, 2, 5
    ).reshape(seqs, rows, 2 * hidden)
    kv_grad = kv_grad + jnp.stack(
        [local_dkey.transpose(0, 2, 1, 3), local_dvalue.transpose(0, 2, 1, 3)], 2
    ).reshape(seqs, rows, 2 * hidden)
    end_dquery, end_dkey_all, end_dvalue_all = (
        lax.psum(end_dquery_part.astype(jnp.bfloat16), "seq").astype(jnp.float32),
        lax.psum(end_dkey.astype(jnp.bfloat16), "seq").astype(jnp.float32),
        lax.psum(end_dvalue.astype(jnp.bfloat16), "seq").astype(jnp.float32),
    )
    end_kv = jnp.stack(
        [end_dkey_all.transpose(0, 2, 1, 3), end_dvalue_all.transpose(0, 2, 1, 3)], 2
    ).reshape(seqs, 2 * block, 2 * hidden)
    kv_grad = kv_grad + jnp.concatenate(
        [
            jnp.where(is_first, end_kv[:, :block], 0.0),
            middle_zero,
            jnp.where(is_last, end_kv[:, block:], 0.0),
        ],
        1,
    )
    end_q = end_dquery.transpose(0, 2, 1, 3).reshape(seqs, 2 * block, hidden)
    query_zero = jnp.zeros((seqs, rows - 2 * block, hidden), jnp.float32)
    grad_query = grad_qblocks.transpose(0, 1, 3, 2, 4).reshape(seqs, rows, hidden)
    grad_query = grad_query + jnp.concatenate(
        [
            jnp.where(is_first, end_q[:, :block], 0.0),
            query_zero,
            jnp.where(is_last, end_q[:, block:], 0.0),
        ],
        1,
    )
    query_glow = grad_query.reshape(n_tok, hidden).astype(jnp.bfloat16)
    kv_glow = kv_grad.reshape(n_tok, 2 * hidden).astype(jnp.bfloat16)
    key_glow = kv_glow[:, :hidden]
    value_glow = kv_glow[:, hidden:]
    grad_qbias = jnp.sum(query_glow.astype(jnp.float32), 0)
    grad_vbias = jnp.sum(value_glow.astype(jnp.float32), 0)
    grad_qweight = rows_dot(flat, query_glow)
    grad_kweight = rows_dot(flat, key_glow)
    grad_vweight = rows_dot(flat, value_glow)
    into_tokens = (
        back_dot(query_glow, query_weight)
        + back_dot(key_glow, key_weight)
        + back_dot(value_glow, value_weight)
    )
    input_grad = (grad_resid + head_sum_back(into_tokens)).reshape(seqs, rows, width)
    totals = lax.psum(
        (
            grad_qweight,
            grad_qbias,
            grad_kweight,
            grad_vweight,
            grad_vbias,
            grad_oweight,
            grad_obias,
            grad_attngain,
            grad_attnshift,
            grad_upweight,
            grad_upbias,
            grad_downweight,
            grad_downbias,
            grad_ffngain,
            grad_ffnshift,
        ),
        "seq",
    )
    return (
        layer_output,
        input_grad,
        totals[0],
        totals[1],
        totals[2],
        totals[3],
        totals[4],
        totals[5],
        totals[6],
        totals[7],
        totals[8],
        totals[9],
        totals[10],
        totals[11],
        totals[12],
        totals[13],
        totals[14],
    )


HALF_ROOT = 0.7071067811865476
PDF_SCALE = 0.3989422804014327


MESH = pl.DeviceIdType.MESH


def place():
    me, t = lax.axis_index("seq"), lax.axis_index("tp")
    side, core = lax.div(t, 2), lax.rem(t, 2)
    return me, t, side, core


def tp_peer(side, core, bits):
    there = 1 - side if bits & 2 else side
    return there * 2 + (1 - core if bits & 1 else core)


def greet(peers):
    barrier = pltpu.get_barrier_semaphore()
    for peer in peers:
        pl.semaphore_signal(barrier, inc=1, device_id=peer, device_id_type=MESH)
    pl.semaphore_wait(barrier, len(peers))


def remote(src, dst, sends, recvs, at, peer):
    return pltpu.make_async_remote_copy(
        src_ref=src,
        dst_ref=dst,
        send_sem=sends.at[at],
        recv_sem=recvs.at[at],
        device_id=peer,
        device_id_type=MESH,
    )


class Piece:
    def __init__(self, at, bit, own, held, spots, sems):
        me, t, side, core = spots
        self.at, self.own, self.far = at, own, partial(held, 2 + core)
        mate, self.half = flip(me, bit)
        self.mate = (mate, t)
        self.near, self.across = (me, tp_peer(side, core, 1)), (me, tp_peer(side, core, 2))
        self.sems = sems
        self.then = []

    def move(self, n):
        h = 1 - self.half if n == 3 else self.half
        src = self.own(h) if n == 0 else self.far(h)
        peer = (self.across, self.mate, self.near, self.near)[n]
        return remote(src, self.far(h), *self.sems, (self.at, n), peer)

    def start(self):
        self.move(0).start()

    def pass_on(self):
        self.move(0).wait_recv()
        for piece in self.then:
            piece.start()
        self.move(1).start()
        self.move(2).start()

    def pass_side(self):
        self.move(1).wait_recv()
        self.move(3).start()

    def arrive(self):
        self.move(2).wait_recv()
        self.move(3).wait_recv()

    def sent(self):
        for n in range(4):
            self.move(n).wait_send()


def enter_kernel(
    n_dev, tok, cot, rand, wq, wk, wv, qb, vb, ub, wo, up, down,
    x, q, ko, kf, vo, vf, attn, lse, ids, ubs, wt_out, cot_out, wo_out, up_out, down_out,
    wt, qbs, vbs, ids_for, own_wo, own_up, own_down,
    tok_send, tok_recv, cot_send, cot_recv, p_send, p_recv, o_send, o_recv, s_send, s_recv, kv_send, kv_recv, local,
):
    spots = me, t, side, core = place()
    near = (me, tp_peer(side, core, 1))
    hidden, width = wq.shape
    units = down.shape[0]
    span = x.shape[0]
    heads = hidden // HD
    pairs = width // (2 * HD)
    part = hidden // 2
    n_part = units // 2 // part
    own_buf = (own_wo, own_up, own_down)

    holds = [(w, lambda j, m=m: wt.at[m, j]) for m, w in ((1, wk), (2, wv), (0, wq))]
    holds += [
        (wo, lambda j: wo_out.at[pl.ds(j * hidden, hidden), :]),
        (up, lambda j: up_out.at[:, pl.ds(j * units, units)]),
        (down, lambda j: down_out.at[pl.ds(j * units, units), :]),
    ]
    pieces = []
    for n, (ref, block) in enumerate(holds):
        for i in range(1 if n < 4 else n_part):
            count = 1 if n < 4 else n_part

            def rows(r, h, i=i, count=count):
                return r.at[pl.ds((h * count + i) * part, part), :]

            at = len(pieces)
            pieces.append(
                Piece(
                    at, (1, 2)[at % 2],
                    lambda h, ref=ref, rows=rows: rows(ref, h),
                    lambda j, h, block=block, rows=rows: rows(block(j), h),
                    spots, (p_send, p_recv),
                )
            )

    ahead = 4
    for piece, later in zip(pieces, pieces[ahead:]):
        piece.then = [later]

    def own_near(n):
        return remote(holds[n][0], holds[n][1](core), o_send, o_recv, n, near)

    def own_here(n):
        src = holds[n][0] if n < 3 else own_buf[n - 3]
        return pltpu.make_async_copy(src, holds[n][1](core), local.at[n])

    def own_in(n):
        return pltpu.make_async_copy(holds[n][0], own_buf[n - 3], local.at[6 + n])

    def spread(src, dst, sends, recvs):
        return [
            remote(
                src.at[2 * lax.rem(me + k, n_dev) + side, pl.ds(core * BLOCK, BLOCK), :],
                dst.at[pl.ds(k * BLOCK, BLOCK), :],
                sends, recvs, k - 1, (lax.rem(me + k, n_dev), t),
            )
            for k in range(1, n_dev)
        ]

    def kept(n):
        src, dst = ((tok, x), (cot, cot_out))[n]
        return pltpu.make_async_copy(
            src.at[2 * me + side, pl.ds(core * BLOCK, BLOCK), :], dst.at[pl.ds(0, BLOCK), :], local.at[12 + n]
        )

    def shared(bits, which=(0, 1, 2, 3)):
        slot = (bits & 2) + core
        to = tp_peer(side, core, bits)
        moves = (
            (qbs.at[core], qbs.at[slot]), (vbs.at[core], vbs.at[slot]), (ubs.at[core], ubs.at[slot]),
            (ids_for.at[to], ids.at[pl.ds(slot * heads, heads)]),
        )
        return [
            remote(*moves[n], s_send, s_recv, (bits - 1, n), (me, to)) for n in which
        ]

    greet(all_peers(n_dev, *spots) + [(me, tp_peer(side, core, 3))])
    for move in spread(tok, x, tok_send, tok_recv):
        move.start()
    for piece in pieces[:ahead]:
        piece.start()
    kept(0).start()
    for n in range(3):
        own_near(n).start()
        own_here(n).start()
    for ref, rows in ((qb, qbs), (vb, vbs), (ub, ubs)):
        rows[core] = ref[...].reshape(1, ref.shape[0])
    for bits in (1, 2, 3):
        for move in shared(bits, (0, 1, 2)):
            move.start()
    for n in range(3, 6):
        own_in(n).start()

    lane = lax.broadcasted_iota(jnp.int32, (1, span), 1)
    for y in range(2):
        for c in range(2):
            block = 2 * lax.rem(me - lane // BLOCK + n_dev, n_dev) + c
            for h in range(heads):
                for r in range(3):
                    line = rand[h, r, pl.ds(2 * me + y, 1), :]
                    row = jnp.zeros((1, span), jnp.int32)
                    for b in range(c, 2 * n_dev, 2):
                        row = jnp.where(block == b, line[:, b : b + 1], row)
                    ids_for[2 * y + c, h, r : r + 1, :] = row
    ids[pl.ds(core * heads, heads)] = ids_for[t]
    for bits in (1, 2, 3):
        shared(bits, (3,))[0].start()

    def advance(n):
        pieces[n].pass_on()
        if n:
            pieces[n - 1].pass_side()

    for n in range(4):
        advance(n)
    for move in spread(tok, x, tok_send, tok_recv):
        move.wait_recv()
    kept(0).wait()
    for move in spread(cot, cot_out, cot_send, cot_recv):
        move.start()
    kept(1).start()
    for n in range(3, 6):
        own_near(n).start()
        own_in(n).wait()
        own_here(n).start()
    for bits in (1, 2, 3):
        for move in shared(bits):
            move.wait_recv()

    def bias_of(ref):
        return jnp.concatenate([ref[j] for j in range(4)], 1)

    def project(n, m):
        own_near(n).wait_recv()
        own_here(n).wait()
        pieces[n].arrive()
        return back_dot(x[...], wt[m].reshape(width, width))

    def swap_kv(n):
        src, dst = ((ko, kf), (vo, vf))[n]
        return remote(src, dst, kv_send, kv_recv, n, near)

    ko[...] = project(0, 1).astype(jnp.bfloat16)
    swap_kv(0).start()
    vo[...] = (project(1, 2) + bias_of(vbs)).astype(jnp.bfloat16)
    swap_kv(1).start()
    advance(4)
    q[...] = (project(2, 0) + bias_of(qbs)).astype(jnp.bfloat16)
    keep = pltpu.make_async_copy(wt, wt_out, local.at[14])
    keep.start()
    advance(5)
    swap_kv(0).wait_recv()
    swap_kv(1).wait_recv()

    def pair(p, carry):
        lanes = pl.ds(pl.multiple_of(p * 2 * HD, 2 * HD), 2 * HD)
        attend_pair(n_dev, p, lanes, q, ko, kf, vo, vf, ids, attn, lse, me, core)
        for k in range(3):

            @pl.when(p == 2 * k + 1)
            def _():
                advance(6 + k)

        return carry

    lax.fori_loop(0, pairs, pair, 0)
    for n in range(9, len(pieces)):
        advance(n)
    pieces[-1].pass_side()
    for n in range(3, len(pieces)):
        pieces[n].arrive()
    for move in spread(cot, cot_out, cot_send, cot_recv):
        move.wait()
    kept(1).wait()
    keep.wait()
    for move in spread(tok, x, tok_send, tok_recv):
        move.wait_send()
    for piece in pieces:
        piece.sent()
    for n in range(6):
        own_near(n).wait_send()
        if n > 2:
            own_near(n).wait_recv()
            own_here(n).wait()
    for bits in (1, 2, 3):
        for move in shared(bits):
            move.wait_send()
    for n in range(2):
        swap_kv(n).wait_send()


def enter(tok, cot, rand, wq, wk, wv, qb, vb, ub, wo, up, down, n_dev):
    hidden, width = wq.shape
    units = down.shape[0]
    span = n_dev * BLOCK
    heads = hidden // HD
    pieces = 4 + 2 * (units // hidden)
    vmem = pl.BlockSpec(memory_space=pltpu.VMEM)
    hbm = pl.BlockSpec(memory_space=pl.ANY)
    shape = lambda dtype, *dims: jax.ShapeDtypeStruct(dims, dtype)
    low = partial(shape, jnp.bfloat16)
    dma = pltpu.SemaphoreType.DMA
    return pl.pallas_call(
        partial(enter_kernel, n_dev),
        in_specs=[hbm, hbm, vmem] + [hbm] * 3 + [vmem] * 3 + [hbm] * 3,
        out_specs=[vmem] * 10 + [hbm] * 5,
        out_shape=[low(span, width)] * 7
        + [
            shape(jnp.float32, 2 * heads, 2, span),
            shape(jnp.int32, 4 * heads, 3, span),
            shape(jnp.float32, 4, 1, units),
            low(3, 4, hidden, width),
            low(span, width),
            low(width, width),
            low(width, 4 * units),
            low(4 * units, width),
        ],
        scratch_shapes=[
            pltpu.VMEM((3, 4, hidden, width), jnp.bfloat16),
            pltpu.VMEM((4, 1, hidden), jnp.float32),
            pltpu.VMEM((4, 1, hidden), jnp.float32),
            pltpu.VMEM((4, heads, 3, span), jnp.int32),
            pltpu.VMEM(wo.shape, jnp.bfloat16),
            pltpu.VMEM(up.shape, jnp.bfloat16),
            pltpu.VMEM(down.shape, jnp.bfloat16),
            dma((n_dev - 1,)),
            dma((n_dev - 1,)),
            dma((n_dev - 1,)),
            dma((n_dev - 1,)),
            dma((pieces, 4)),
            dma((pieces, 4)),
            dma((6,)),
            dma((6,)),
            dma((3, 4)),
            dma((3, 4)),
            dma((2,)),
            dma((2,)),
            dma((15,)),
        ],
        compiler_params=pltpu.CompilerParams(
            collective_id=0, has_side_effects=True, vmem_limit_bytes=56 * 2**20
        ),
    )(tok, cot, rand, wq, wk, wv, qb, vb, ub, wo, up, down)


def list_bias(ids_ref, h, key_shift, me, core, n_dev, span):
    n_blocks = 2 * n_dev
    row = lax.broadcasted_iota(jnp.int32, (n_dev, span), 0)
    lane = lax.broadcasted_iota(jnp.int32, (n_dev, span), 1)
    wrap = lambda i: lax.rem(me - i + n_dev, n_dev)
    k = 2 * wrap(row) + (1 - core if key_shift else core)
    b = 2 * wrap(lane // BLOCK) + core
    one = lambda flag: jnp.where(flag, 1.0, 0.0)
    count = (
        one(k == 0)
        + one(k == n_blocks - 1)
        + one((k == b - 1) & (b != 1))
        + one(k == b)
        + one((k == b + 1) & (b != n_blocks - 2))
    )
    for r in range(3):
        count = count + one(ids_ref[h, r : r + 1, :] == k)
    count = jnp.where((b == 0) | (b == n_blocks - 1), 1.0, count)
    return jnp.where(count > 0.5, jnp.log(jnp.maximum(count, 1.0)), masked_score)


def attend_pair(n_dev, p, lanes, q_ref, ko, kf, vo, vf, ids, attn, lse, me, core):
    span = q_ref.shape[0]
    blocks = span // BLOCK
    lane = lax.broadcasted_iota(jnp.int32, (1, 2 * HD), 1) // HD
    q = q_ref[:, lanes]
    keys = (ko[:, lanes], kf[:, lanes])
    values = (vo[:, lanes].T, vf[:, lanes].T)
    outs = []
    for h in range(2):
        qh = (jnp.where(lane == h, q, 0.0) * 0.125).astype(jnp.bfloat16)
        scores = []
        for far in range(2):
            bias = list_bias(ids, 2 * p + h, far == 1, me, core, n_dev, span)
            raw = back_dot(keys[far], qh).reshape(blocks, BLOCK, span)
            scores.append((raw + bias[:, None, :]).reshape(span, span))
        top = jnp.maximum(*(jnp.max(s, 0, keepdims=True) for s in scores))
        expo = [jnp.exp(s - top) for s in scores]
        total = sum(jnp.sum(e, 0, keepdims=True) for e in expo)
        rows = slice(h * HD, (h + 1) * HD)
        acc = sum(plain_dot(v[rows], e.astype(jnp.bfloat16)) for v, e in zip(values, expo))
        outs.append(acc / total)
        lse[p, h : h + 1, :] = top + jnp.log(total)
    attn[:, lanes] = jnp.concatenate(outs, 0).T.astype(jnp.bfloat16)


def flip(index, bit):
    value = lax.rem(lax.div(index, bit), 2)
    return index + bit - 2 * bit * value, value


class Reduction:
    def __init__(self, away, mine, spots, bufs, sems):
        self.away, self.mine = away, mine
        self.jobs, self.ahead = [], 3
        self.me, self.t, self.side, self.core = spots
        self.b0, self.b1, self.acc, self.halves, self.got, self.f = bufs
        self.send, self.recv, self.send0, self.recv0 = sems
        self.near = (self.me, tp_peer(self.side, self.core, 1))
        self.across = (self.me, tp_peer(self.side, self.core, 2))
        self.mates = []
        self.bits = []
        for bit in (1, 2, 4):
            mate, value = flip(self.me, bit)
            self.mates.append((mate, self.t))
            self.bits.append(value)

    def span(self, ref, start, size):
        return ref.at[pl.ds(pl.multiple_of(start, 16), size), :]

    def rows(self, depth):
        start, size, inner = 0, self.f.shape[1], 0
        for level in range(depth):
            size //= 2
            start = start + self.bits[level] * size
            inner = inner + (self.bits[level] * size if level else 0)
        return start, inner, size

    def first(self, ch):
        return [
            remote(self.away(ch, y), self.b0.at[ch, y], self.send0, self.recv0, (ch, y), self.near)
            for y in range(2)
        ]

    def over_y(self, ch):
        return remote(self.mine(ch, 1), self.b1.at[ch], self.send, self.recv, (ch, 0), self.across)

    def next_y(self, job):
        if job + self.ahead < len(self.jobs):
            self.jobs[job + self.ahead]().start()

    def halving(self, ch, level):
        size = self.rows(level + 1)[2]
        return remote(
            self.halves.at[ch, pl.ds(size, size), :],
            self.got.at[ch, pl.ds(size, size), :],
            self.send, self.recv, (ch, 1 + level), self.mates[level],
        )

    def gather(self, ch, level):
        start, _, size = self.rows(level + 1)
        held = self.span(self.f.at[ch], start, size)
        return remote(held, held, self.send, self.recv, (ch, 4 + level), self.mates[level])

    def stage(self, ch, s):
        full = jnp.float32
        if s == 0:
            for move in self.first(ch):
                move.start()
        elif s == 1:
            for move in self.first(ch):
                move.wait()
            out = self.mine(ch, 1)
            out[...] = (out[...].astype(full) + self.b0[ch, 1].astype(full)).astype(jnp.bfloat16)
            if ch < self.ahead:
                self.over_y(ch).start()
        elif s == 2:
            self.over_y(ch).wait_recv()
            self.next_y(ch)
            size = self.rows(1)[2]

            def total(start):
                terms = (self.mine(ch, 0), self.b0.at[ch, 0], self.b1.at[ch])
                one, two, three = (self.span(ref, start, size)[...].astype(full) for ref in terms)
                return one + two + three

            self.halves[ch, pl.ds(size, size), :] = total((1 - self.bits[0]) * size).astype(jnp.bfloat16)
            self.halving(ch, 0).start()
            self.acc[ch] = total(self.bits[0] * size)
        elif s <= 5:
            level = s - 3
            _, inner, size = self.rows(level + 1)
            self.halving(ch, level).wait_recv()
            total = self.span(self.acc.at[ch], inner, size)[...] + self.got[ch, pl.ds(size, size), :].astype(full)
            if s == 5:
                self.span(self.f.at[ch], self.rows(3)[0], size)[...] = total.astype(jnp.bfloat16)
                self.gather(ch, 2).start()
            else:
                self.span(self.acc.at[ch], inner, size)[...] = total
                small = size // 2
                other = self.span(self.acc.at[ch], inner + (1 - self.bits[level + 1]) * small, small)
                self.halves[ch, pl.ds(small, small), :] = other[...].astype(jnp.bfloat16)
                self.halving(ch, level + 1).start()
        elif s <= 7:
            self.gather(ch, 8 - s).wait_recv()
            self.gather(ch, 7 - s).start()
        else:
            self.gather(ch, 0).wait_recv()

    def finish(self, ch):
        self.over_y(ch).wait_send()
        for level in range(3):
            self.halving(ch, level).wait_send()
            self.gather(ch, level).wait_send()


class Return:
    def __init__(self, at, n_dev, src, dst, spots, sems):
        self.at, self.n_dev, self.src, self.dst = at, n_dev, src, dst
        self.me, self.t, self.side, self.core = spots
        self.send, self.recv, self.local = sems
        self.near = (self.me, tp_peer(self.side, self.core, 1))
        self.across = (self.me, tp_peer(self.side, self.core, 2))

    def block(self, s, side):
        return self.dst.at[s, side, pl.ds(self.core * BLOCK, BLOCK), :]

    def keep(self):
        return pltpu.make_async_copy(
            self.src.at[pl.ds(0, BLOCK), :], self.block(self.me, self.side), self.local.at[self.at]
        )

    def out(self, k):
        to = lax.rem(self.me - k + self.n_dev, self.n_dev)
        return remote(
            self.src.at[pl.ds(k * BLOCK, BLOCK), :], self.block(self.me, self.side),
            self.send, self.recv, (self.at, k - 1), (to, self.t),
        )

    def pass_on(self, n):
        side = 1 - self.side if n == 2 else self.side
        held = self.dst.at[:, side, pl.ds(self.core * BLOCK, BLOCK), :]
        peer = self.across if n == 0 else self.near
        return remote(held, held, self.send, self.recv, (self.at, self.n_dev - 1 + n), peer)

    def stage(self, s):
        if s == 0:
            self.keep().start()
            for k in range(1, self.n_dev):
                self.out(k).start()
        elif s == 1:
            self.keep().wait()
            for k in range(1, self.n_dev):
                self.out(k).wait_recv()
            self.pass_on(1).start()
        elif s == 2:
            self.pass_on(0).wait_recv()
            self.then()
            self.pass_on(2).start()
        else:
            for k in range(1, self.n_dev):
                self.out(k).wait_send()
            self.pass_on(0).wait_send()
            self.pass_on(1).wait()
            self.pass_on(2).wait()


class SmallSum:
    def __init__(self, out, came, spots, sems):
        self.out, self.came = out, came
        me, t, side, core = spots
        self.send, self.recv = sems
        self.peers = [(me, tp_peer(side, core, 1)), (me, tp_peer(side, core, 2))]
        self.peers += [(flip(me, bit)[0], t) for bit in (1, 2, 4)]

    def move(self, n):
        held = self.out.at[n]
        return remote(held, self.came.at[n], self.send, self.recv, n, self.peers[n])

    def stage(self, n):
        if n:
            self.move(n - 1).wait_recv()
            self.out[n] = self.out[n - 1] + self.came[n - 1]
        if n < len(self.peers):
            self.move(n).start()

    def finish(self):
        for n in range(len(self.peers)):
            self.move(n).wait_send()


def all_peers(n_dev, me, t, side, core):
    return [(lax.rem(me + k, n_dev), t) for k in range(1, n_dev)] + [
        (me, tp_peer(side, core, bits)) for bits in (1, 2)
    ]


def tail_kernel(
    n_dev, q, ko, kf, vo, vf, ids, lse, attn, gat, x, gres, early, normed, g_ffn, act, g_pre, low, wt_hbm,
    f, out, iout, total,
    load, p2, wt, b0, b1, acc, halves, got, came, dq, own, far, far_in, ig,
    send, recv, send0, recv0, local, x_send, x_recv, r_send, r_recv, r_local, s_send, s_recv,
):
    spots = me, t, side, core = place()
    span, width = q.shape
    units, hidden = act.shape[1] // 4, width // 4
    rows = f.shape[1]
    n_down = units // rows
    n_ffn = n_down + width // rows
    count = f.shape[0]
    pairs = width // (2 * HD)
    near = (me, tp_peer(side, core, 1))

    def own_rows(ch, block):
        return p2.at[block, pl.ds((ch - n_ffn) * rows, rows), :]

    def away(ch, y):
        return halves.at[2 * (ch % 4) + y] if ch < n_ffn else own_rows(ch, 2 * y + 1 - core)

    def mine(ch, y):
        return load.at[ch, y] if ch < n_ffn else own_rows(ch, 2 * y + core)

    red = Reduction(away, mine, spots, (b0, b1, acc, halves, got, f), (send, recv, send0, recv0))
    back = [
        Return(n, n_dev, src, dst, spots, (r_send, r_recv, r_local))
        for n, (src, dst) in enumerate(((low, out), (ig, iout)))
    ]
    tiny = SmallSum(total, came, spots, (s_send, s_recv))

    def loads(n):
        src = (act, g_pre)[n]
        for j in range(4):
            dst = (p2.at[j, pl.ds(0, span), :], wt.at[pl.ds(j * span, span), :])[n]
            yield pltpu.make_async_copy(src.at[:, pl.ds(j * units, units)], dst, local.at[4 * n + j])
        yield pltpu.make_async_copy((g_ffn, normed)[n], (ig, dq)[n], local.at[9 + n])

    def weights_in():
        return pltpu.make_async_copy(wt_hbm, wt, local.at[8])

    def ffn_grad(ch, block):
        if ch < n_down:
            left, right = p2[block, 0:span, ch * rows : (ch + 1) * rows], ig[...]
        else:
            left = dq[:, (ch - n_down) * rows : (ch - n_down + 1) * rows]
            right = wt[pl.ds(pl.multiple_of(block * span, span), span), :]
        return plain_dot(left.T, right).astype(jnp.bfloat16)

    def swap_far(p, n):
        return remote(far.at[n, p], far_in.at[n, p], x_send, x_recv, (p, n), near)

    red.jobs = [partial(red.over_y, ch) for ch in range(count)]
    red.jobs += [partial(b.pass_on, 0) for b in back]
    back[0].then, back[1].then = partial(red.next_y, count), partial(red.next_y, count + 1)

    def begin(ch):
        for y in range(2):
            away(ch, y)[...] = ffn_grad(ch, 2 * y + 1 - core)
        red.stage(ch, 0)
        for y in range(2):
            load[ch, y] = ffn_grad(ch, 2 * y + core)

    for n in range(2):
        for move in loads(n):
            move.start()
    greet(all_peers(n_dev, *spots))
    back[0].stage(0)
    for n in range(2):
        for move in loads(n):
            move.wait()
        for ch in (range(n_down), range(n_down, n_ffn))[n]:
            if ch >= 4:
                red.stage(ch - 4, 1)
            begin(ch)
    weights_in().start()

    def pair(p, carry):
        lanes = pl.ds(pl.multiple_of(p * 2 * HD, 2 * HD), 2 * HD)
        attend_pair_back(n_dev, p, lanes, q, ko, kf, vo, vf, ids, lse, attn, gat, dq, own, far, me, core)
        for n in range(2):
            swap_far(p, n).start()
        for k in range(2):

            @pl.when(p == k)
            def _():
                for ch in range(n_ffn - 4 + 2 * k, n_ffn - 2 + 2 * k):
                    red.stage(ch, 1)

        return carry

    lax.fori_loop(0, pairs, pair, 0)

    for p in range(pairs):
        for n in range(2):
            swap_far(p, n).wait_recv()

    def joined_low(n):
        cat = jnp.concatenate([far_in[n, p] for p in range(pairs)], 1)
        return (own[n] + cat.astype(jnp.float32)).astype(jnp.bfloat16)

    def weight_grad(left, right, at):
        grad = plain_dot(left.T, right).astype(jnp.bfloat16)
        for j in range(4):
            p2[j, pl.ds(at * hidden, hidden), :] = grad[j * hidden : (j + 1) * hidden]

    def column_sum(low_grad):
        sums = jnp.sum(low_grad.astype(jnp.float32), 0, keepdims=True)
        turned = jnp.concatenate([sums[:, width // 2 :], sums[:, : width // 2]], 1)
        return jnp.where(side == 0, sums, turned)

    red.stage(0, 2)
    weight_grad(attn[...], gres[...].astype(jnp.bfloat16), 0)
    weight_grad(dq[...], x[...], 1)
    red.stage(n_ffn, 0)
    dk = joined_low(0)
    weight_grad(dk, x[...], 2)
    red.stage(n_ffn + 1, 0)
    red.stage(1, 2)
    dv = joined_low(1)
    weight_grad(dv, x[...], 3)
    for ch in range(n_ffn + 2, count):
        red.stage(ch, 0)
    red.stage(0, 3)
    total[0] = early[...]
    total[0, 0:1, :] = column_sum(dq[...])
    total[0, 1:2, :] = column_sum(dv)
    tiny.stage(0)
    weights_in().wait()
    matrix = lambda m: wt[m * width : (m + 1) * width]
    into = gres[...] + plain_dot(dq[...], matrix(0))
    into = into + plain_dot(dk, matrix(1))
    ig[...] = (into + plain_dot(dv, matrix(2))).astype(jnp.bfloat16)
    back[1].stage(0)
    for ch in range(n_ffn, count):
        red.stage(ch, 1)
    back[0].stage(1)

    events = []
    done = [(0, 2), (0, 3), (1, 2)]
    for ch in range(count):
        for s in range(2, 9):
            if (ch, s) not in done:
                events.append((10 + 8 * (ch + 1) + (0, 10, 18, 26, 34, 42, 51)[s - 2], red, (ch, s)))
    events += [(33 + 7 * n, tiny, (n,)) for n in range(1, 6)]
    events += [(68, back[1], (1,)), (106, back[0], (2,)), (123, back[1], (2,))]
    for _, who, what in sorted(events, key=lambda e: e[0]):
        who.stage(*what)
    for b in back:
        b.stage(3)
    for ch in range(count):
        red.finish(ch)
    tiny.finish()
    for p in range(pairs):
        for n in range(2):
            swap_far(p, n).wait_send()


def attend_pair_back(n_dev, p, lanes, q_ref, ko, kf, vo, vf, ids, lse_ref, attn, gat, dq, own, far, me, core):
    span = q_ref.shape[0]
    blocks = span // BLOCK
    lane = lax.broadcasted_iota(jnp.int32, (1, 2 * HD), 1) // HD
    q, g = q_ref[:, lanes], gat[:, lanes]
    weighted = (attn[:, lanes].astype(jnp.float32) * g.astype(jnp.float32)).T
    parts = ((ko[:, lanes], vo[:, lanes]), (kf[:, lanes], vf[:, lanes]))
    k_ts = [k.T for k, _ in parts]
    dks = [None, None]
    dvs = [None, None]
    dq_ts = []
    for h in range(2):
        rows = slice(h * HD, (h + 1) * HD)
        qh = (jnp.where(lane == h, q, 0.0) * 0.125).astype(jnp.bfloat16)
        gh = jnp.where(lane == h, g, 0.0).astype(jnp.bfloat16)
        delta = jnp.sum(weighted[rows], 0, keepdims=True)
        lse = lse_ref[p, h : h + 1, :]
        dq_t = None
        for at, (k, v) in enumerate(parts):
            bias = list_bias(ids, 2 * p + h, at == 1, me, core, n_dev, span)
            raw = back_dot(k, qh).reshape(blocks, BLOCK, span)
            raw = (raw + bias[:, None, :]).reshape(span, span)
            prob = jnp.exp(raw - lse)
            dprob = back_dot(v, gh)
            dscore = (prob * (dprob - delta)).astype(jnp.bfloat16)
            dv = plain_dot(prob.astype(jnp.bfloat16), gh)
            dk = plain_dot(dscore, qh)
            dvs[at] = dv if dvs[at] is None else dvs[at] + dv
            dks[at] = dk if dks[at] is None else dks[at] + dk
            piece = plain_dot(k_ts[at][rows], dscore)
            dq_t = piece if dq_t is None else dq_t + piece
        dq_ts.append(dq_t * 0.125)
    dq[:, lanes] = jnp.concatenate(dq_ts, 0).T.astype(jnp.bfloat16)
    for n, grads in enumerate((dks, dvs)):
        own[n, :, lanes] = grads[0]
        far[n, p] = grads[1].astype(jnp.bfloat16)


def tail(q, ko, kf, vo, vf, ids, lse, attn, gat, x, gres, early, normed, g_ffn, act, g_pre, low, wt, n_dev):
    span, width = q.shape
    rows = 256
    n_ffn = (act.shape[1] // 4 + width) // rows
    count = n_ffn + width // rows
    pairs = width // (2 * HD)
    vmem = pl.BlockSpec(memory_space=pltpu.VMEM)
    hbm = pl.BlockSpec(memory_space=pl.ANY)
    dma = pltpu.SemaphoreType.DMA
    landed = jax.ShapeDtypeStruct((n_dev, 2, 2 * BLOCK, width), jnp.bfloat16)
    low_buf = lambda *shape: pltpu.VMEM(shape + (width,), jnp.bfloat16)
    pair_buf = pltpu.VMEM((2, pairs, span, 2 * HD), jnp.bfloat16)
    return pl.pallas_call(
        partial(tail_kernel, n_dev),
        in_specs=[vmem] * 12 + [hbm] * 6,
        out_specs=[vmem, hbm, hbm, vmem],
        out_shape=[
            jax.ShapeDtypeStruct((count, rows, width), jnp.bfloat16),
            landed,
            landed,
            jax.ShapeDtypeStruct((6,) + early.shape, jnp.float32),
        ],
        scratch_shapes=[
            low_buf(n_ffn, 2, rows),
            low_buf(4, width),
            pltpu.VMEM(wt.shape, jnp.bfloat16),
            low_buf(count, 2, rows),
            low_buf(count, rows),
            pltpu.VMEM((count, rows // 2, width), jnp.float32),
            low_buf(count, rows),
            low_buf(count, rows),
            pltpu.VMEM((5,) + early.shape, jnp.float32),
            low_buf(span),
            pltpu.VMEM((2, span, width), jnp.float32),
            pair_buf,
            pair_buf,
            low_buf(span),
            dma((count, 7)),
            dma((count, 7)),
            dma((count, 2)),
            dma((count, 2)),
            dma((11,)),
            dma((pairs, 2)),
            dma((pairs, 2)),
            dma((2, n_dev + 2)),
            dma((2, n_dev + 2)),
            dma((2,)),
            dma((5,)),
            dma((5,)),
        ],
        compiler_params=pltpu.CompilerParams(
            collective_id=2, has_side_effects=True, vmem_limit_bytes=60 * 2**20
        ),
    )(q, ko, kf, vo, vf, ids, lse, attn, gat, x, gres, early, normed, g_ffn, act, g_pre, low, wt)


def norm_parts(resid):
    centre = resid - jnp.mean(resid, -1, keepdims=True)
    inverse = lax.rsqrt(jnp.mean(centre * centre, -1, keepdims=True) + norm_eps)
    return centre * inverse, inverse


def norm_back(grad, unit, inverse, gain):
    scaled = grad * gain
    pull = scaled - jnp.mean(scaled, -1, keepdims=True)
    pull = pull - unit * jnp.mean(scaled * unit, -1, keepdims=True)
    return pull * inverse, jnp.sum(grad * unit, 0), jnp.sum(grad, 0)


def whole_sequences(
    tokens,
    rand_blocks,
    query_weight,
    query_bias,
    key_weight,
    value_weight,
    value_bias,
    output_weight,
    output_bias,
    attn_gain,
    attn_shift,
    up_weight,
    up_bias,
    down_weight,
    down_bias,
    ffn_gain,
    ffn_shift,
    cotangent,
):
    seqs, rows, width = tokens.shape
    n_dev = lax.axis_size("seq")
    me = lax.axis_index("seq")
    t = lax.axis_index("tp")
    side, core = t // 2, t % 2
    n_blocks = rows // BLOCK * n_dev
    hidden = query_weight.shape[1]
    units = up_weight.shape[1]
    span = n_dev * BLOCK

    (
        x, q, k_own, k_far, v_own, v_far, attn_low, lse, ids, u_bias, wt, cot, wo, w_up, w_down,
    ) = enter(
        tokens, cotangent, rand_blocks.transpose(2, 3, 0, 1), query_weight.T, key_weight.T, value_weight.T,
        query_bias, value_bias, up_bias, output_weight, up_weight, down_weight, n_dev,
    )
    u_bias = u_bias.reshape(4 * units)
    branch = plain_dot(attn_low, wo) + output_bias
    unit_one, inverse_one = norm_parts(x.astype(jnp.float32) + branch)
    normed = unit_one * attn_gain + attn_shift
    normed_low = normed.astype(jnp.bfloat16)
    pre_act = plain_dot(normed_low, w_up) + u_bias
    cdf = 0.5 * (1.0 + lax.erf(pre_act * HALF_ROOT))
    act_low = (pre_act * cdf).astype(jnp.bfloat16)
    slope = (cdf + pre_act * (PDF_SCALE * jnp.exp(-0.5 * pre_act * pre_act))).astype(jnp.bfloat16)
    ffn = plain_dot(act_low, w_down) + down_bias
    unit_two, inverse_two = norm_parts(normed + ffn)
    out_low = (unit_two * ffn_gain + ffn_shift).astype(jnp.bfloat16)

    g_resid2, grad_ffngain, grad_ffnshift = norm_back(
        cot.astype(jnp.float32), unit_two, inverse_two, ffn_gain
    )
    g_ffn = g_resid2.astype(jnp.bfloat16)
    grad_downbias = jnp.sum(g_ffn.astype(jnp.float32), 0)
    g_pre = (back_dot(g_ffn, w_down) * slope.astype(jnp.float32)).astype(jnp.bfloat16)
    grad_upbias = jnp.sum(g_pre.astype(jnp.float32), 0)
    g_normed = g_resid2 + back_dot(g_pre, w_up)
    g_resid, grad_attngain, grad_attnshift = norm_back(g_normed, unit_one, inverse_one, attn_gain)
    g_branch = g_resid.astype(jnp.bfloat16)
    grad_obias = jnp.sum(g_branch.astype(jnp.float32), 0)
    g_attn = back_dot(g_branch, wo).astype(jnp.bfloat16)

    ups = grad_upbias.reshape(2, 2, units)
    ups = jnp.where(side == 0, ups, ups[::-1]).reshape(4, width)
    late = jnp.zeros((2, width), jnp.float32)
    lines = [grad_obias, grad_attngain, grad_attnshift, grad_downbias, grad_ffngain, grad_ffnshift]
    early = jnp.concatenate([late, ups, jnp.stack(lines), late, late], 0)
    sums, layer_output, input_out, small = tail(
        q, k_own, k_far, v_own, v_far, ids, lse, attn_low, g_attn, x, g_resid, early,
        normed_low, g_ffn, act_low, g_pre, out_low, wt.reshape(3 * width, width), n_dev,
    )
    small = small[5]

    def share(first, size):
        whole = small[first : first + 4 * size // width].reshape(4, size)
        return lax.dynamic_index_in_dim(whole, t, 0, False)

    sums = sums.astype(jnp.float32)
    half = units // sums.shape[1]
    g_down = sums[:half].reshape(units, width)
    g_up = sums[half : half + width // sums.shape[1]].reshape(width, units)
    rest = sums[half + width // sums.shape[1] :].reshape(4, hidden, width)
    g_o, g_q, g_k, g_v = rest
    return (
        layer_output.reshape(seqs, rows, width),
        input_out.astype(jnp.float32).reshape(seqs, rows, width),
        g_q.T,
        share(0, hidden),
        g_k.T,
        g_v.T,
        share(1, hidden),
        g_o,
        small[6],
        small[7],
        small[8],
        g_up,
        share(2, units),
        g_down,
        small[9],
        small[10],
        small[11],
    )


def per_device(tokens, *rest):
    seqs, rows, _ = tokens.shape
    n_dev = lax.axis_size("seq")
    if lax.axis_size("tp") == 4 and n_dev == 8 and seqs == 2 * n_dev and rows == 2 * BLOCK:
        return whole_sequences(tokens, *rest)
    return split_sequences(tokens, *rest)


def solution(mesh):
    placed = (
        P(None, "seq", None),
        P(None, None, "tp", None),
        P(None, "tp"),
        P("tp"),
        P(None, "tp"),
        P(None, "tp"),
        P("tp"),
        P("tp", None),
        P(),
        P(),
        P(),
        P(None, "tp"),
        P("tp"),
        P("tp", None),
        P(),
        P(),
        P(),
        P(None, "seq", None),
    )
    return jax.shard_map(
        per_device,
        mesh=mesh,
        in_specs=placed,
        out_specs=(
            P(None, "seq", None),
            P(None, "seq", None),
            P(None, "tp"),
            P("tp"),
            P(None, "tp"),
            P(None, "tp"),
            P("tp"),
            P("tp", None),
            P(),
            P(),
            P(),
            P(None, "tp"),
            P("tp"),
            P("tp", None),
            P(),
            P(),
            P(),
        ),
        check_vma=False,
    )
```
